32 devices in a mesh: rows: 8 (over z, y), seq: 4 (over x, core).
Axes of the slice: x: 2, y: 2, z: 4, core: 2. Of those that a mesh axis runs over, the one named last changes fastest.
Arguments:
- tokens: bfloat16 [32, 512, 768], P('rows', 'seq'), may hold values from -6 to 6
- w_query: bfloat16 [768, 768], replicated, may hold values from -0.4375 to 0.4375
- b_query: float32 [768], replicated, may hold values from -3 to 3
- w_key: bfloat16 [768, 768], replicated, may hold values from -0.21875 to 0.21875
- w_value: bfloat16 [768, 768], replicated, may hold values from -0.21875 to 0.21875
- b_value: float32 [768], replicated, may hold values from -0.6 to 0.6
- w_out: bfloat16 [768, 768], replicated, may hold values from -0.875 to 0.875
- b_out: float32 [768], replicated, may hold values from -1.8 to 1.8
- gain_one: float32 [768], replicated, may hold values from 0.5 to 1.5
- shift_one: float32 [768], replicated, may hold values from -1.2 to 1.2
- w_up: bfloat16 [768, 3072], replicated, may hold values from -0.21875 to 0.21875
- b_up: float32 [3072], replicated, may hold values from -3 to 3
- w_down: bfloat16 [3072, 768], replicated, may hold values from -0.109375 to 0.109375
- b_down: float32 [768], replicated, may hold values from -1.2 to 1.2
- gain_two: float32 [768], replicated, may hold values from 0.5 to 1.5
- shift_two: float32 [768], replicated, may hold values from -1.2 to 1.2
- passage_starts: int32 [32, 6], P('rows'), may hold values from 0 to 511, as said below
- queries: bfloat16 [1024, 768], P(('rows', 'seq')), may hold values from -3 to 3
- choices: int32 [1024, 32], P(('rows', 'seq')), may hold values from 0 to 191
- cotangent: bfloat16 [32, 512, 768], P('rows', 'seq'), may hold values from -6 to 6
Outputs:
- mixed: bfloat16 [32, 512, 768], P('rows', 'seq')
- query_losses: float32 [1024], P(('rows', 'seq'))
- grad_tokens: bfloat16 [32, 512, 768], P('rows', 'seq')
- grad_w_query: float32 [768, 768], P('seq')
- grad_b_query: float32 [768], P('seq')
- grad_w_key: float32 [768, 768], P('seq')
- grad_w_value: float32 [768, 768], P('seq')
- grad_b_value: float32 [768], P('seq')
- grad_w_out: float32 [768, 768], P('seq')
- grad_b_out: float32 [768], P('seq')
- grad_gain_one: float32 [768], P('seq')
- grad_shift_one: float32 [768], P('seq')
- grad_w_up: float32 [768, 3072], P('seq')
- grad_b_up: float32 [3072], P('seq')
- grad_w_down: float32 [3072, 768], P('seq')
- grad_b_down: float32 [768], P('seq')
- grad_gain_two: float32 [768], P('seq')
- grad_shift_two: float32 [768], P('seq')
The draws below stay inside these ranges and needn't reach their ends.
Inputs may be any that keep to these rules, and one draw needn't show every extreme that they name: `passage_starts`: each row lists the first positions of its 6 passages in rising order, the first being 0; a passage runs up to the next one's first position or to the row's end. In every aligned block of 4 rows one row's first passage reaches into the row's last 128 positions, and that row's last passage is its last position alone. `choices`: entry 0 of each row is the query's positive passage; passage r * 6 + j is passage j of row r.
All inputs are finite; a program needn't handle non-finite values.
Results may differ from the reference program's by a relative error of at most 0.015.
The reference program's roundings to bfloat16 on the way count: a program that leaves them out, or rounds other values in their place, can miss the bound.
Values may be sent and summed in bfloat16 or wider, within the bound.
No kernel may reach another device: no remote copies, remote signals or barrier semaphores. Data moves between devices by JAX's collectives and lax.ppermute only.
A program may use at most 192 MiB of HBM per device.

```python
import math
import jax
import jax.numpy as jnp
from jax import lax

D = 768
HEADS = 12
HEAD = 64
FF = 3072
PIECE = 128
PASS = 6
CH = 32
ROWS_DEV = 4
Q_DEV = 32
ROWS = 32
LEN = 512
ALLP = 192
NQ = 1024
N_SEQ = 4


def draw_passage_starts(key, part):
    key = jax.random.fold_in(key, 17)
    row_keys = jax.random.split(jax.random.fold_in(key, 1), ROWS)

    def drawn(row_key):
        cut_points = jax.random.permutation(row_key, LEN - 1)[:PASS - 1] + 1
        return jnp.concatenate([jnp.zeros((1,), jnp.int32), jnp.sort(cut_points).astype(jnp.int32)])

    def spanning(row_key):
        inner = jax.random.permutation(jax.random.fold_in(row_key, 2), PIECE - 2)[:PASS - 2] + 1 + LEN - PIECE
        return jnp.concatenate([jnp.zeros((1,), jnp.int32), jnp.sort(inner).astype(jnp.int32), jnp.full((1,), LEN - 1, jnp.int32)])
    drawn_rows = jax.vmap(drawn)(row_keys)
    spanning_rows = jax.vmap(spanning)(row_keys)
    picked = jax.random.randint(jax.random.fold_in(key, 3), (ROWS // ROWS_DEV,), 0, ROWS_DEV)
    chosen_rows = jnp.arange(ROWS, dtype=jnp.int32) % ROWS_DEV == jnp.repeat(picked, ROWS_DEV)
    return jnp.where(chosen_rows[:, None], spanning_rows, drawn_rows).astype(jnp.int32)


def ramp_scales(low_end, high_end):
    piece_number = jnp.arange(NQ, dtype=jnp.int32) // Q_DEV % N_SEQ
    fraction = piece_number.astype(jnp.float32) / max(N_SEQ - 1, 1)
    return (low_end + (high_end - low_end) * fraction) * D ** (-0.5)


def draw_queries(key, part):
    key = jax.random.fold_in(key, 29)
    unit = jnp.clip(jax.random.normal(key, (NQ, D), jnp.float32), -4.0, 4.0)
    scales = ramp_scales(1.0, 3.2)
    return (unit * scales[:, None]).astype(jnp.bfloat16)


def with_ends(entries, key, smallest, top_value):
    dims = entries.shape
    index_at = [jax.random.randint(jax.random.fold_in(key, axis), (), 0, dims[axis]) for axis in range(len(dims))]
    entries = entries.at[tuple(index_at)].set(smallest)
    longest = dims.index(max(dims))
    index_at[longest] = (index_at[longest] + 1) % dims[longest]
    return entries.at[tuple(index_at)].set(top_value)


def shard_levels(stream_key, dims, shards, smallest, high):
    level, own = 1.0, jax.random.fold_in(stream_key, 6)
    for dim, blocks in shards:
        steps = jnp.exp(jax.random.uniform(jax.random.fold_in(own, dim), (blocks,), jnp.float32, smallest / len(shards), high / len(shards)))
        level = level * jnp.repeat(steps, dims[dim] // blocks).reshape([-1 if axis == dim else 1 for axis in range(len(dims))])
    return level


def centred(rng, extent, deviation, most, cuts=(), held_as=jnp.bfloat16):
    result = jax.random.normal(rng, extent, jnp.float32) * deviation
    if len(cuts) > 0:
        result = shard_levels(rng, extent, cuts, -0.22, 0.18) * result
    return jnp.clip(result, min=-most, max=most).astype(held_as)


def setup_inputs(seed: int = 0) -> dict:
    key_of = jax.random.split(jax.random.key(seed), 21)
    tokens = centred(key_of[0], (ROWS, LEN, D), 1.0, 6.0, ((0, 8), (1, 4)))
    w_query = centred(key_of[1], (D, D), (D // 4) ** -0.5, 0.4375)
    b_query = centred(key_of[2], (D,), 0.5, 3.0, (), jnp.float32)
    w_key = centred(key_of[3], (D, D), D ** -0.5, 0.21875)
    w_value = centred(key_of[4], (D, D), D ** -0.5, 0.21875)
    b_value = centred(key_of[5], (D,), 0.1, 0.6, (), jnp.float32)
    w_out = centred(key_of[6], (D, D), (D // 16) ** -0.5, 0.875)
    b_out = centred(key_of[7], (D,), 0.3, 1.8, (), jnp.float32)
    gain_one = jnp.clip(1.0 + 0.1 * jax.random.normal(key_of[8], (D,), jnp.float32), 0.5, 1.5)
    shift_one = centred(key_of[9], (D,), 0.2, 1.2, (), jnp.float32)
    w_up = centred(key_of[10], (D, FF), D ** -0.5, 0.21875)
    b_up = centred(key_of[11], (FF,), 0.5, 3.0, (), jnp.float32)
    w_down = centred(key_of[12], (FF, D), FF ** -0.5, 0.109375)
    b_down = centred(key_of[13], (D,), 0.2, 1.2, (), jnp.float32)
    gain_two = jnp.clip(1.0 + 0.1 * jax.random.normal(key_of[14], (D,), jnp.float32), 0.5, 1.5)
    shift_two = centred(key_of[15], (D,), 0.2, 1.2, (), jnp.float32)
    passage_starts = draw_passage_starts(jax.random.fold_in(key_of[20], 71), 0)
    queries = draw_queries(jax.random.fold_in(key_of[20], 71), 0)
    choices = with_ends(jax.random.randint(key_of[18], (NQ, CH), 0, ALLP), jax.random.fold_in(key_of[18], 1), 0, ALLP - 1).astype(jnp.int32)
    cotangent = centred(key_of[19], (ROWS, LEN, D), 1.0, 6.0, ((0, 8), (1, 4)))
    return dict(tokens=tokens, w_query=w_query, b_query=b_query, w_key=w_key, w_value=w_value, b_value=b_value, w_out=w_out, b_out=b_out, gain_one=gain_one, shift_one=shift_one, w_up=w_up, b_up=b_up, w_down=w_down, b_down=b_down, gain_two=gain_two, shift_two=shift_two, passage_starts=passage_starts, queries=queries, choices=choices, cotangent=cotangent)


@jax.custom_vjp
def low(v):
    return lax.optimization_barrier(v.astype(jnp.bfloat16)).astype(jnp.float32)

@jax.custom_vjp
def low_back(v):
    return v

def low_keep(v):
    return (low(v), None)

def low_pass(kept, grad):
    return (grad,)

def back_keep(v):
    return (v, None)

def back_low(kept, grad):
    return (low(grad),)
low.defvjp(low_keep, low_pass)
low_back.defvjp(back_keep, back_low)
norm_eps = 1e-05
highest = lax.Precision.HIGHEST

def matmul(left, right):
    return jnp.dot(left, right, precision=highest)

def layer_norm(values, gain, shift):
    center = values - lax.optimization_barrier(jnp.mean(values, -1, keepdims=True))
    spread = lax.optimization_barrier(jnp.mean(center * center, -1, keepdims=True))
    return center * lax.rsqrt(spread + norm_eps) * gain + shift

def segment_ids(starts, length):
    places = jnp.arange(length, dtype=jnp.int32)
    return lax.optimization_barrier(jnp.sum((starts[:, None, :] <= places[None, :, None]).astype(jnp.int32), -1)) - 1

def block_layer(inputs, segments, weights):
    w_query, b_query, w_key, w_value, b_value, w_out, b_out, gain_one, shift_one, w_up, b_up, w_down, b_down, gain_two, shift_two = weights
    count, length, features = inputs.shape
    query = low(low_back(matmul(inputs, w_query) + b_query)).reshape(count, length, HEADS, HEAD)
    keyed = low(low_back(matmul(inputs, w_key))).reshape(count, length, HEADS, HEAD)
    valued = low(low_back(matmul(inputs, w_value) + b_value)).reshape(count, length, HEADS, HEAD)
    raw = jnp.einsum('bqhd,bkhd->bhqk', query, keyed, precision=highest)
    same_passage = segments[:, None, :, None] == segments[:, None, None, :]
    scores = jnp.where(same_passage, low_back(raw) * HEAD ** (-0.5), -1e+30)
    attention = jax.nn.softmax(scores, axis=-1)
    context = jnp.einsum('bhqk,bkhd->bqhd', low(attention), valued, precision=highest)
    context = low(low_back(context.reshape(count, length, features)))
    attended = low_back(matmul(context, w_out) + b_out)
    hidden_one = low(layer_norm(inputs + attended, gain_one, shift_one))
    upward = low_back(matmul(hidden_one, w_up) + b_up)
    active = low(jax.nn.gelu(upward, approximate=False))
    downward = low_back(matmul(active, w_down) + b_down)
    return low(layer_norm(hidden_one + downward, gain_two, shift_two))

def reference(tokens, w_query, b_query, w_key, w_value, b_value, w_out, b_out, gain_one, shift_one, w_up, b_up, w_down, b_down, gain_two, shift_two, passage_starts, queries, choices, cotangent):
    weights = tuple((item.astype(jnp.float32) for item in (w_query, b_query, w_key, w_value, b_value, w_out, b_out, gain_one, shift_one, w_up, b_up, w_down, b_down, gain_two, shift_two)))
    token_values = tokens.astype(jnp.float32)
    query_values = queries.astype(jnp.float32)
    cot_values = cotangent.astype(jnp.float32)
    segments = segment_ids(passage_starts, LEN)
    block_rows = math.gcd(ROWS, 8)
    blocks = ROWS // block_rows

    def objective(inputs, params):

        def one_block(pair):
            return block_layer(pair[0], pair[1], params)
        mixed = lax.map(jax.checkpoint(one_block), (inputs.reshape(blocks, block_rows, LEN, D), segments.reshape(blocks, block_rows, LEN)))
        mixed = mixed.reshape(ROWS, LEN, D)
        pooled = jnp.take_along_axis(mixed, passage_starts[:, :, None], axis=1).reshape(ALLP, D)
        logits = jnp.einsum('ncd,nd->nc', pooled[choices], query_values, precision=highest)
        losses = jax.nn.logsumexp(logits, axis=-1) - logits[:, 0]
        total = jnp.sum(mixed * cot_values) + jnp.sum(losses)
        return (total, (mixed, losses))
    total, backward, (mixed, losses) = jax.vjp(objective, token_values, weights, has_aux=True)
    grad_inputs, grad_weights = backward(jnp.ones((), jnp.float32))
    return (mixed.astype(jnp.bfloat16), losses, grad_inputs.astype(jnp.bfloat16), grad_weights[0], grad_weights[1], grad_weights[2], grad_weights[3], grad_weights[4], grad_weights[5], grad_weights[6], grad_weights[7], grad_weights[8], grad_weights[9], grad_weights[10], grad_weights[11], grad_weights[12], grad_weights[13], grad_weights[14])
```

```python
import functools

import jax
import jax.numpy as jnp
from jax import lax
from jax.experimental import pallas as pl
from jax.experimental.pallas import tpu as pltpu
from jax.sharding import PartitionSpec as P

HEADS = 12
HEAD = 64
PASS = 6
CH = 32
SLOT = 8
GROUP = 4

norm_eps = 1e-05
f32 = jnp.float32
bf16 = jnp.bfloat16
VMEM_BYTES = 56 * 1024 * 1024


def params():
    return pltpu.CompilerParams(
        dimension_semantics=None, vmem_limit_bytes=VMEM_BYTES
    )


def nt(a, b):
    return lax.dot_general(a, b, (((1,), (1,)), ((), ())), preferred_element_type=f32)


def tn(a, b):
    return lax.dot_general(a, b, (((0,), (0,)), ((), ())), preferred_element_type=f32)


def nn(a, b):
    return jnp.dot(a, b, preferred_element_type=f32)


def stats(values):
    center = values - jnp.mean(values, -1, keepdims=True)
    inv = lax.rsqrt(jnp.mean(center * center, -1, keepdims=True) + norm_eps)
    return center * inv, inv


def norm_back(grad, xhat, inv, gain):
    gx = grad * gain
    return inv * (
        gx - jnp.mean(gx, -1, keepdims=True) - xhat * jnp.mean(gx * xhat, -1, keepdims=True)
    )


def true_places(own_seq, count, piece, axis):
    shape = (count, 1) if axis == 0 else (1, count)
    local = lax.broadcasted_iota(jnp.int32, shape, axis)
    block = local // piece
    return (block ^ own_seq) * piece + (local - block * piece)


def segments(sc_ref, places):
    total = jnp.zeros(places.shape, jnp.int32)
    for j in range(PASS):
        total += (sc_ref[1 + j] <= places).astype(jnp.int32)
    return total


def attention_kernel(
    piece, sc_ref, x_ref, wq_ref, wk_ref, wv_ref, bq_ref, bv_ref, wo_ref, bo_ref, go_ref, so_ref,
    q_ref, k_ref, v_ref, ctxt_ref, lse_ref, resid_ref, hid_ref, hidt_ref, xt_ref,
    acc, ctx,
):
    step = pl.program_id(0)
    length = x_ref.shape[0]
    x = x_ref[...]
    q_ref[...] = (nn(x, wq_ref[...]) + bq_ref[...]).astype(bf16)
    k_ref[...] = nn(x, wk_ref[...]).astype(bf16)
    v_ref[...] = (nn(x, wv_ref[...]) + bv_ref[...]).astype(bf16)

    @pl.when(step == 0)
    def _():
        xt_ref[...] = x.T
        lse_ref[...] = jnp.zeros_like(lse_ref)
        acc[...] = jnp.zeros_like(acc)

    seg_col = segments(sc_ref, true_places(sc_ref[0], length, piece, 0))
    seg_row = segments(sc_ref, true_places(sc_ref[0], length, piece, 1))
    lanes = lax.broadcasted_iota(jnp.int32, (1, 128), 1)
    for h in range(GROUP):
        cols = slice(h * HEAD, (h + 1) * HEAD)
        k = k_ref[:, cols]
        v = v_ref[:, cols]
        for b in range(length // 128):
            rows = slice(b * 128, (b + 1) * 128)
            raw = nt(q_ref[rows, cols], k)
            scores = jnp.where(seg_col[rows] == seg_row, raw * (HEAD ** (-0.5)), -1e30)
            top = jnp.max(scores, -1, keepdims=True)
            e = jnp.exp(scores - top)
            total = jnp.sum(e, -1, keepdims=True)
            p = (e * (1.0 / total)).astype(bf16)
            ctx[rows, cols] = nn(p, v).astype(bf16)
            lse = top + jnp.log(total)
            lse_ref[rows, :] = jnp.where(lanes == step * GROUP + h, lse, lse_ref[rows, :])
    c = ctx[...]
    ctxt_ref[...] = c.T
    acc[...] += nn(c, wo_ref[...])

    @pl.when(step == pl.num_programs(0) - 1)
    def _():
        resid = x_ref[...].astype(f32) + (acc[...] + bo_ref[...])
        resid_ref[...] = resid
        xhat, _ = stats(resid)
        hid = (xhat * go_ref[...] + so_ref[...]).astype(bf16)
        hid_ref[...] = hid
        hidt_ref[...] = hid.T


def attention_forward(sc, x, wq, wk, wv, bq, bv, wo, bo, go, so, piece):
    length, d = x.shape
    wide = GROUP * HEAD
    steps = d // wide
    whole = lambda r, c: pl.BlockSpec((r, c), lambda i, s: (0, 0))
    cols = lambda r: pl.BlockSpec((r, wide), lambda i, s: (0, i))
    rows = lambda c: pl.BlockSpec((wide, c), lambda i, s: (i, 0))
    return pl.pallas_call(
        functools.partial(attention_kernel, piece),
        grid_spec=pltpu.PrefetchScalarGridSpec(
            num_scalar_prefetch=1,
            grid=(steps,),
            in_specs=[
                whole(length, d), cols(d), cols(d), cols(d), cols(1), cols(1), rows(d),
                whole(1, d), whole(1, d), whole(1, d),
            ],
            out_specs=[
                cols(length), cols(length), cols(length), rows(length), whole(length, 128),
                whole(length, d), whole(length, d), whole(d, length), whole(d, length),
            ],
            scratch_shapes=[pltpu.VMEM((length, d), f32), pltpu.VMEM((length, wide), bf16)],
        ),
        out_shape=[
            jax.ShapeDtypeStruct((length, d), bf16),
            jax.ShapeDtypeStruct((length, d), bf16),
            jax.ShapeDtypeStruct((length, d), bf16),
            jax.ShapeDtypeStruct((d, length), bf16),
            jax.ShapeDtypeStruct((length, 128), f32),
            jax.ShapeDtypeStruct((length, d), f32),
            jax.ShapeDtypeStruct((length, d), bf16),
            jax.ShapeDtypeStruct((d, length), bf16),
            jax.ShapeDtypeStruct((d, length), bf16),
        ],
        compiler_params=params(),
        name="attention_forward",
    )(sc, x, wq, wk, wv, bq, bv, wo, bo, go, so)


def feed_kernel(
    piece, sc_ref, hid_ref, wu_ref, bu_ref, wd_ref, bd_ref, gt_ref, st_ref,
    actt_ref, slope_ref, resid_ref, mixed_ref, pool_ref,
    acc,
):
    step = pl.program_id(0)
    length = hid_ref.shape[0]
    up = nn(hid_ref[...], wu_ref[...]) + bu_ref[...]
    phi_cum = 0.5 * (1.0 + lax.erf(up * (2.0 ** -0.5)))
    density = jnp.exp(-0.5 * up * up) * (0.3989422804014327)
    slope_ref[0] = phi_cum + up * density
    act = (up * phi_cum).astype(bf16)
    actt_ref[...] = act.T
    part = nn(act, wd_ref[...])

    @pl.when(step == 0)
    def _():
        acc[...] = part

    @pl.when(step > 0)
    def _():
        acc[...] += part

    @pl.when(step == pl.num_programs(0) - 1)
    def _():
        resid = hid_ref[...].astype(f32) + acc[...] + bd_ref[...]
        resid_ref[...] = resid
        xhat, _ = stats(resid)
        mixed = (xhat * gt_ref[...] + st_ref[...]).astype(bf16)
        mixed_ref[...] = mixed
        places = true_places(sc_ref[0], length, piece, 1)
        slot = lax.broadcasted_iota(jnp.int32, (SLOT, 1), 0)
        start = jnp.full((SLOT, 1), -1, jnp.int32)
        for j in range(PASS):
            start = jnp.where(slot == j, sc_ref[1 + j], start)
        pool_ref[...] = nn((places == start).astype(f32).astype(bf16), mixed)


def feed_forward(sc, hid, wu, bu, wd, bd, gt, st, piece, wide):
    length, d = hid.shape
    ff = wu.shape[1]
    steps = ff // wide
    whole = lambda r, c: pl.BlockSpec((r, c), lambda i, s: (0, 0))
    return pl.pallas_call(
        functools.partial(feed_kernel, piece),
        grid_spec=pltpu.PrefetchScalarGridSpec(
            num_scalar_prefetch=1,
            grid=(steps,),
            in_specs=[
                whole(length, d),
                pl.BlockSpec((d, wide), lambda i, s: (0, i)),
                pl.BlockSpec((1, wide), lambda i, s: (0, i)),
                pl.BlockSpec((wide, d), lambda i, s: (i, 0)),
                whole(1, d), whole(1, d), whole(1, d),
            ],
            out_specs=[
                pl.BlockSpec((wide, length), lambda i, s: (i, 0)),
                pl.BlockSpec((1, length, wide), lambda i, s: (i, 0, 0)),
                whole(length, d), whole(length, d), whole(SLOT, d),
            ],
            scratch_shapes=[pltpu.VMEM((length, d), f32)],
        ),
        out_shape=[
            jax.ShapeDtypeStruct((ff, length), bf16),
            jax.ShapeDtypeStruct((steps, length, wide), f32),
            jax.ShapeDtypeStruct((length, d), f32),
            jax.ShapeDtypeStruct((length, d), bf16),
            jax.ShapeDtypeStruct((SLOT, d), f32),
        ],
        compiler_params=params(),
        name="feed_forward",
    )(sc, hid, wu, bu, wd, bd, gt, st)


def loss_kernel(q_ref, pos_ref, pool_ref, loss_ref, grad_ref):
    step = pl.program_id(0)
    queries = q_ref[...]
    logits = nt(queries, pool_ref[...])
    count, width = logits.shape
    lanes = lax.broadcasted_iota(jnp.int32, (1, width), 1)
    pos = pos_ref[...]
    first = (pos[:, 0:1] == lanes).astype(f32)
    times = first
    for c in range(1, CH):
        times += (pos[:, c : c + 1] == lanes).astype(f32)
    held = times > 0.0
    top = jnp.max(jnp.where(held, logits, -jnp.inf), -1, keepdims=True)
    e = jnp.where(held, times * jnp.exp(jnp.minimum(logits - top, 0.0)), 0.0)
    total = jnp.sum(e, -1, keepdims=True)
    positive = jnp.sum(first * logits, -1, keepdims=True)
    loss_ref[...] = top + jnp.log(total) - positive
    grad = e[:, :128] * (1.0 / total) - first[:, :128]
    high = grad.astype(bf16)
    lower = (grad - high.astype(f32)).astype(bf16)
    part = (tn(high, queries) + tn(lower, queries))[:SLOT]

    @pl.when(step == 0)
    def _():
        grad_ref[...] = part

    @pl.when(step > 0)
    def _():
        grad_ref[...] += part


def retrieval(queries, pos, pooled):
    count, d = queries.shape
    block = 256
    return pl.pallas_call(
        loss_kernel,
        grid=(count // block,),
        in_specs=[
            pl.BlockSpec((block, d), lambda i: (i, 0)),
            pl.BlockSpec((block, CH), lambda i: (i, 0)),
            pl.BlockSpec(pooled.shape, lambda i: (0, 0)),
        ],
        out_specs=[
            pl.BlockSpec((block, 1), lambda i: (i, 0)),
            pl.BlockSpec((SLOT, d), lambda i: (0, 0)),
        ],
        out_shape=[
            jax.ShapeDtypeStruct((count, 1), f32),
            jax.ShapeDtypeStruct((SLOT, d), f32),
        ],
        compiler_params=params(),
        name="retrieval",
    )(queries, pos, pooled)


def norm_two_kernel(piece, sc_ref, cot_ref, gp_ref, resid_ref, gt_ref, gd_ref, gr_ref, sums_ref):
    length = cot_ref.shape[0]
    places = true_places(sc_ref[0], length, piece, 0)
    grad = cot_ref[...].astype(f32)
    for j in range(PASS):
        grad += jnp.where(places == sc_ref[1 + j], gp_ref[j : j + 1, :], 0.0)
    xhat, inv = stats(resid_ref[...])
    back = norm_back(grad, xhat, inv, gt_ref[...])
    gr_ref[...] = back
    down = back.astype(bf16)
    gd_ref[...] = down
    sums_ref[0:1, :] = jnp.sum(down.astype(f32), 0, keepdims=True)
    sums_ref[1:2, :] = jnp.sum(grad * xhat, 0, keepdims=True)
    sums_ref[2:3, :] = jnp.sum(grad, 0, keepdims=True)


def norm_two_back(sc, cot, gp, resid, gain, piece):
    length, d = cot.shape
    whole = pl.BlockSpec(memory_space=pltpu.VMEM)
    return pl.pallas_call(
        functools.partial(norm_two_kernel, piece),
        in_specs=[pl.BlockSpec(memory_space=pltpu.SMEM)] + [whole] * 4,
        out_specs=[whole] * 3,
        out_shape=[
            jax.ShapeDtypeStruct((length, d), bf16),
            jax.ShapeDtypeStruct((length, d), f32),
            jax.ShapeDtypeStruct((SLOT, d), f32),
        ],
        compiler_params=params(),
        name="norm_two_back",
    )(sc, cot, gp, resid, gain)


def feed_back_kernel(
    gd_ref, gr_ref, wd_ref, wu_ref, slope_ref, resid_ref, go_ref, wo_ref,
    gup_ref, bup_ref, gr1_ref, gab_ref, gctx_ref, sums_ref,
    acc,
):
    step = pl.program_id(0)
    gact = nt(gd_ref[...], wd_ref[...])
    gup = (gact * slope_ref[0]).astype(bf16)
    gup_ref[0] = gup
    bup_ref[0] = jnp.sum(gup.astype(f32), 0, keepdims=True)
    part = nt(gup, wu_ref[...])

    @pl.when(step == 0)
    def _():
        acc[...] = gr_ref[...] + part

    @pl.when(step > 0)
    def _():
        acc[...] += part

    @pl.when(step == pl.num_programs(0) - 1)
    def _():
        grad = acc[...]
        xhat, inv = stats(resid_ref[...])
        back = norm_back(grad, xhat, inv, go_ref[...])
        gr1_ref[...] = back
        gab = back.astype(bf16)
        gab_ref[...] = gab
        gctx_ref[...] = nt(gab, wo_ref[...]).astype(bf16)
        sums_ref[0:1, :] = jnp.sum(gab.astype(f32), 0, keepdims=True)
        sums_ref[1:2, :] = jnp.sum(grad * xhat, 0, keepdims=True)
        sums_ref[2:3, :] = jnp.sum(grad, 0, keepdims=True)


def feed_back(gd, gr, wd, wu, slope, resid, go, wo):
    length, d = gd.shape
    steps, _, wide = slope.shape
    whole = lambda r, c: pl.BlockSpec((r, c), lambda i: (0, 0))
    return pl.pallas_call(
        feed_back_kernel,
        grid=(steps,),
        in_specs=[
            whole(length, d), whole(length, d),
            pl.BlockSpec((wide, d), lambda i: (i, 0)),
            pl.BlockSpec((d, wide), lambda i: (0, i)),
            pl.BlockSpec((1, length, wide), lambda i: (i, 0, 0)),
            whole(length, d), whole(1, d), whole(d, d),
        ],
        out_specs=[
            pl.BlockSpec((1, length, wide), lambda i: (i, 0, 0)),
            pl.BlockSpec((1, 1, wide), lambda i: (i, 0, 0)),
            whole(length, d), whole(length, d), whole(length, d), whole(SLOT, d),
        ],
        out_shape=[
            jax.ShapeDtypeStruct((steps, length, wide), bf16),
            jax.ShapeDtypeStruct((steps, 1, wide), f32),
            jax.ShapeDtypeStruct((length, d), f32),
            jax.ShapeDtypeStruct((length, d), bf16),
            jax.ShapeDtypeStruct((length, d), bf16),
            jax.ShapeDtypeStruct((SLOT, d), f32),
        ],
        scratch_shapes=[pltpu.VMEM((length, d), f32)],
        compiler_params=params(),
        name="feed_back",
    )(gd, gr, wd, wu, slope, resid, go, wo)


def attention_back_kernel(
    piece, sc_ref, q_ref, k_ref, v_ref, gctx_ref, lse_ref, wq_ref, wk_ref, wv_ref, gr_ref,
    gqkv_ref, gtok_ref, sums_ref,
    acc, prob, graw,
):
    step = pl.program_id(0)
    length = q_ref.shape[0]
    seg_col = segments(sc_ref, true_places(sc_ref[0], length, piece, 0))
    seg_row = segments(sc_ref, true_places(sc_ref[0], length, piece, 1))
    lanes = lax.broadcasted_iota(jnp.int32, (1, 128), 1)
    scale = HEAD ** (-0.5)
    for h in range(GROUP):
        cols = slice(h * HEAD, (h + 1) * HEAD)
        q = q_ref[:, cols]
        k = k_ref[:, cols]
        v = v_ref[:, cols]
        gctx = gctx_ref[:, cols]
        for b in range(length // 128):
            rows = slice(b * 128, (b + 1) * 128)
            lse = jnp.sum(
                jnp.where(lanes == step * GROUP + h, lse_ref[rows, :], 0.0), -1, keepdims=True
            )
            raw = nt(q[rows], k)
            scores = jnp.where(seg_col[rows] == seg_row, raw * scale, -1e30)
            p = jnp.exp(scores - lse)
            prob[rows, :] = p.astype(bf16)
            ga = nt(gctx[rows], v)
            dots = jnp.sum(p * ga, -1, keepdims=True)
            g = (p * (ga - dots) * scale).astype(bf16)
            graw[rows, :] = g
            gqkv_ref[0, rows, cols] = nn(g, k).astype(bf16)
        gqkv_ref[1, :, cols] = tn(graw[...], q).astype(bf16)
        gqkv_ref[2, :, cols] = tn(prob[...], gctx).astype(bf16)
    gq, gk, gv = gqkv_ref[0], gqkv_ref[1], gqkv_ref[2]
    sums_ref[0:1, :] = jnp.sum(gq.astype(f32), 0, keepdims=True)
    sums_ref[1:2, :] = jnp.sum(gv.astype(f32), 0, keepdims=True)
    part = nt(gq, wq_ref[...]) + nt(gk, wk_ref[...]) + nt(gv, wv_ref[...])

    @pl.when(step == 0)
    def _():
        acc[...] = gr_ref[...] + part

    @pl.when(step > 0)
    def _():
        acc[...] += part

    @pl.when(step == pl.num_programs(0) - 1)
    def _():
        gtok_ref[...] = acc[...].astype(bf16)


def attention_back(sc, q, k, v, gctx, lse, wq, wk, wv, gr, piece):
    length, d = q.shape
    wide = GROUP * HEAD
    steps = d // wide
    whole = lambda r, c: pl.BlockSpec((r, c), lambda i, s: (0, 0))
    cols = lambda r: pl.BlockSpec((r, wide), lambda i, s: (0, i))
    return pl.pallas_call(
        functools.partial(attention_back_kernel, piece),
        grid_spec=pltpu.PrefetchScalarGridSpec(
            num_scalar_prefetch=1,
            grid=(steps,),
            in_specs=[
                cols(length), cols(length), cols(length), cols(length), whole(length, 128),
                cols(d), cols(d), cols(d), whole(length, d),
            ],
            out_specs=[
                pl.BlockSpec((3, length, wide), lambda i, s: (0, 0, i)),
                whole(length, d), cols(SLOT),
            ],
            scratch_shapes=[
                pltpu.VMEM((length, d), f32),
                pltpu.VMEM((length, length), bf16),
                pltpu.VMEM((length, length), bf16),
            ],
        ),
        out_shape=[
            jax.ShapeDtypeStruct((3, length, d), bf16),
            jax.ShapeDtypeStruct((length, d), bf16),
            jax.ShapeDtypeStruct((SLOT, d), f32),
        ],
        compiler_params=params(),
        name="attention_back",
    )(sc, q, k, v, gctx, lse, wq, wk, wv, gr)


def weight_send_kernel(sc_ref, lo_ref, lp_ref, go_ref, gp_ref, out_ref):
    out_ref[0] = (nn(lo_ref[0], go_ref[0]) + nn(lp_ref[0], gp_ref[0])).astype(bf16)


def weight_keep_kernel(sc_ref, lo_ref, lp_ref, go_ref, gp_ref, recv_ref, out_ref):
    total = nn(lo_ref[0], go_ref[0]) + nn(lp_ref[0], gp_ref[0]) + recv_ref[0].astype(f32)
    out_ref[0] = total.astype(bf16)


def weight_split_kernel(own_slot, sc_ref, lo_ref, lp_ref, go_ref, gp_ref, recv_ref, keep_ref, send_ref):
    step = pl.program_id(0)
    total = nn(lo_ref[0], go_ref[0]) + nn(lp_ref[0], gp_ref[0]) + recv_ref[0].astype(f32)
    half = total.shape[0] // 2
    for h in range(2):
        slot = (2 * step + h) ^ sc_ref[own_slot]
        rows = total[h * half : (h + 1) * half]

        @pl.when(slot < 4)
        def _():
            keep_ref[slot] = rows

        @pl.when(slot >= 4)
        def _():
            send_ref[slot - 4] = rows.astype(bf16)


def weight_specs(lo, lp, go, gp, other, steps, walk_rows):
    rows = lo.shape[1] // (steps if walk_rows else 1)
    length = lo.shape[2]
    wide = go.shape[2]
    r = (lambda i: i) if walk_rows else (lambda i: 0)
    g = (lambda i: 0) if walk_rows else (lambda i: i)
    x = (lambda s: 1 - s[0]) if other else (lambda s: s[0])
    return [
        pl.BlockSpec((1, rows, length), lambda i, s: (2 * x(s) + s[1], r(i), 0)),
        pl.BlockSpec((1, rows, length), lambda i, s: (x(s), r(i), 0)),
        pl.BlockSpec((1, length, wide), lambda i, s: (g(i), 0, 0)),
        pl.BlockSpec((1, length, wide), lambda i, s: (g(i), 0, 0)),
    ], rows, wide


def weight_send(sc, lo, lp, go, gp, steps, walk_rows, name):
    specs, rows, wide = weight_specs(lo, lp, go, gp, True, steps, walk_rows)
    block = pl.BlockSpec((1, rows, wide), lambda i, s: (i, 0, 0))
    return pl.pallas_call(
        weight_send_kernel,
        grid_spec=pltpu.PrefetchScalarGridSpec(
            num_scalar_prefetch=1, grid=(steps,), in_specs=specs, out_specs=block
        ),
        out_shape=jax.ShapeDtypeStruct((steps, rows, wide), bf16),
        compiler_params=params(),
        name=name,
    )(sc, lo, lp, go, gp)


def weight_keep(sc, lo, lp, go, gp, recv, steps, walk_rows, name):
    specs, rows, wide = weight_specs(lo, lp, go, gp, False, steps, walk_rows)
    block = pl.BlockSpec((1, rows, wide), lambda i, s: (i, 0, 0))
    return pl.pallas_call(
        weight_keep_kernel,
        grid_spec=pltpu.PrefetchScalarGridSpec(
            num_scalar_prefetch=1, grid=(steps,), in_specs=specs + [block], out_specs=block
        ),
        out_shape=jax.ShapeDtypeStruct((steps, rows, wide), bf16),
        compiler_params=params(),
        name=name,
    )(sc, lo, lp, go, gp, recv)


def weight_split(sc, lo, lp, go, gp, recv, own_slot, walk_rows, name):
    steps = 4
    specs, rows, wide = weight_specs(lo, lp, go, gp, False, steps, walk_rows)
    block = pl.BlockSpec((1, rows, wide), lambda i, s: (i, 0, 0))
    half = pl.BlockSpec((4, rows // 2, wide), lambda i, s: (0, 0, 0))
    return pl.pallas_call(
        functools.partial(weight_split_kernel, own_slot),
        grid_spec=pltpu.PrefetchScalarGridSpec(
            num_scalar_prefetch=1, grid=(steps,), in_specs=specs + [block], out_specs=[half, half]
        ),
        out_shape=[
            jax.ShapeDtypeStruct((4, rows // 2, wide), f32),
            jax.ShapeDtypeStruct((4, rows // 2, wide), bf16),
        ],
        compiler_params=params(),
        name=name,
    )(sc, lo, lp, go, gp, recv)


def place_kernel(own_slot, wide_out, sc_ref, near_ref, far_ref, out_ref):
    own = sc_ref[own_slot]
    rows, wide = near_ref.shape[1:]
    for k in range(8):
        piece = (near_ref[k] if k < 4 else far_ref[k - 4]).astype(f32)
        spot = own ^ k
        if wide_out:
            top = pl.multiple_of((spot % 2) * rows, rows)
            left = pl.multiple_of((spot // 2) * wide, wide)
            out_ref[pl.ds(top, rows), pl.ds(left, wide)] = piece
        else:
            out_ref[pl.ds(pl.multiple_of(spot * rows, rows), rows), :] = piece


def place(sc, near, far, own_slot, wide_out, name):
    rows, wide = near.shape[1:]
    shape = (2 * rows, 4 * wide) if wide_out else (8 * rows, wide)
    whole = pl.BlockSpec(memory_space=pltpu.VMEM)
    return pl.pallas_call(
        functools.partial(place_kernel, own_slot, wide_out),
        in_specs=[pl.BlockSpec(memory_space=pltpu.SMEM), whole, whole],
        out_specs=whole,
        out_shape=jax.ShapeDtypeStruct(shape, f32),
        compiler_params=params(),
        name=name,
    )(sc, near, far)


def flip(value, axis, mask):
    count = lax.axis_size(axis)
    return lax.ppermute(value, axis, [(i, i ^ mask) for i in range(count)])


def flip_both(value, row_mask, seq_mask):
    rows, seq = lax.axis_size("rows"), lax.axis_size("seq")
    pairs = [
        (r * seq + s, (r ^ row_mask) * seq + (s ^ seq_mask)) for r in range(rows) for s in range(seq)
    ]
    return lax.ppermute(value, ("rows", "seq"), pairs)


def row_flips():
    count = lax.axis_size("rows")
    assert count >= 8 and count & (count - 1) == 0
    return [1, 2, 6], [1 << b for b in range(3, count.bit_length() - 1)]


def halving(keep, send, order, extra):
    for stage, mask in enumerate(order):
        got = flip(send, "rows", mask).astype(f32) + keep
        if stage < 2:
            cut = got.shape[0] // 2
            keep, send = got[:cut], got[cut:].astype(bf16)
    own = got.astype(bf16)
    for mask in extra:
        own = (own.astype(f32) + flip(own, "rows", mask).astype(f32)).astype(bf16)
    near = own
    for mask in (order[2], order[1]):
        near = jnp.concatenate([near, flip(near, "rows", mask)], 0)
    return near, flip(near, "rows", order[0])


def doubling(value, order):
    for mask in order:
        value = value.astype(bf16)
        value = value.astype(f32) + flip(value, "rows", mask).astype(f32)
    return value


def spread(rows):
    own = lax.axis_index("seq")
    count = lax.axis_size("seq")
    assert rows.shape[0] == count
    pieces = [
        flip(lax.dynamic_index_in_dim(rows, own ^ mask, 0, keepdims=False), "seq", mask)
        if mask
        else lax.dynamic_index_in_dim(rows, own, 0, keepdims=False)
        for mask in range(count)
    ]
    return jnp.concatenate(pieces, 0)


def gather_back(row, count):
    own = lax.axis_index("seq")
    row = row.reshape(count, -1, row.shape[-1])
    out = jnp.zeros_like(row)
    for mask in range(count):
        piece = flip(row[mask], "seq", mask) if mask else row[0]
        out = lax.dynamic_update_index_in_dim(out, piece, own ^ mask, 0)
    return out


def per_device(
    tokens,
    w_query,
    b_query,
    w_key,
    w_value,
    b_value,
    w_out,
    b_out,
    gain_one,
    shift_one,
    w_up,
    b_up,
    w_down,
    b_down,
    gain_two,
    shift_two,
    passage_starts,
    queries,
    choices,
    cotangent,
):
    seq_count = lax.axis_size("seq")
    row_count = lax.axis_size("rows")
    own_s = lax.axis_index("seq")
    own_r = lax.axis_index("rows")
    row_block, piece, d = tokens.shape
    assert row_block == seq_count == 4
    ff = w_up.shape[1]
    core, xside = own_s % 2, own_s // 2
    base, extra = row_flips()
    bit_y = own_r % 2
    bit_b = (own_r // 4) % 2
    bit_a = (own_r // 2) % 2 ^ bit_b
    coord = {base[0]: bit_y, base[1]: bit_a, base[2]: bit_b}
    order_down = [base[1], base[2], base[0]]
    order_up = [base[2], base[0], base[1]]
    slot_of = lambda order: coord[order[0]] * 4 + coord[order[1]] * 2 + coord[order[2]]
    wsc = jnp.stack([xside, core, slot_of(order_down), slot_of(order_up)]).astype(jnp.int32)
    starts = lax.dynamic_index_in_dim(passage_starts, own_s, 0, keepdims=False)
    sc = jnp.concatenate([own_s[None].astype(jnp.int32), starts, jnp.zeros((1,), jnp.int32)])
    row = lambda v: v.reshape(1, -1)

    x = spread(tokens)

    code = jnp.concatenate(
        [queries, (choices // PASS).astype(bf16), (choices % PASS).astype(bf16)], axis=1
    )
    code_all = lax.all_gather(code, ("rows", "seq"), axis=0, tiled=True)

    cot = spread(cotangent)

    q, k, v, ctxt, lse, resid_one, hid, hidt, xt = attention_forward(
        sc, x, w_query, w_key, w_value, row(b_query), row(b_value), w_out, row(b_out),
        row(gain_one), row(shift_one), piece,
    )
    actt, slope, resid_two, mixed_row, pool = feed_forward(
        sc, hid, w_up, row(b_up), w_down, row(b_down), row(gain_two), row(shift_two), piece, d
    )

    pool = pool.astype(bf16)
    own_lin = own_r * seq_count + own_s
    devices = row_count * seq_count
    queries_all = code_all[:, :d]
    owner = code_all[:, d : d + CH].astype(jnp.int32)
    inner = code_all[:, d + CH :].astype(jnp.int32)
    if row_count == 8:
        near = jnp.concatenate(
            [pool, flip(pool, "seq", 2), flip(pool, "rows", 1), flip_both(pool, 1, 2)], 0
        )
        mid = jnp.concatenate(
            [near, flip(near, "rows", 2), flip(near, "rows", 6), flip(near, "rows", 4)], 0
        )
        pooled = jnp.concatenate([mid, flip(mid, "seq", 1)], 0)
        off = owner ^ own_lin
        z = off // 8
        spot = (off % 2) * 16 + (z ^ (z // 2)) * 4 + (off // 2) % 4
    else:
        pooled = lax.all_gather(pool, ("rows", "seq"), axis=0, tiled=True)
        pooled = jnp.roll(pooled, -own_lin * SLOT, 0)
        spot = (owner - own_lin) % devices
    losses_all, grad_pool = retrieval(queries_all, spot * SLOT + inner, pooled)
    query_losses = lax.dynamic_slice_in_dim(losses_all[:, 0], own_lin * queries.shape[0], queries.shape[0])

    other_half = lambda t, rows: lax.dynamic_index_in_dim(
        t.reshape(2, 2, rows, t.shape[-1]), 1 - core, 1, keepdims=False
    )
    quarters = lambda t: t.reshape(4, -1, t.shape[-1])
    swap = lambda t: flip(t, "seq", 1)
    actt_p = swap(other_half(actt, ff // 4))
    hidt_p = swap(other_half(hidt, d // 4))
    ctxt_p = swap(other_half(ctxt, d // 4))
    xt_p = swap(other_half(xt, d // 4))

    mixed = gather_back(mixed_row, seq_count)

    gd, gr_two, sums_two = norm_two_back(sc, cot, grad_pool, resid_two, row(gain_two), piece)
    gd_p = swap(gd)
    gup, bup, gr_one, gab, gctx, sums_one = feed_back(
        gd, gr_two, w_down, w_up, slope, resid_one, row(gain_one), w_out
    )
    gup_p = swap(gup)
    gab_p = swap(gab)

    down_in = (quarters(actt), actt_p, gd[None], gd_p[None])
    up_in = (quarters(hidt), hidt_p, gup, gup_p)
    out_in = (quarters(ctxt), ctxt_p, gab[None], gab_p[None])
    down_got = flip(weight_send(wsc, *down_in, 4, True, "down_send"), "seq", 2)
    up_got = flip(weight_send(wsc, *up_in, 4, False, "up_send"), "seq", 2)
    out_got = flip(weight_send(wsc, *out_in, 1, False, "out_send"), "seq", 2)

    gqkv, gtok, sums_qkv = attention_back(
        sc, q, k, v, gctx, lse, w_query, w_key, w_value, gr_one, piece
    )
    gqkv_p = swap(gqkv)

    down_parts = weight_split(wsc, *down_in, down_got, 2, True, "down_keep")
    near_down, far_down = halving(*down_parts, order_down, extra)
    up_parts = weight_split(wsc, *up_in, up_got, 3, False, "up_keep")
    near_up, far_up = halving(*up_parts, order_up, extra)
    grad_out = weight_keep(wsc, *out_in, out_got, 1, False, "out_keep")

    qkv_in = (quarters(xt), xt_p, gqkv, gqkv_p)
    qkv_send = weight_send(wsc, *qkv_in, 3, False, "qkv_send")

    vec = jnp.concatenate(
        [sums_qkv[:2], sums_one[:3], sums_two[:3]], 0
    )
    vec = vec.reshape(8, 4, d // 4).transpose(1, 0, 2).reshape(4, 2, d)
    vec = jnp.concatenate([vec, bup.reshape(4, ff // 4 // d, d)], 1)
    vec = vec.reshape(2, 2, 3, d)
    vec = lax.dynamic_index_in_dim(vec, core, 1, keepdims=False) + swap(
        lax.dynamic_index_in_dim(vec, 1 - core, 1, keepdims=False)
    )
    vec = jnp.pad(vec, ((0, 0), (0, 13), (0, 0)))
    vec_send = lax.dynamic_index_in_dim(vec, 1 - xside, 0, keepdims=False).astype(bf16)
    vec_keep = lax.dynamic_index_in_dim(vec, xside, 0, keepdims=False)

    got_q = flip(qkv_send[0], "seq", 2)
    got_k = flip(qkv_send[1], "seq", 2)
    got_v = flip(jnp.concatenate([qkv_send[2], vec_send], 0), "seq", 2)
    quarter = d // 4
    vec_sum = vec_keep + got_v[quarter:].astype(f32)
    got_v = got_v[:quarter]
    keep = weight_keep(
        wsc, *qkv_in, jnp.stack([got_q, got_k, got_v]), 3, False, "qkv_keep"
    )
    y, a, b = base
    grad_q = doubling(keep[0], [y, a, b] + extra)
    grad_k = doubling(keep[1], [a, b, y] + extra)
    last = doubling(jnp.concatenate([keep[2].astype(f32), vec_sum], 0), [b, y, a] + extra)
    grad_v = last[:quarter]
    small = last[quarter : quarter + 3]
    grad_o = doubling(grad_out[0], [a, b, y] + extra)

    grad_down = place(wsc, near_down, far_down, 2, False, "down_place")
    grad_up = place(wsc, near_up, far_up, 3, True, "up_place")
    grad_tokens = gather_back(gtok, seq_count)

    eight = small[:2].reshape(8, quarter)
    return (
        mixed,
        query_losses,
        grad_tokens,
        grad_q,
        eight[0],
        grad_k,
        grad_v,
        eight[1],
        grad_o,
        eight[2],
        eight[3],
        eight[4],
        grad_up,
        small[2],
        grad_down,
        eight[5],
        eight[6],
        eight[7],
    )


def solution(mesh):
    weights = (P(),) * 15
    placed = (
        (P("rows", "seq", None),)
        + weights
        + (
            P("rows", None),
            P(("rows", "seq"), None),
            P(("rows", "seq"), None),
            P("rows", "seq", None),
        )
    )
    return jax.shard_map(
        per_device,
        mesh=mesh,
        in_specs=placed,
        out_specs=(
            P("rows", "seq", None),
            P(("rows", "seq")),
            P("rows", "seq", None),
            P("seq", None),
            P("seq"),
            P("seq", None),
            P("seq", None),
            P("seq"),
            P("seq", None),
            P("seq"),
            P("seq"),
            P("seq"),
            P("seq", None),
            P("seq"),
            P("seq", None),
            P("seq"),
            P("seq"),
            P("seq"),
        ),
        check_vma=False,
    )
```

```python
import functools

import jax
import jax.numpy as jnp
from jax import lax
from jax.experimental import pallas as pl
from jax.experimental.pallas import tpu as pltpu
from jax.sharding import PartitionSpec as P

HEADS = 12
HEAD = 64
PASS = 6
CH = 32
SLOT = 8
GROUP = 4
SUB = 256
TAIL = (
    0.0925346463, 0.0902475115, 0.103641987, 0.0105003931,
    0.230693277, -0.20728912, 0.250823127, -0.0711517759,
)
SCALE = HEAD ** (-0.5)

norm_eps = 1e-05
f32 = jnp.float32
bf16 = jnp.bfloat16
VMEM_BYTES = 56 * 1024 * 1024


def params():
    return pltpu.CompilerParams(vmem_limit_bytes=VMEM_BYTES)


def cost(micros):
    return pl.CostEstimate(flops=int(micros * 1.15e9), bytes_accessed=0, transcendentals=0)


def nt(a, b):
    return lax.dot_general(a, b, (((1,), (1,)), ((), ())), preferred_element_type=f32)


def tn(a, b):
    return lax.dot_general(a, b, (((0,), (0,)), ((), ())), preferred_element_type=f32)


def nn(a, b):
    return jnp.dot(a, b, preferred_element_type=f32)


def stats(values):
    center = values - jnp.mean(values, -1, keepdims=True)
    inv = lax.rsqrt(jnp.mean(center * center, -1, keepdims=True) + norm_eps)
    return center * inv, inv


def norm_back(grad, xhat, inv, gain):
    gx = grad * gain
    return inv * (
        gx - jnp.mean(gx, -1, keepdims=True) - xhat * jnp.mean(gx * xhat, -1, keepdims=True)
    )


def true_places(own_seq, count, piece, axis):
    shape = (count, 1) if axis == 0 else (1, count)
    local = lax.broadcasted_iota(jnp.int32, shape, axis)
    block = local // piece
    return (block ^ own_seq) * piece + (local - block * piece)


def segments(sc_ref, places):
    total = jnp.zeros(places.shape, jnp.int32)
    for j in range(PASS):
        total += (sc_ref[1 + j] <= places).astype(jnp.int32)
    return total


def segment_bias(sc_ref, length, piece):
    col = segments(sc_ref, true_places(sc_ref[0], length, piece, 0))
    row = segments(sc_ref, true_places(sc_ref[0], length, piece, 1))
    return jnp.where(col == row, 0.0, -1e30)


def normal_tail(size):
    t = 1.0 / (1.0 + 0.2316419 * size)
    total = jnp.full_like(t, TAIL[-1])
    for term in TAIL[-2::-1]:
        total = total * t + term
    return total * t


def call(kernel, sc, args, specs, outs, out_specs, grid, scratch, name, micros, deps=()):
    count = len(args)

    def body(sc_ref, *refs):
        kernel(sc_ref, *refs[:count], *refs[count + len(deps) :])

    hold = pl.BlockSpec(memory_space=pl.ANY)
    return pl.pallas_call(
        body,
        grid_spec=pltpu.PrefetchScalarGridSpec(
            num_scalar_prefetch=1,
            grid=grid,
            in_specs=list(specs) + [hold] * len(deps),
            out_specs=out_specs,
            scratch_shapes=scratch,
        ),
        out_shape=outs,
        compiler_params=params(),
        cost_estimate=cost(micros),
        name=name,
    )(sc, *args, *deps)


def shape(t, *dims):
    return jax.ShapeDtypeStruct(dims, t)


def whole(*dims):
    return pl.BlockSpec(dims, lambda i, s: (0,) * len(dims))


def attention_kernel(
    piece, sc_ref, x_ref, wq_ref, wk_ref, wv_ref, bq_ref, bv_ref, wo_ref, bo_ref, go_ref, so_ref,
    q_ref, k_ref, v_ref, ctxt_ref, lse_ref, xt_ref, xhat_ref, inv_ref, hid_ref, hidt_ref,
    acc, bias,
):
    step = pl.program_id(0)
    length = x_ref.shape[0]
    x = x_ref[...]
    q_ref[...] = (nn(x, wq_ref[...]) + bq_ref[...]).astype(bf16)
    k_ref[...] = nn(x, wk_ref[...]).astype(bf16)
    v_ref[...] = (nn(x, wv_ref[...]) + bv_ref[...]).astype(bf16)

    @pl.when(step == 0)
    def _():
        bias[...] = segment_bias(sc_ref, length, piece)
        acc[...] = x.astype(f32) + bo_ref[...]

    for h in range(GROUP):
        cols = slice(h * HEAD, (h + 1) * HEAD)
        raw = nt(k_ref[:, cols], q_ref[:, cols] * jnp.asarray(SCALE, bf16))
        scores = raw + bias[...]
        top = jnp.max(scores, 0, keepdims=True)
        e = jnp.exp(scores - top)
        total = jnp.sum(e, 0, keepdims=True)
        p = (e * (1.0 / total)).astype(bf16)
        ctxt_ref[cols, :] = tn(v_ref[:, cols], p).astype(bf16)
        lse_ref[0, h : h + 1, :] = top + jnp.log(total)
    acc[...] += tn(ctxt_ref[...], wo_ref[...])

    for j in range(x_ref.shape[1] // xt_ref.shape[0]):
        wide = xt_ref.shape[0]

        @pl.when(step == j)
        def _():
            xt_ref[...] = x_ref[:, j * wide : (j + 1) * wide].T

    @pl.when(step == pl.num_programs(0) - 1)
    def _():
        xhat, inv = stats(acc[...])
        xhat_ref[...] = xhat
        inv_ref[...] = inv
        hid = (xhat * go_ref[...] + so_ref[...]).astype(bf16)
        hid_ref[...] = hid
        hidt_ref[...] = hid.T


def attention_forward(sc, x, wq, wk, wv, bq, bv, wo, bo, go, so, piece):
    length, d = x.shape
    wide = GROUP * HEAD
    steps = d // wide
    cols = lambda r: pl.BlockSpec((r, wide), lambda i, s: (0, i))
    rows = lambda c: pl.BlockSpec((wide, c), lambda i, s: (i, 0))
    return call(
        functools.partial(attention_kernel, piece),
        sc,
        (x, wq, wk, wv, bq, bv, wo, bo, go, so),
        [
            whole(length, d), cols(d), cols(d), cols(d), cols(1), cols(1), rows(d),
            whole(1, d), whole(1, d), whole(1, d),
        ],
        [
            shape(bf16, length, d), shape(bf16, length, d), shape(bf16, length, d),
            shape(bf16, d, length), shape(f32, steps, SLOT, length), shape(bf16, d, length),
            shape(f32, length, d), shape(f32, length, 1), shape(bf16, length, d),
            shape(bf16, d, length),
        ],
        [
            cols(length), cols(length), cols(length), rows(length),
            pl.BlockSpec((1, SLOT, length), lambda i, s: (i, 0, 0)), rows(length),
            whole(length, d), whole(length, 1), whole(length, d), whole(d, length),
        ],
        (steps,),
        [pltpu.VMEM((length, d), f32), pltpu.VMEM((length, length), f32)],
        "attention_forward", 18,
    )


def feed_kernel(
    piece, sc_ref, hid_ref, wu_ref, bu_ref, wd_ref, bd_ref, gt_ref, st_ref,
    actt_ref, slope_ref, xhat_ref, inv_ref, mixed_ref, pool_ref,
    acc,
):
    step = pl.program_id(0)
    length = hid_ref.shape[0]

    @pl.when(step == 0)
    def _():
        acc[...] = hid_ref[...].astype(f32) + bd_ref[...]

    for c in range(0, wu_ref.shape[1], SUB):
        cols = slice(c, c + SUB)
        up = nn(hid_ref[...], wu_ref[:, cols]) + bu_ref[:, cols]
        e = jnp.exp(-0.5 * up * up)
        tail = normal_tail(jnp.abs(up)) * e
        cum = jnp.where(up < 0.0, tail, 1.0 - tail)
        slope_ref[0, :, cols] = cum + up * (e * 0.3989422804014327)
        act = (up * cum).astype(bf16)
        actt_ref[cols, :] = act.T
        acc[...] += nn(act, wd_ref[cols, :])

    @pl.when(step == pl.num_programs(0) - 1)
    def _():
        xhat, inv = stats(acc[...])
        xhat_ref[...] = xhat
        inv_ref[...] = inv
        mixed = (xhat * gt_ref[...] + st_ref[...]).astype(bf16)
        mixed_ref[...] = mixed
        places = true_places(sc_ref[0], length, piece, 1)
        slot = lax.broadcasted_iota(jnp.int32, (SLOT, 1), 0)
        start = jnp.full((SLOT, 1), -1, jnp.int32)
        for j in range(PASS):
            start = jnp.where(slot == j, sc_ref[1 + j], start)
        pool_ref[...] = nn((places == start).astype(f32).astype(bf16), mixed)


def feed_forward(sc, hid, wu, bu, wd, bd, gt, st, piece, deps):
    length, d = hid.shape
    ff = wu.shape[1]
    steps = ff // d
    return call(
        functools.partial(feed_kernel, piece),
        sc,
        (hid, wu, bu, wd, bd, gt, st),
        [
            whole(length, d),
            pl.BlockSpec((d, d), lambda i, s: (0, i)),
            pl.BlockSpec((1, d), lambda i, s: (0, i)),
            pl.BlockSpec((d, d), lambda i, s: (i, 0)),
            whole(1, d), whole(1, d), whole(1, d),
        ],
        [
            shape(bf16, ff, length), shape(f32, steps, length, d), shape(f32, length, d),
            shape(f32, length, 1), shape(bf16, length, d), shape(f32, SLOT, d),
        ],
        [
            pl.BlockSpec((d, length), lambda i, s: (i, 0)),
            pl.BlockSpec((1, length, d), lambda i, s: (i, 0, 0)),
            whole(length, d), whole(length, 1), whole(length, d), whole(SLOT, d),
        ],
        (steps,),
        [pltpu.VMEM((length, d), f32)],
        "feed_forward", 14, deps,
    )


def loss_kernel(
    piece, steps, devices, code_ref, sc_ref, q_ref, pool_ref, cot_ref, xhat_ref, inv_ref, gt_ref,
    loss_ref, gd_ref, gr_ref, sums_ref, gp,
):
    step = pl.program_id(0)
    d = pool_ref.shape[1]

    @pl.when(step == 0)
    def _():
        gp[...] = jnp.zeros_like(gp)
        sums_ref[...] = jnp.zeros_like(sums_ref)

    @pl.when(step < steps)
    def _():
        queries = q_ref[:, :d]
        logits = nt(queries, pool_ref[...])
        lanes = lax.broadcasted_iota(jnp.int32, (1, logits.shape[1]), 1)
        owner = q_ref[:, d : d + CH].astype(f32).astype(jnp.int32)
        inner = q_ref[:, d + CH :].astype(f32).astype(jnp.int32)
        pos = code_ref(owner, sc_ref[7], devices) * SLOT + inner
        first = (pos[:, 0:1] == lanes).astype(f32)
        times = first
        for c in range(1, CH):
            times += (pos[:, c : c + 1] == lanes).astype(f32)
        held = times > 0.0
        top = jnp.max(jnp.where(held, logits, -jnp.inf), -1, keepdims=True)
        e = jnp.where(held, times * jnp.exp(jnp.minimum(logits - top, 0.0)), 0.0)
        total = jnp.sum(e, -1, keepdims=True)
        positive = jnp.sum(first * logits, -1, keepdims=True)
        loss_ref[...] = top + jnp.log(total) - positive
        grad = e[:, :128] * (1.0 / total) - first[:, :128]
        high = grad.astype(bf16)
        lower = (grad - high.astype(f32)).astype(bf16)
        gp[...] += (tn(high, queries) + tn(lower, queries))[:SLOT]

    @pl.when(step >= steps)
    def _():
        block = (step - steps) ^ sc_ref[0]
        places = block * piece + lax.broadcasted_iota(jnp.int32, (piece, 1), 0)
        grad = cot_ref[...].astype(f32)
        for j in range(PASS):
            grad += jnp.where(places == sc_ref[1 + j], gp[j : j + 1, :], 0.0)
        xhat = xhat_ref[...]
        back = norm_back(grad, xhat, inv_ref[...], gt_ref[...])
        gr_ref[...] = back
        down = back.astype(bf16)
        gd_ref[...] = down
        sums_ref[0:1, :] += jnp.sum(down.astype(f32), 0, keepdims=True)
        sums_ref[1:2, :] += jnp.sum(grad * xhat, 0, keepdims=True)
        sums_ref[2:3, :] += jnp.sum(grad, 0, keepdims=True)


def cube_place(owner, own, devices):
    off = owner ^ own
    z = off >> 3
    return (off & 1) * 16 + (z ^ (z >> 1)) * 4 + ((off >> 1) & 3)


def turned_place(owner, own, devices):
    off = owner - own
    return jnp.where(off < 0, off + devices, off)


def retrieval(sc, code_all, pooled, cot, xhat, inv, gain, piece, places, devices):
    count, width = code_all.shape
    length, d = cot.shape
    block = 256
    steps, pieces = count // block, length // piece
    first = lambda i: jnp.minimum(i, steps - 1)
    second = lambda i: jnp.maximum(i - steps, 0)
    part = lambda c: pl.BlockSpec((piece, c), lambda i, s: (second(i), 0))
    return call(
        functools.partial(loss_kernel, piece, steps, devices, places),
        sc,
        (code_all, pooled, cot, xhat, inv, gain),
        [
            pl.BlockSpec((block, width), lambda i, s: (first(i), 0)),
            whole(*pooled.shape), part(d), part(d), part(1), whole(1, d),
        ],
        [shape(f32, count, 1), shape(bf16, length, d), shape(f32, length, d), shape(f32, SLOT, d)],
        [
            pl.BlockSpec((block, 1), lambda i, s: (first(i), 0)), part(d), part(d), whole(SLOT, d),
        ],
        (steps + pieces,),
        [pltpu.VMEM((SLOT, d), f32)],
        "retrieval", 12,
    )


def feed_back_kernel(
    sc_ref, gd_ref, gr_ref, wd_ref, wu_ref, slope_ref, xhat_ref, inv_ref, go_ref, wo_ref,
    gug_ref, bup_ref, gr1_ref, gctx_ref, sums_ref,
    acc,
):
    step = pl.program_id(0)
    last = pl.num_programs(0) - 1

    @pl.when(step == 0)
    def _():
        acc[...] = gr_ref[...]

    @pl.when(step < last)
    def _():
        gact = nt(gd_ref[...], wd_ref[...])
        gup = (gact * slope_ref[0]).astype(bf16)
        gug_ref[0] = gup
        bup_ref[0] = jnp.sum(gup.astype(f32), 0, keepdims=True)
        acc[...] += nt(gup, wu_ref[...])

    @pl.when(step == last)
    def _():
        grad = acc[...]
        xhat = xhat_ref[...]
        back = norm_back(grad, xhat, inv_ref[...], go_ref[...])
        gr1_ref[...] = back
        gab = back.astype(bf16)
        gug_ref[0] = gab
        gctx_ref[...] = nt(gab, wo_ref[...]).astype(bf16)
        sums_ref[0:1, :] = jnp.sum(gab.astype(f32), 0, keepdims=True)
        sums_ref[1:2, :] = jnp.sum(grad * xhat, 0, keepdims=True)
        sums_ref[2:3, :] = jnp.sum(grad, 0, keepdims=True)


def feed_back(sc, gd, gr, wd, wu, slope, xhat, inv, go, wo, deps):
    length, d = gd.shape
    steps = slope.shape[0]
    at = lambda i: jnp.minimum(i, steps - 1)
    return call(
        feed_back_kernel,
        sc,
        (gd, gr, wd, wu, slope, xhat, inv, go, wo),
        [
            whole(length, d), whole(length, d),
            pl.BlockSpec((d, d), lambda i, s: (at(i), 0)),
            pl.BlockSpec((d, d), lambda i, s: (0, at(i))),
            pl.BlockSpec((1, length, d), lambda i, s: (at(i), 0, 0)),
            whole(length, d), whole(length, 1), whole(1, d), whole(d, d),
        ],
        [
            shape(bf16, steps + 1, length, d), shape(f32, steps, 1, d), shape(f32, length, d),
            shape(bf16, length, d), shape(f32, SLOT, d),
        ],
        [
            pl.BlockSpec((1, length, d), lambda i, s: (i, 0, 0)),
            pl.BlockSpec((1, 1, d), lambda i, s: (at(i), 0, 0)),
            whole(length, d), whole(length, d), whole(SLOT, d),
        ],
        (steps + 1,),
        [pltpu.VMEM((length, d), f32)],
        "feed_back", 0, deps,
    )


def attention_back_kernel(
    piece, sc_ref, q_ref, k_ref, v_ref, gctx_ref, lse_ref, wq_ref, wk_ref, wv_ref, gr_ref,
    gqkv_ref, gtok_ref, sums_ref,
    acc, bias, gkt, gvt,
):
    step = pl.program_id(0)
    length = q_ref.shape[0]

    @pl.when(step == 0)
    def _():
        bias[...] = segment_bias(sc_ref, length, piece)
        acc[...] = gr_ref[...]

    lse = lse_ref[0].T
    for h in range(GROUP):
        cols = slice(h * HEAD, (h + 1) * HEAD)
        q = q_ref[:, cols]
        k = k_ref[:, cols]
        gctx = gctx_ref[:, cols]
        scores = nt(q * jnp.asarray(SCALE, bf16), k) + bias[...]
        p = jnp.exp(scores - lse[:, h : h + 1])
        ga = nt(gctx, v_ref[:, cols])
        dots = jnp.sum(p * ga, -1, keepdims=True)
        g = (p * (ga - dots)).astype(bf16)
        gqkv_ref[0, :, cols] = (nn(g, k) * SCALE).astype(bf16)
        gkt[cols, :] = (tn(q, g) * SCALE).astype(bf16)
        gvt[cols, :] = tn(gctx, p.astype(bf16)).astype(bf16)
    gqkv_ref[1] = gkt[...].T
    gqkv_ref[2] = gvt[...].T
    gq, gk, gv = gqkv_ref[0], gqkv_ref[1], gqkv_ref[2]
    sums_ref[0:1, :] = jnp.sum(gq.astype(f32), 0, keepdims=True)
    sums_ref[1:2, :] = jnp.sum(gv.astype(f32), 0, keepdims=True)
    acc[...] += nt(gq, wq_ref[...]) + nt(gk, wk_ref[...]) + nt(gv, wv_ref[...])

    @pl.when(step == pl.num_programs(0) - 1)
    def _():
        gtok_ref[...] = acc[...].astype(bf16)


def attention_back(sc, q, k, v, gctx, lse, wq, wk, wv, gr, piece, deps):
    length, d = q.shape
    wide = GROUP * HEAD
    steps = d // wide
    cols = lambda r: pl.BlockSpec((r, wide), lambda i, s: (0, i))
    return call(
        functools.partial(attention_back_kernel, piece),
        sc,
        (q, k, v, gctx, lse, wq, wk, wv, gr),
        [
            cols(length), cols(length), cols(length), cols(length),
            pl.BlockSpec((1, SLOT, length), lambda i, s: (i, 0, 0)),
            cols(d), cols(d), cols(d), whole(length, d),
        ],
        [shape(bf16, 3, length, d), shape(bf16, length, d), shape(f32, SLOT, d)],
        [pl.BlockSpec((3, length, wide), lambda i, s: (0, 0, i)), whole(length, d), cols(SLOT)],
        (steps,),
        [
            pltpu.VMEM((length, d), f32), pltpu.VMEM((length, length), f32),
            pltpu.VMEM((wide, length), bf16), pltpu.VMEM((wide, length), bf16),
        ],
        "attention_back", 0, deps,
    )


def weight_total(two, lo_refs, lp_ref, go_ref, gp_ref):
    lo = lo_refs[0][...].reshape(lo_refs[0].shape[-2:])
    if len(lo_refs) > 1:
        lo = jnp.where(pl.program_id(0) < two, lo, lo_refs[1][...].reshape(lo.shape))
    return nn(lo, go_ref[0]) + nn(lp_ref[0, 0], gp_ref[0])


def weight_send_kernel(lefts, two, sc_ref, *refs):
    lo_refs, (lp_ref, go_ref, gp_ref, out_ref) = refs[:lefts], refs[lefts:]
    out_ref[0] = weight_total(two, lo_refs, lp_ref, go_ref, gp_ref).astype(bf16)


def weight_keep_kernel(lefts, two, sc_ref, *refs):
    lo_refs, (lp_ref, go_ref, gp_ref, recv_ref, keep_ref, send_ref) = refs[:lefts], refs[lefts:]
    total = weight_total(two, lo_refs, lp_ref, go_ref, gp_ref) + recv_ref[0].astype(f32)
    half = total.shape[0] // 2
    for h in range(2):
        rows = total[h * half : (h + 1) * half]

        @pl.when(sc_ref[2] == h)
        def _():
            keep_ref[0] = rows

        @pl.when(sc_ref[2] != h)
        def _():
            send_ref[0] = rows.astype(bf16)


def weight_specs(lefts, halves, grads, grads_p, other, steps, turn):
    x = (lambda s: 1 - s[0]) if other else (lambda s: s[0])
    specs = []
    for left in lefts:
        if left.ndim == 4:
            specs.append(
                pl.BlockSpec((1, 1) + left.shape[2:], lambda i, s: (2 * x(s) + s[1], i, 0, 0))
            )
        else:
            specs.append(pl.BlockSpec((1,) + left.shape[1:], lambda i, s: (2 * x(s) + s[1], 0, 0)))
    specs.append(pl.BlockSpec((1, 1) + halves.shape[2:], lambda i, s: (x(s), turn(i), 0, 0)))
    one = grads.shape[0] == 1
    block = pl.BlockSpec((1,) + grads.shape[1:], lambda i, s: (0 if one else i, 0, 0))
    return (*lefts, halves, grads, grads_p), specs + [block, block]


def weight_send(sc, operands, steps, two, turn, name, deps=(), micros=0):
    args, specs = weight_specs(*operands, True, steps, turn)
    rows, wide = operands[1].shape[2], operands[2].shape[2]
    return call(
        functools.partial(weight_send_kernel, len(operands[0]), two),
        sc, args, specs, shape(bf16, steps, rows, wide),
        pl.BlockSpec((1, rows, wide), lambda i, s: (i, 0, 0)), (steps,), [],
        name, micros, deps,
    )


def weight_keep(sc, operands, recv, steps, two, turn, name, deps=(), micros=0):
    args, specs = weight_specs(*operands, False, steps, turn)
    rows, wide = operands[1].shape[2], operands[2].shape[2]
    half = pl.BlockSpec((1, rows // 2, wide), lambda i, s: (i, 0, 0))
    return call(
        functools.partial(weight_keep_kernel, len(operands[0]), two),
        sc, args + (recv,), specs + [pl.BlockSpec((1, rows, wide), lambda i, s: (i, 0, 0))],
        [shape(f32, steps, rows // 2, wide), shape(bf16, steps, rows // 2, wide)],
        [half, half], (steps,), [],
        name, micros, deps,
    )


def place_kernel(spots, sc_ref, own_ref, far_ref, *out_refs):
    half = own_ref.shape[1]
    wide = own_ref.shape[2]
    for n, (out, down, left) in enumerate(spots):
        for part, side in ((own_ref, 0), (far_ref, 1)):
            h = sc_ref[2] ^ side
            top = pl.multiple_of(down * 2 * half + h * half, half)
            out_refs[out][pl.ds(top, half), left * wide : (left + 1) * wide] = part[n].astype(f32)


def place(sc, own, far, spots, dims, name):
    return call(
        functools.partial(place_kernel, spots),
        sc, (own, far), [whole(*own.shape), whole(*far.shape)],
        [shape(f32, *dim) for dim in dims], [whole(*dim) for dim in dims], (1,), [],
        name, 3,
    )


def flip(value, axis, mask):
    count = lax.axis_size(axis)
    return lax.ppermute(value, axis, [(i, i ^ mask) for i in range(count)])


def flip_both(value, row_mask, seq_mask):
    rows, seq = lax.axis_size("rows"), lax.axis_size("seq")
    pairs = [
        (r * seq + s, (r ^ row_mask) * seq + (s ^ seq_mask)) for r in range(rows) for s in range(seq)
    ]
    return lax.ppermute(value, ("rows", "seq"), pairs)


def row_flips():
    count = lax.axis_size("rows")
    assert count >= 8 and count & (count - 1) == 0
    return [2, 6] + [1 << b for b in range(3, count.bit_length() - 1)]


def over_rows(keep, send, masks):
    value = (keep + flip(send, "rows", 1).astype(f32)).astype(bf16)
    for mask in masks:
        value = (value.astype(f32) + flip(value, "rows", mask).astype(f32)).astype(bf16)
    return value, flip(value, "rows", 1)


def spread(rows):
    own = lax.axis_index("seq")
    count = lax.axis_size("seq")
    assert rows.shape[0] == count
    pieces = [
        flip(lax.dynamic_index_in_dim(rows, own ^ mask, 0, keepdims=False), "seq", mask)
        if mask
        else lax.dynamic_index_in_dim(rows, own, 0, keepdims=False)
        for mask in range(count)
    ]
    return jnp.concatenate(pieces, 0)


def gather_back(row, count):
    own = lax.axis_index("seq")
    row = row.reshape(count, -1, row.shape[-1])
    out = jnp.zeros_like(row)
    for mask in range(count):
        piece = flip(row[mask], "seq", mask) if mask else row[0]
        out = lax.dynamic_update_index_in_dim(out, piece, own ^ mask, 0)
    return out


def per_device(
    tokens,
    w_query,
    b_query,
    w_key,
    w_value,
    b_value,
    w_out,
    b_out,
    gain_one,
    shift_one,
    w_up,
    b_up,
    w_down,
    b_down,
    gain_two,
    shift_two,
    passage_starts,
    queries,
    choices,
    cotangent,
):
    seq_count = lax.axis_size("seq")
    row_count = lax.axis_size("rows")
    own_s = lax.axis_index("seq")
    own_r = lax.axis_index("rows")
    row_block, piece, d = tokens.shape
    assert row_block == seq_count == 4
    ff = w_up.shape[1]
    quarter = d // 4
    core, xside = own_s % 2, own_s // 2
    own_lin = own_r * seq_count + own_s
    devices = row_count * seq_count
    masks = row_flips()
    wsc = jnp.stack([xside, core, own_r % 2, own_r % 2]).astype(jnp.int32)
    starts = lax.dynamic_index_in_dim(passage_starts, own_s, 0, keepdims=False)
    sc = jnp.concatenate([own_s[None].astype(jnp.int32), starts, own_lin[None].astype(jnp.int32)])
    row = lambda v: v.reshape(1, -1)
    swap = lambda t: flip(t, "seq", 1)

    x = spread(tokens)

    code = jnp.concatenate(
        [queries, (choices // PASS).astype(bf16), (choices % PASS).astype(bf16)], axis=1
    )
    code_all = lax.all_gather(code, ("rows", "seq"), axis=0, tiled=True)

    cot = spread(cotangent)

    q, k, v, ctxt, lse, xt, xhat_one, inv_one, hid, hidt = attention_forward(
        sc, x, w_query, w_key, w_value, row(b_query), row(b_value), w_out, row(b_out),
        row(gain_one), row(shift_one), piece,
    )
    actt, slope, xhat_two, inv_two, mixed_row, pool = feed_forward(
        sc, hid, w_up, row(b_up), w_down, row(b_down), row(gain_two), row(shift_two), piece, (cot,)
    )

    pool = pool.astype(bf16)
    if row_count == 8:
        near = jnp.concatenate(
            [pool, flip(pool, "seq", 2), flip(pool, "rows", 1), flip_both(pool, 1, 2)], 0
        )
        mid = jnp.concatenate(
            [near, flip(near, "rows", 2), flip(near, "rows", 6), flip(near, "rows", 4)], 0
        )
        pooled = jnp.concatenate([mid, flip(mid, "seq", 1)], 0)
        places = cube_place
    else:
        pooled = lax.all_gather(pool, ("rows", "seq"), axis=0, tiled=True)
        pooled = jnp.roll(pooled, -own_lin * SLOT, 0)
        places = turned_place

    other_half = lambda t: lax.dynamic_index_in_dim(
        t.reshape(2, 2, -1, quarter, t.shape[-1]), 1 - core, 1, keepdims=False
    )
    halves = swap(
        jnp.concatenate([other_half(hidt), other_half(ctxt), other_half(xt), other_half(actt)], 1)
    )
    quarters = lambda t: t.reshape(4, -1, t.shape[-1])

    losses_all, gd, gr_two, sums_two = retrieval(
        sc, code_all, pooled, cot, xhat_two, inv_two, row(gain_two), piece, places, devices
    )
    query_losses = lax.dynamic_slice_in_dim(
        losses_all[:, 0], own_lin * queries.shape[0], queries.shape[0]
    )

    down_ops = ((actt.reshape(4, 4, quarter, -1),), halves, gd[None], swap(gd)[None])
    down_turn = lambda i: 3 + i
    down_sent = weight_send(wsc, down_ops, 4, 0, down_turn, "down_send")
    down_got = flip(down_sent, "seq", 2)

    gug, bup, gr_one, gctx, sums_one = feed_back(
        sc, gd, gr_two, w_down, w_up, slope, xhat_one, inv_one, row(gain_one), w_out, (down_sent,)
    )
    down_parts = weight_keep(wsc, down_ops, down_got, 4, 0, down_turn, "down_keep", (gug,), 100)
    up_ops = ((quarters(hidt), quarters(ctxt)), halves, gug, swap(gug))
    up_turn = lambda i: i // 4
    up_sent = weight_send(wsc, up_ops, 5, 4, up_turn, "up_send", (down_parts[0],))
    up_got = flip(up_sent, "seq", 2)

    gqkv, gtok, sums_qkv = attention_back(
        sc, q, k, v, gctx, lse, w_query, w_key, w_value, gr_one, piece, (up_sent,)
    )
    up_parts = weight_keep(wsc, up_ops, up_got, 5, 4, up_turn, "up_keep", (gqkv,), 100)
    qkv_ops = ((quarters(xt),), halves, gqkv, swap(gqkv))
    qkv_turn = lambda i: 2
    qkv_sent = weight_send(wsc, qkv_ops, 3, 0, qkv_turn, "qkv_send", (up_parts[0],))
    qkv_got = flip(qkv_sent, "seq", 2)

    down_sum = over_rows(*down_parts, masks)
    up_sum = over_rows(*up_parts, masks)
    qkv_parts = weight_keep(wsc, qkv_ops, qkv_got, 3, 0, qkv_turn, "qkv_keep", (up_parts[0],))
    qkv_sum = over_rows(*qkv_parts, masks)

    vec = jnp.concatenate([sums_qkv[:2], sums_one[:3], sums_two[:3]], 0)
    vec = vec.reshape(8, 4, quarter).transpose(1, 0, 2).reshape(4, 2, d)
    vec = jnp.concatenate([vec, bup.reshape(4, ff // 4 // d, d)], 1)
    vec = vec.reshape(2, 2, 3, d)
    vec = lax.dynamic_index_in_dim(vec, core, 1, keepdims=False) + swap(
        lax.dynamic_index_in_dim(vec, 1 - core, 1, keepdims=False)
    )
    vec = lax.dynamic_index_in_dim(vec, xside, 0, keepdims=False) + flip(
        lax.dynamic_index_in_dim(vec, 1 - xside, 0, keepdims=False), "seq", 2
    )
    for mask in [1] + masks:
        vec = vec + flip(vec, "rows", mask)

    mixed = gather_back(mixed_row, seq_count)
    grad_tokens = gather_back(gtok, seq_count)

    (grad_down,) = place(
        wsc, *down_sum, [(0, n, 0) for n in range(4)], [(4 * quarter, d)], "down_place"
    )
    grad_up, grad_o = place(
        wsc, *up_sum, [(0, 0, n) for n in range(4)] + [(1, 0, 0)],
        [(quarter, ff), (quarter, d)], "up_place",
    )
    grad_q, grad_k, grad_v = place(
        wsc, *qkv_sum, [(n, 0, 0) for n in range(3)], [(quarter, d)] * 3, "qkv_place"
    )

    eight = vec[:2].reshape(8, quarter)
    return (
        mixed,
        query_losses,
        grad_tokens,
        grad_q,
        eight[0],
        grad_k,
        grad_v,
        eight[1],
        grad_o,
        eight[2],
        eight[3],
        eight[4],
        grad_up,
        vec[2],
        grad_down,
        eight[5],
        eight[6],
        eight[7],
    )


def solution(mesh):
    weights = (P(),) * 15
    placed = (
        (P("rows", "seq", None),)
        + weights
        + (
            P("rows", None),
            P(("rows", "seq"), None),
            P(("rows", "seq"), None),
            P("rows", "seq", None),
        )
    )
    return jax.shard_map(
        per_device,
        mesh=mesh,
        in_specs=placed,
        out_specs=(
            P("rows", "seq", None),
            P(("rows", "seq")),
            P("rows", "seq", None),
            P("seq", None),
            P("seq"),
            P("seq", None),
            P("seq", None),
            P("seq"),
            P("seq", None),
            P("seq"),
            P("seq"),
            P("seq"),
            P("seq", None),
            P("seq"),
            P("seq", None),
            P("seq"),
            P("seq"),
            P("seq"),
        ),
        check_vma=False,
    )
```

```python
import functools

import jax
import jax.numpy as jnp
from jax import lax
from jax.experimental import pallas as pl
from jax.experimental.pallas import tpu as pltpu
from jax.sharding import PartitionSpec as P

HEADS = 12
HEAD = 64
PASS = 6
CH = 32
SLOT = 8
GROUP = 4
SUB = 384
SCALE = HEAD ** (-0.5)

norm_eps = 1e-05
f32 = jnp.float32
bf16 = jnp.bfloat16
VMEM_BYTES = 28 * 1024 * 1024
PIN = 100
EXTRA = 16
SMALL = 128


def params():
    return pltpu.CompilerParams(vmem_limit_bytes=VMEM_BYTES)


def cost(micros):
    return pl.CostEstimate(flops=int(micros * 1.15e9), bytes_accessed=0, transcendentals=0)


def nt(a, b):
    return lax.dot_general(a, b, (((1,), (1,)), ((), ())), preferred_element_type=f32)


def tn(a, b):
    return lax.dot_general(a, b, (((0,), (0,)), ((), ())), preferred_element_type=f32)


def nn(a, b):
    return jnp.dot(a, b, preferred_element_type=f32)


def stats(values):
    center = values - jnp.mean(values, -1, keepdims=True)
    inv = lax.rsqrt(jnp.mean(center * center, -1, keepdims=True) + norm_eps)
    return center * inv, inv


def norm_back(grad, xhat, inv, gain):
    gx = grad * gain
    return inv * (
        gx - jnp.mean(gx, -1, keepdims=True) - xhat * jnp.mean(gx * xhat, -1, keepdims=True)
    )


def true_places(own_seq, count, piece, axis):
    shape = (count, 1) if axis == 0 else (1, count)
    local = lax.broadcasted_iota(jnp.int32, shape, axis)
    block = local // piece
    return (block ^ own_seq) * piece + (local - block * piece)


def segments(sc_ref, places):
    total = jnp.zeros(places.shape, jnp.int32)
    for j in range(PASS):
        total += (sc_ref[1 + j] <= places).astype(jnp.int32)
    return total


def segment_bias(sc_ref, length, piece):
    col = segments(sc_ref, true_places(sc_ref[0], length, piece, 0))
    row = segments(sc_ref, true_places(sc_ref[0], length, piece, 1))
    return jnp.where(col == row, 0.0, -1e30)


def call(kernel, sc, args, specs, outs, out_specs, grid, scratch, name, micros, deps=()):
    count = len(args)

    def body(sc_ref, *refs):
        kernel(sc_ref, *refs[:count], *refs[count + len(deps) :])

    hold = pl.BlockSpec(memory_space=pl.ANY)
    return pl.pallas_call(
        body,
        grid_spec=pltpu.PrefetchScalarGridSpec(
            num_scalar_prefetch=1,
            grid=grid,
            in_specs=list(specs) + [hold] * len(deps),
            out_specs=out_specs,
            scratch_shapes=scratch,
        ),
        out_shape=outs,
        compiler_params=params(),
        cost_estimate=cost(micros),
        name=name,
    )(sc, *args, *deps)


def shape(t, *dims):
    return jax.ShapeDtypeStruct(dims, t)


def kept(t, *dims):
    return pltpu.HBM(dims, t)


def far(*values):
    return tuple(pltpu.with_memory_space_constraint(v, pltpu.HBM) for v in values)


def whole(*dims):
    return pl.BlockSpec(dims, lambda i, s: (0,) * len(dims))


def attention_kernel(
    piece, sc_ref, x_ref, wq_ref, wk_ref, wv_ref, bq_ref, bv_ref, wo_ref, bo_ref, go_ref, so_ref,
    q_ref, k_ref, v_ref, ctxt_ref, lse_ref, xt_ref, xhat_ref, inv_ref, hid_ref, hidt_ref,
    acc, bias,
):
    step = pl.program_id(0)
    length = x_ref.shape[0]
    x = x_ref[...]
    q_ref[...] = (nn(x, wq_ref[...]) + bq_ref[...]).astype(bf16)
    k_ref[...] = nn(x, wk_ref[...]).astype(bf16)
    v_ref[...] = (nn(x, wv_ref[...]) + bv_ref[...]).astype(bf16)

    @pl.when(step == 0)
    def _():
        bias[...] = segment_bias(sc_ref, length, piece)
        acc[...] = x.astype(f32) + bo_ref[...]

    for h in range(GROUP):
        cols = slice(h * HEAD, (h + 1) * HEAD)
        raw = nt(k_ref[:, cols], q_ref[:, cols] * jnp.asarray(SCALE, bf16))
        scores = raw + bias[...]
        top = jnp.max(scores, 0, keepdims=True)
        e = jnp.exp(scores - top)
        total = jnp.sum(e, 0, keepdims=True)
        p = (e * (1.0 / total)).astype(bf16)
        ctxt_ref[cols, :] = tn(v_ref[:, cols], p).astype(bf16)
        lse_ref[0, h : h + 1, :] = top + jnp.log(total)
    acc[...] += tn(ctxt_ref[...], wo_ref[...])

    for j in range(x_ref.shape[1] // xt_ref.shape[0]):
        wide = xt_ref.shape[0]

        @pl.when(step == j)
        def _():
            xt_ref[...] = x_ref[:, j * wide : (j + 1) * wide].T

    @pl.when(step == pl.num_programs(0) - 1)
    def _():
        xhat, inv = stats(acc[...])
        xhat_ref[...] = xhat
        inv_ref[...] = inv
        hid = (xhat * go_ref[...] + so_ref[...]).astype(bf16)
        hid_ref[...] = hid
        hidt_ref[...] = hid.T


def attention_forward(sc, x, wq, wk, wv, bq, bv, wo, bo, go, so, piece):
    length, d = x.shape
    wide = GROUP * HEAD
    steps = d // wide
    cols = lambda r: pl.BlockSpec((r, wide), lambda i, s: (0, i))
    rows = lambda c: pl.BlockSpec((wide, c), lambda i, s: (i, 0))
    return call(
        functools.partial(attention_kernel, piece),
        sc,
        (x, *far(wq, wk, wv), bq, bv, *far(wo), bo, go, so),
        [
            whole(length, d), cols(d), cols(d), cols(d), cols(1), cols(1), rows(d),
            whole(1, d), whole(1, d), whole(1, d),
        ],
        [
            kept(bf16, length, d), kept(bf16, length, d), kept(bf16, length, d),
            kept(bf16, d, length), kept(f32, steps, SLOT, length), kept(bf16, d, length),
            kept(f32, length, d), kept(f32, length, 1), shape(bf16, length, d),
            kept(bf16, d, length),
        ],
        [
            cols(length), cols(length), cols(length), rows(length),
            pl.BlockSpec((1, SLOT, length), lambda i, s: (i, 0, 0)), rows(length),
            whole(length, d), whole(length, 1), whole(length, d), whole(d, length),
        ],
        (steps,),
        [pltpu.VMEM((length, d), f32), pltpu.VMEM((length, length), f32)],
        "attention_forward", 0,
    )


def feed_kernel(
    piece, sc_ref, hid_ref, wu_ref, bu_ref, wd_ref, bd_ref, gt_ref, st_ref,
    actt_ref, slope_ref, xhat_ref, inv_ref, mixed_ref, pool_ref,
    acc,
):
    step = pl.program_id(0)
    length = hid_ref.shape[0]

    @pl.when(step == 0)
    def _():
        acc[...] = hid_ref[...].astype(f32) + bd_ref[...]

    for c in range(0, wu_ref.shape[1], SUB):
        cols = slice(c, c + SUB)
        up = nn(hid_ref[...], wu_ref[:, cols]) + bu_ref[:, cols]
        e = jnp.exp(-0.5 * up * up)
        cum = 0.5 + 0.5 * lax.erf(up * (2.0 ** -0.5))
        slope_ref[0, :, cols] = (cum + up * (e * 0.3989422804014327)).astype(bf16)
        act = (up * cum).astype(bf16)
        actt_ref[cols, :] = act.T
        acc[...] += nn(act, wd_ref[cols, :])

    @pl.when(step == pl.num_programs(0) - 1)
    def _():
        xhat, inv = stats(acc[...])
        xhat_ref[...] = xhat
        inv_ref[...] = inv
        mixed = (xhat * gt_ref[...] + st_ref[...]).astype(bf16)
        mixed_ref[...] = mixed
        places = true_places(sc_ref[0], length, piece, 1)
        slot = lax.broadcasted_iota(jnp.int32, (SLOT, 1), 0)
        start = jnp.full((SLOT, 1), -1, jnp.int32)
        for j in range(PASS):
            start = jnp.where(slot == j, sc_ref[1 + j], start)
        pool_ref[...] = nn((places == start).astype(f32).astype(bf16), mixed)


def feed_forward(sc, hid, wu, bu, wd, bd, gt, st, piece, deps):
    length, d = hid.shape
    ff = wu.shape[1]
    steps = ff // d
    return call(
        functools.partial(feed_kernel, piece),
        sc,
        (hid, *far(wu), bu, *far(wd), bd, gt, st),
        [
            whole(length, d),
            pl.BlockSpec((d, d), lambda i, s: (0, i)),
            pl.BlockSpec((1, d), lambda i, s: (0, i)),
            pl.BlockSpec((d, d), lambda i, s: (i, 0)),
            whole(1, d), whole(1, d), whole(1, d),
        ],
        [
            kept(bf16, ff, length), kept(bf16, steps, length, d), kept(f32, length, d),
            kept(f32, length, 1), kept(bf16, length, d), shape(f32, SLOT, d),
        ],
        [
            pl.BlockSpec((d, length), lambda i, s: (i, 0)),
            pl.BlockSpec((1, length, d), lambda i, s: (i, 0, 0)),
            whole(length, d), whole(length, 1), whole(length, d), whole(SLOT, d),
        ],
        (steps,),
        [pltpu.VMEM((length, d), f32)],
        "feed_forward", 0, deps,
    )


def loss_kernel(
    piece, steps, devices, code_ref, sc_ref, q_ref, pool_ref, cot_ref, xhat_ref, inv_ref, gt_ref,
    loss_ref, gd_ref, gr_ref, sums_ref, gp,
):
    step = pl.program_id(0)
    d = pool_ref.shape[1]

    @pl.when(step == 0)
    def _():
        gp[...] = jnp.zeros_like(gp)
        sums_ref[...] = jnp.zeros_like(sums_ref)

    @pl.when(step < steps)
    def _():
        queries = q_ref[:, :d]
        logits = nt(queries, pool_ref[...])
        lanes = lax.broadcasted_iota(jnp.int32, (1, logits.shape[1]), 1)
        owner = q_ref[:, d : d + CH].astype(f32).astype(jnp.int32)
        inner = q_ref[:, d + CH :].astype(f32).astype(jnp.int32)
        pos = code_ref(owner, sc_ref[7], devices) * SLOT + inner
        first = (pos[:, 0:1] == lanes).astype(f32)
        times = first
        for c in range(1, CH):
            times += (pos[:, c : c + 1] == lanes).astype(f32)
        held = times > 0.0
        top = jnp.max(jnp.where(held, logits, -jnp.inf), -1, keepdims=True)
        e = jnp.where(held, times * jnp.exp(jnp.minimum(logits - top, 0.0)), 0.0)
        total = jnp.sum(e, -1, keepdims=True)
        positive = jnp.sum(first * logits, -1, keepdims=True)
        loss_ref[...] = top + jnp.log(total) - positive
        grad = e[:, :128] * (1.0 / total) - first[:, :128]
        high = grad.astype(bf16)
        lower = (grad - high.astype(f32)).astype(bf16)
        gp[...] += (tn(high, queries) + tn(lower, queries))[:SLOT]

    @pl.when(step >= steps)
    def _():
        block = (step - steps) ^ sc_ref[0]
        places = block * piece + lax.broadcasted_iota(jnp.int32, (piece, 1), 0)
        grad = cot_ref[...].astype(f32)
        for j in range(PASS):
            grad += jnp.where(places == sc_ref[1 + j], gp[j : j + 1, :], 0.0)
        xhat = xhat_ref[...]
        back = norm_back(grad, xhat, inv_ref[...], gt_ref[...])
        gr_ref[...] = back
        down = back.astype(bf16)
        gd_ref[...] = down
        sums_ref[0:1, :] += jnp.sum(down.astype(f32), 0, keepdims=True)
        sums_ref[1:2, :] += jnp.sum(grad * xhat, 0, keepdims=True)
        sums_ref[2:3, :] += jnp.sum(grad, 0, keepdims=True)


def cube_place(owner, own, devices):
    off = owner ^ own
    z = off >> 3
    return (off & 1) * 16 + (z ^ (z >> 1)) * 4 + ((off >> 1) & 3)


def turned_place(owner, own, devices):
    off = owner - own
    return jnp.where(off < 0, off + devices, off)


def retrieval(sc, code_all, pooled, cot, xhat, inv, gain, piece, places, devices, deps):
    count, width = code_all.shape
    length, d = cot.shape
    block = 256
    steps, pieces = count // block, length // piece
    first = lambda i: jnp.minimum(i, steps - 1)
    second = lambda i: jnp.maximum(i - steps, 0)
    part = lambda c: pl.BlockSpec((piece, c), lambda i, s: (second(i), 0))
    return call(
        functools.partial(loss_kernel, piece, steps, devices, places),
        sc,
        (*far(code_all), pooled, *far(cot, xhat, inv), gain),
        [
            pl.BlockSpec((block, width), lambda i, s: (first(i), 0)),
            whole(*pooled.shape), part(d), part(d), part(1), whole(1, d),
        ],
        [shape(f32, count, 1), shape(bf16, length, d), shape(f32, length, d), shape(f32, SLOT, d)],
        [
            pl.BlockSpec((block, 1), lambda i, s: (first(i), 0)), part(d), part(d), whole(SLOT, d),
        ],
        (steps + pieces,),
        [pltpu.VMEM((SLOT, d), f32)],
        "retrieval", 0, deps,
    )


def feed_back_kernel(
    sc_ref, gd_ref, gr_ref, wd_ref, wu_ref, slope_ref, xhat_ref, inv_ref, go_ref, wo_ref,
    gug_ref, bup_ref, gr1_ref, gctx_ref, sums_ref,
    acc,
):
    step = pl.program_id(0)
    last = pl.num_programs(0) - 1

    @pl.when(step == 0)
    def _():
        acc[...] = gr_ref[...]

    @pl.when(step < last)
    def _():
        gact = nt(gd_ref[...], wd_ref[...])
        gup = (gact * slope_ref[0].astype(f32)).astype(bf16)
        gug_ref[0] = gup
        bup_ref[0] = jnp.sum(gup.astype(f32), 0, keepdims=True)
        acc[...] += nt(gup, wu_ref[...])

    @pl.when(step == last)
    def _():
        grad = acc[...]
        xhat = xhat_ref[...]
        back = norm_back(grad, xhat, inv_ref[...], go_ref[...])
        gr1_ref[...] = back
        gab = back.astype(bf16)
        gug_ref[0] = gab
        gctx_ref[...] = nt(gab, wo_ref[...]).astype(bf16)
        sums_ref[0:1, :] = jnp.sum(gab.astype(f32), 0, keepdims=True)
        sums_ref[1:2, :] = jnp.sum(grad * xhat, 0, keepdims=True)
        sums_ref[2:3, :] = jnp.sum(grad, 0, keepdims=True)


def feed_back(sc, gd, gr, wd, wu, slope, xhat, inv, go, wo, deps):
    length, d = gd.shape
    steps = slope.shape[0]
    at = lambda i: jnp.minimum(i, steps - 1)
    return call(
        feed_back_kernel,
        sc,
        (gd, gr, *far(wd, wu, slope, xhat, inv), go, *far(wo)),
        [
            whole(length, d), whole(length, d),
            pl.BlockSpec((d, d), lambda i, s: (at(i), 0)),
            pl.BlockSpec((d, d), lambda i, s: (0, at(i))),
            pl.BlockSpec((1, length, d), lambda i, s: (at(i), 0, 0)),
            whole(length, d), whole(length, 1), whole(1, d), whole(d, d),
        ],
        [
            shape(bf16, steps + 1, length, d), shape(f32, steps, 1, d), shape(f32, length, d),
            shape(bf16, length, d), shape(f32, SLOT, d),
        ],
        [
            pl.BlockSpec((1, length, d), lambda i, s: (i, 0, 0)),
            pl.BlockSpec((1, 1, d), lambda i, s: (at(i), 0, 0)),
            whole(length, d), whole(length, d), whole(SLOT, d),
        ],
        (steps + 1,),
        [pltpu.VMEM((length, d), f32)],
        "feed_back", 0, deps,
    )


def attention_back_kernel(
    piece, sc_ref, q_ref, k_ref, v_ref, gctx_ref, lse_ref, wq_ref, wk_ref, wv_ref, gr_ref,
    gq_ref, gk_ref, gv_ref, gtok_ref, sums_ref,
    acc, bias, gkt, gvt,
):
    step = pl.program_id(0)
    length = q_ref.shape[0]

    @pl.when(step == 0)
    def _():
        bias[...] = segment_bias(sc_ref, length, piece)
        acc[...] = gr_ref[...]

    lse = lse_ref[0].T
    for h in range(GROUP):
        cols = slice(h * HEAD, (h + 1) * HEAD)
        q = q_ref[:, cols]
        k = k_ref[:, cols]
        gctx = gctx_ref[:, cols]
        scores = nt(q * jnp.asarray(SCALE, bf16), k) + bias[...]
        p = jnp.exp(scores - lse[:, h : h + 1])
        ga = nt(gctx, v_ref[:, cols])
        dots = jnp.sum(p * ga, -1, keepdims=True)
        g = (p * (ga - dots)).astype(bf16)
        gq_ref[:, cols] = (nn(g, k) * SCALE).astype(bf16)
        gkt[cols, :] = (tn(q, g) * SCALE).astype(bf16)
        gvt[cols, :] = tn(gctx, p.astype(bf16)).astype(bf16)
    gk_ref[...] = gkt[...].T
    gv_ref[...] = gvt[...].T
    gq, gk, gv = gq_ref[...], gk_ref[...], gv_ref[...]
    sums_ref[0:1, :] = jnp.sum(gq.astype(f32), 0, keepdims=True)
    sums_ref[1:2, :] = jnp.sum(gv.astype(f32), 0, keepdims=True)
    acc[...] += nt(gq, wq_ref[...]) + nt(gk, wk_ref[...]) + nt(gv, wv_ref[...])

    @pl.when(step == pl.num_programs(0) - 1)
    def _():
        gtok_ref[...] = acc[...].astype(bf16)


def attention_back(sc, q, k, v, gctx, lse, wq, wk, wv, gr, piece, deps):
    length, d = q.shape
    wide = GROUP * HEAD
    steps = d // wide
    cols = lambda r: pl.BlockSpec((r, wide), lambda i, s: (0, i))
    return call(
        functools.partial(attention_back_kernel, piece),
        sc,
        (*far(q, k, v), gctx, *far(lse, wq, wk, wv), gr),
        [
            cols(length), cols(length), cols(length), cols(length),
            pl.BlockSpec((1, SLOT, length), lambda i, s: (i, 0, 0)),
            cols(d), cols(d), cols(d), whole(length, d),
        ],
        [shape(bf16, length, d)] * 4 + [shape(f32, SLOT, d)],
        [cols(length), cols(length), cols(length), whole(length, d), cols(SLOT)],
        (steps,),
        [
            pltpu.VMEM((length, d), f32), pltpu.VMEM((length, length), f32),
            pltpu.VMEM((wide, length), bf16), pltpu.VMEM((wide, length), bf16),
        ],
        "attention_back", 0, deps,
    )


def weight_total(two, lo_refs, lp_ref, go_ref, gp_ref):
    lo = lo_refs[0][...].reshape(lo_refs[0].shape[-2:])
    if len(lo_refs) > 1:
        lo = jnp.where(pl.program_id(0) < two, lo, lo_refs[1][...].reshape(lo.shape))
    return nn(lo, go_ref[0]) + nn(lp_ref[0, 0], gp_ref[0])


def weight_send_kernel(lefts, two, sc_ref, *refs):
    lo_refs, (lp_ref, go_ref, gp_ref, out_ref) = refs[:lefts], refs[lefts:]
    out_ref[0] = weight_total(two, lo_refs, lp_ref, go_ref, gp_ref).astype(bf16)


def deal(sc_ref, total, step, keep_ref, send_ref):
    rows = total.shape[0] // 4
    spot = pl.ds(step * rows if isinstance(step, int) else pl.multiple_of(step * rows, rows), rows)
    for h in range(2):
        for z in range(2):
            part = total[(2 * h + z) * rows : (2 * h + z + 1) * rows].astype(bf16)

            @pl.when(sc_ref[2] == h)
            def _():
                keep_ref[sc_ref[3] ^ z, spot, :] = part

            @pl.when(sc_ref[2] != h)
            def _():
                send_ref[sc_ref[3] ^ z, spot, :] = part


def weight_keep_kernel(lefts, two, sc_ref, *refs):
    lo_refs, (lp_ref, go_ref, gp_ref, recv_ref, keep_ref, send_ref) = refs[:lefts], refs[lefts:]
    total = weight_total(two, lo_refs, lp_ref, go_ref, gp_ref) + recv_ref[0].astype(f32)
    deal(sc_ref, total, pl.program_id(0), keep_ref, send_ref)


def pack_kernel(sc_ref, qkv_ref, one_ref, two_ref, bup_ref, own_ref, far_ref):
    rows = jnp.concatenate([qkv_ref[0:2], one_ref[0:3], two_ref[0:3]], 0)
    quarter = rows.shape[1] // 4
    own_ref[...] = jnp.zeros_like(own_ref)
    far_ref[...] = jnp.zeros_like(far_ref)
    for x in range(2):
        for c in range(2):
            q = 2 * x + c
            left = rows[:, q * quarter : (q + 1) * quarter]

            def put(ref):
                ref[x, 0:8, :quarter] = left
                for j in range(4):
                    ref[x, 8 + j : 9 + j, :quarter] = bup_ref[q, :, j * quarter : (j + 1) * quarter]

            @pl.when(sc_ref[1] == c)
            def _():
                put(own_ref)

            @pl.when(sc_ref[1] != c)
            def _():
                put(far_ref)


def pack(sc, qkv, one, two, bup):
    out = shape(f32, 2, EXTRA, 2 * SMALL)
    return call(
        pack_kernel, sc, (qkv, one, two, bup), [whole(*t.shape) for t in (qkv, one, two, bup)],
        [out, out], [whole(*out.shape)] * 2, (1,), [], "pack", 0,
    )


def qkv_totals(lo_ref, lp_ref, own, par):
    return [nn(lo_ref[0], o[...]) + nn(lp_ref[0, 0], p[...]) for o, p in zip(own, par)]


def qkv_send_kernel(sc_ref, lo_ref, lp_ref, own_ref, par_ref, *refs):
    out_ref = refs[6]
    rows = lo_ref.shape[1]
    for n, total in enumerate(qkv_totals(lo_ref, lp_ref, refs[:3], refs[3:6])):
        out_ref[n * rows : (n + 1) * rows, :] = total.astype(bf16)
    vec = own_ref[1 - sc_ref[0]] + par_ref[1 - sc_ref[0]]
    out_ref[3 * rows :, :] = jnp.zeros((EXTRA, out_ref.shape[1]), bf16)
    out_ref[3 * rows :, : vec.shape[1]] = vec.astype(bf16)


def qkv_keep_kernel(sc_ref, lo_ref, lp_ref, own_ref, par_ref, *refs):
    recv_ref, keep_ref, send_ref = refs[6:]
    rows = lo_ref.shape[1]
    for n, total in enumerate(qkv_totals(lo_ref, lp_ref, refs[:3], refs[3:6])):
        total += recv_ref[n * rows : (n + 1) * rows, :].astype(f32)
        deal(sc_ref, total, n, keep_ref, send_ref)
    base = keep_ref.shape[1] - EXTRA
    vec = own_ref[sc_ref[0]] + par_ref[sc_ref[0]]
    wide = vec.shape[1]
    vec += recv_ref[3 * rows :, :wide].astype(f32)
    blank = jnp.zeros((EXTRA, keep_ref.shape[2]), bf16)
    for ref in (keep_ref, send_ref):
        for z in range(2):
            ref[z, base:, :] = blank
            ref[z, base:, :wide] = vec.astype(bf16)


def qkv_specs(xt, halves, own, other):
    x = (lambda s: 1 - s[0]) if other else (lambda s: s[0])
    return [
        pl.BlockSpec((1,) + xt.shape[1:], lambda i, s: (2 * x(s) + s[1], 0, 0)),
        pl.BlockSpec((1, 1) + halves.shape[2:], lambda i, s: (x(s), 2, 0, 0)),
    ] + [whole(2, EXTRA, 2 * SMALL)] * 2 + [whole(*own.shape)] * 6


def qkv_send(sc, operands, deps):
    xt, halves, _, _, own = operands[:5]
    rows, wide = xt.shape[1], own.shape[1]
    out = shape(bf16, 3 * rows + EXTRA, wide)
    return call(
        qkv_send_kernel, sc, far(xt, halves) + operands[2:], qkv_specs(xt, halves, own, True), out, whole(*out.shape),
        (1,), [], "qkv_send", 0, deps,
    )


def qkv_keep(sc, operands, recv, deps):
    xt, halves, _, _, own = operands[:5]
    rows, wide = xt.shape[1], own.shape[1]
    out = shape(bf16, 2, 3 * rows // 4 + EXTRA, wide)
    return call(
        qkv_keep_kernel, sc, far(xt, halves) + operands[2:] + (recv,),
        qkv_specs(xt, halves, own, False) + [whole(*recv.shape)],
        [out, out], [whole(*out.shape)] * 2, (1,), [], "qkv_keep", 0, deps,
    )


def order_kernel(sc_ref, *refs):
    out_ref = refs[-1]
    for mask, piece in enumerate(refs[:-1]):
        out_ref[sc_ref[0] ^ mask] = piece[...]


def weight_specs(lefts, halves, grads, grads_p, other, steps, turn):
    x = (lambda s: 1 - s[0]) if other else (lambda s: s[0])
    specs = []
    for left in lefts:
        if left.ndim == 4:
            specs.append(
                pl.BlockSpec((1, 1) + left.shape[2:], lambda i, s: (2 * x(s) + s[1], i, 0, 0))
            )
        else:
            specs.append(pl.BlockSpec((1,) + left.shape[1:], lambda i, s: (2 * x(s) + s[1], 0, 0)))
    specs.append(pl.BlockSpec((1, 1) + halves.shape[2:], lambda i, s: (x(s), turn(i), 0, 0)))
    one = grads.shape[0] == 1
    block = pl.BlockSpec((1,) + grads.shape[1:], lambda i, s: (0 if one else i, 0, 0))
    return (*far(*lefts), *far(halves), grads, grads_p), specs + [block, block]


def weight_send(sc, operands, steps, two, turn, name, deps=(), micros=0):
    args, specs = weight_specs(*operands, True, steps, turn)
    rows, wide = operands[1].shape[2], operands[2].shape[2]
    return call(
        functools.partial(weight_send_kernel, len(operands[0]), two),
        sc, args, specs, shape(bf16, steps, rows, wide),
        pl.BlockSpec((1, rows, wide), lambda i, s: (i, 0, 0)), (steps,), [],
        name, micros, deps,
    )


def weight_keep(sc, operands, recv, steps, two, turn, name, deps=(), micros=0):
    args, specs = weight_specs(*operands, False, steps, turn)
    rows, wide = operands[1].shape[2], operands[2].shape[2]
    out = shape(bf16, 2, steps * rows // 4, wide)
    return call(
        functools.partial(weight_keep_kernel, len(operands[0]), two),
        sc, args + (recv,), specs + [pl.BlockSpec((1, rows, wide), lambda i, s: (i, 0, 0))],
        [out, out], [whole(*out.shape)] * 2, (steps,), [],
        name, micros, deps,
    )


def place_kernel(spots, extra, sc_ref, *refs):
    parts, out_refs = refs[:4], refs[4:]
    rows = (parts[0].shape[0] - extra) // len(spots)
    wide = parts[0].shape[1]
    for side, part in enumerate(parts):
        slot = 2 * (sc_ref[2] ^ (side // 2)) + (sc_ref[3] ^ (side % 2))
        for n, (out, down, left) in enumerate(spots):
            top = pl.multiple_of((4 * down + slot) * rows, rows)
            out_refs[out][pl.ds(top, rows), left * wide : (left + 1) * wide] = part[
                n * rows : (n + 1) * rows, :
            ].astype(f32)
    if extra:
        small = out_refs[-1]
        small[...] = parts[0][len(spots) * rows :, : small.shape[1]].astype(f32)


def place(sc, parts, spots, dims, extra, name):
    return call(
        functools.partial(place_kernel, spots, extra),
        sc, parts, [whole(*parts[0].shape)] * 4,
        [shape(f32, *dim) for dim in dims], [whole(*dim) for dim in dims], (1,), [],
        name, 0,
    )


def flip(value, axis, mask):
    count = lax.axis_size(axis)
    return lax.ppermute(value, axis, [(i, i ^ mask) for i in range(count)])


def flip_both(value, row_mask, seq_mask):
    rows, seq = lax.axis_size("rows"), lax.axis_size("seq")
    pairs = [
        (r * seq + s, (r ^ row_mask) * seq + (s ^ seq_mask)) for r in range(rows) for s in range(seq)
    ]
    return lax.ppermute(value, ("rows", "seq"), pairs)


def row_flips():
    count = lax.axis_size("rows")
    assert count >= 8 and count & (count - 1) == 0
    return [2, 6] + [1 << b for b in range(3, count.bit_length() - 1)]


def join_kernel(sc_ref, left_ref, right_ref, out_ref):
    out_ref[...] = (left_ref[...].astype(f32) + right_ref[...].astype(f32)).astype(bf16)


def join(sc, left, right, deps):
    block = whole(*left.shape)
    return call(
        join_kernel, sc, (left, right), [block, block], shape(bf16, *left.shape), block, (1,), [],
        "join", 0, deps,
    )


def over_rows(sc, keep, send, masks, deps=(), later=()):
    near, *rest = masks
    value = keep
    if send is not None:
        got = flip(send, "rows", 1)
        value = join(sc, keep, got, deps) if deps else add(keep, got)
    got = flip(value[1], "rows", near)
    value = join(sc, value[0], got, later) if later else add(value[0], got)
    for mask in rest:
        value = add(value, flip(value, "rows", mask))
    return tuple([value] + [flip(value, "rows", mask) for mask in (near, 1, near ^ 1)])


def add(left, right):
    return (left.astype(f32) + right.astype(f32)).astype(bf16)


def spread(rows):
    own = lax.axis_index("seq")
    count = lax.axis_size("seq")
    assert rows.shape[0] == count
    pieces = [
        flip(lax.dynamic_index_in_dim(rows, own ^ mask, 0, keepdims=False), "seq", mask)
        if mask
        else lax.dynamic_index_in_dim(rows, own, 0, keepdims=False)
        for mask in range(count)
    ]
    return jnp.concatenate(pieces, 0)


def gather_back(sc, row, count, name, deps=()):
    row = row.reshape(count, -1, row.shape[-1])
    pieces = tuple(flip(row[mask], "seq", mask) if mask else row[0] for mask in range(count))
    return call(
        order_kernel, sc, pieces, [whole(*row.shape[1:])] * count, shape(row.dtype, *row.shape),
        whole(*row.shape), (1,), [], name, 0, deps,
    )


def per_device(
    tokens,
    w_query,
    b_query,
    w_key,
    w_value,
    b_value,
    w_out,
    b_out,
    gain_one,
    shift_one,
    w_up,
    b_up,
    w_down,
    b_down,
    gain_two,
    shift_two,
    passage_starts,
    queries,
    choices,
    cotangent,
):
    seq_count = lax.axis_size("seq")
    row_count = lax.axis_size("rows")
    own_s = lax.axis_index("seq")
    own_r = lax.axis_index("rows")
    row_block, piece, d = tokens.shape
    assert row_block == seq_count == 4
    ff = w_up.shape[1]
    quarter = d // 4
    core, xside = own_s % 2, own_s // 2
    own_lin = own_r * seq_count + own_s
    devices = row_count * seq_count
    masks = row_flips()
    wsc = jnp.stack([xside, core, own_r % 2, (own_r // 2 ^ own_r // 4) % 2]).astype(jnp.int32)
    starts = lax.dynamic_index_in_dim(passage_starts, own_s, 0, keepdims=False)
    sc = jnp.concatenate([own_s[None].astype(jnp.int32), starts, own_lin[None].astype(jnp.int32)])
    row = lambda v: v.reshape(1, -1)
    swap = lambda t: flip(t, "seq", 1)

    x = spread(tokens)

    code = jnp.concatenate(
        [queries, (choices // PASS).astype(bf16), (choices % PASS).astype(bf16)], axis=1
    )
    code_all = lax.all_gather(code, ("rows", "seq"), axis=0, tiled=True)

    cot = spread(cotangent)

    q, k, v, ctxt, lse, xt, xhat_one, inv_one, hid, hidt = attention_forward(
        sc, x, w_query, w_key, w_value, row(b_query), row(b_value), w_out, row(b_out),
        row(gain_one), row(shift_one), piece,
    )
    actt, slope, xhat_two, inv_two, mixed_row, pool = feed_forward(
        sc, hid, w_up, row(b_up), w_down, row(b_down), row(gain_two), row(shift_two), piece, (cot,)
    )

    pool = pool.astype(bf16)
    if row_count == 8:
        near = jnp.concatenate(
            [pool, flip(pool, "seq", 2), flip(pool, "rows", 1), flip_both(pool, 1, 2)], 0
        )
        mid = jnp.concatenate(
            [near, flip(near, "rows", 2), flip(near, "rows", 6), flip(near, "rows", 4)], 0
        )
        pooled = jnp.concatenate([mid, flip(mid, "seq", 1)], 0)
        places = cube_place
    else:
        pooled = lax.all_gather(pool, ("rows", "seq"), axis=0, tiled=True)
        pooled = jnp.roll(pooled, -own_lin * SLOT, 0)
        places = turned_place

    other_half = lambda t: lax.dynamic_index_in_dim(
        t.reshape(2, 2, -1, quarter, t.shape[-1]), 1 - core, 1, keepdims=False
    )
    halves = swap(
        jnp.concatenate([other_half(hidt), other_half(ctxt), other_half(xt), other_half(actt)], 1)
    )
    quarters = lambda t: t.reshape(4, -1, t.shape[-1])

    losses_all, gd, gr_two, sums_two = retrieval(
        sc, code_all, pooled, cot, xhat_two, inv_two, row(gain_two), piece, places, devices,
        (halves,),
    )
    query_losses = lax.dynamic_slice_in_dim(
        losses_all[:, 0], own_lin * queries.shape[0], queries.shape[0]
    )

    gd_p = swap(gd)
    gug, bup, gr_one, gctx, sums_one = feed_back(
        sc, gd, gr_two, w_down, w_up, slope, xhat_one, inv_one, row(gain_one), w_out, (gd_p,)
    )
    down_ops = ((actt.reshape(4, 4, quarter, -1),), halves, gd[None], gd_p[None])
    down_turn = lambda i: 3 + i
    down_sent = weight_send(wsc, down_ops, 4, 0, down_turn, "down_send", (gug,))
    down_got = flip(down_sent, "seq", 2)

    up_ops = ((quarters(hidt), quarters(ctxt)), halves, gug, swap(gug))
    up_turn = lambda i: i // 4
    up_sent = weight_send(wsc, up_ops, 5, 4, up_turn, "up_send", (down_sent,))
    up_got = flip(up_sent, "seq", 2)

    gq, gk, gv, gtok, sums_qkv = attention_back(
        sc, q, k, v, gctx, lse, w_query, w_key, w_value, gr_one, piece, (up_sent,)
    )
    vec, vec_far = pack(wsc, sums_qkv, sums_one, sums_two, bup)
    qkv_ops = (
        quarters(xt), halves, vec, swap(vec_far), gq, gk, gv, swap(gq), swap(gk), swap(gv)
    )
    up_parts = weight_keep(wsc, up_ops, up_got, 5, 4, up_turn, "up_keep", (vec,))
    qkv_sent = qkv_send(wsc, qkv_ops, (up_parts[0],))
    qkv_got = flip(qkv_sent, "seq", 2)
    up_got_rows = flip(up_parts[1], "rows", 1)
    up_first = join(wsc, up_parts[0], up_got_rows, (qkv_sent,))
    down_parts = weight_keep(
        wsc, down_ops, down_got, 4, 0, down_turn, "down_keep", (up_first,), PIN
    )
    qkv_parts = qkv_keep(wsc, qkv_ops, qkv_got, (down_parts[0],))
    up_sum = over_rows(wsc, up_first, None, masks, later=(qkv_parts[0],))
    down_sum = over_rows(wsc, *down_parts, masks, (qkv_parts[0],))
    qkv_sum = over_rows(wsc, *qkv_parts, masks)

    mixed = gather_back(sc, mixed_row, seq_count, "mixed_order", (qkv_sent,))
    grad_tokens = gather_back(sc, gtok, seq_count, "tokens_order", (qkv_parts[0],))

    (grad_down,) = place(
        wsc, down_sum, [(0, n, 0) for n in range(4)], [(4 * quarter, d)], 0, "down_place"
    )
    grad_up, grad_o = place(
        wsc, up_sum, [(0, 0, n) for n in range(4)] + [(1, 0, 0)],
        [(quarter, ff), (quarter, d)], 0, "up_place",
    )
    grad_q, grad_k, grad_v, small = place(
        wsc, qkv_sum, [(n, 0, 0) for n in range(3)], [(quarter, d)] * 3 + [(EXTRA, 2 * SMALL)],
        EXTRA, "qkv_place",
    )

    eight = small[:, :quarter]
    return (
        mixed,
        query_losses,
        grad_tokens,
        grad_q,
        eight[0],
        grad_k,
        grad_v,
        eight[1],
        grad_o,
        eight[2],
        eight[3],
        eight[4],
        grad_up,
        eight[8:12].reshape(-1),
        grad_down,
        eight[5],
        eight[6],
        eight[7],
    )


def solution(mesh):
    weights = (P(),) * 15
    placed = (
        (P("rows", "seq", None),)
        + weights
        + (
            P("rows", None),
            P(("rows", "seq"), None),
            P(("rows", "seq"), None),
            P("rows", "seq", None),
        )
    )
    return jax.shard_map(
        per_device,
        mesh=mesh,
        in_specs=placed,
        out_specs=(
            P("rows", "seq", None),
            P(("rows", "seq")),
            P("rows", "seq", None),
            P("seq", None),
            P("seq"),
            P("seq", None),
            P("seq", None),
            P("seq"),
            P("seq", None),
            P("seq"),
            P("seq"),
            P("seq"),
            P("seq", None),
            P("seq"),
            P("seq", None),
            P("seq"),
            P("seq"),
            P("seq"),
        ),
        check_vma=False,
    )
```

```python
import functools

import jax
import jax.numpy as jnp
from jax import lax
from jax.experimental import pallas as pl
from jax.experimental.pallas import tpu as pltpu
from jax.sharding import PartitionSpec as P

HEADS = 12
HEAD = 64
PASS = 6
CH = 32
SLOT = 8
GROUP = 4
SUB = 384
SCALE = HEAD ** (-0.5)

norm_eps = 1e-05
f32 = jnp.float32
bf16 = jnp.bfloat16
VMEM_BYTES = 28 * 1024 * 1024
PIN = 100
EXTRA = 16
SMALL = 128


def params():
    return pltpu.CompilerParams(vmem_limit_bytes=VMEM_BYTES)


def cost(micros):
    return pl.CostEstimate(flops=int(micros * 1.15e9), bytes_accessed=0, transcendentals=0)


def nt(a, b):
    return lax.dot_general(a, b, (((1,), (1,)), ((), ())), preferred_element_type=f32)


def tn(a, b):
    return lax.dot_general(a, b, (((0,), (0,)), ((), ())), preferred_element_type=f32)


def nn(a, b):
    return jnp.dot(a, b, preferred_element_type=f32)


def stats(values):
    center = values - jnp.mean(values, -1, keepdims=True)
    inv = lax.rsqrt(jnp.mean(center * center, -1, keepdims=True) + norm_eps)
    return center * inv, inv


def norm_back(grad, xhat, inv, gain):
    gx = grad * gain
    return inv * (
        gx - jnp.mean(gx, -1, keepdims=True) - xhat * jnp.mean(gx * xhat, -1, keepdims=True)
    )


def true_places(own_seq, count, piece, axis):
    shape = (count, 1) if axis == 0 else (1, count)
    local = lax.broadcasted_iota(jnp.int32, shape, axis)
    block = local // piece
    return (block ^ own_seq) * piece + (local - block * piece)


def segments(sc_ref, places):
    total = jnp.zeros(places.shape, jnp.int32)
    for j in range(PASS):
        total += (sc_ref[1 + j] <= places).astype(jnp.int32)
    return total


def segment_bias(sc_ref, length, piece):
    col = segments(sc_ref, true_places(sc_ref[0], length, piece, 0))
    row = segments(sc_ref, true_places(sc_ref[0], length, piece, 1))
    return jnp.where(col == row, 0.0, -1e30)


def call(kernel, sc, args, specs, outs, out_specs, grid, scratch, name, micros, deps=()):
    count = len(args)

    def body(sc_ref, *refs):
        kernel(sc_ref, *refs[:count], *refs[count + len(deps) :])

    hold = pl.BlockSpec(memory_space=pl.ANY)
    return pl.pallas_call(
        body,
        grid_spec=pltpu.PrefetchScalarGridSpec(
            num_scalar_prefetch=1,
            grid=grid,
            in_specs=list(specs) + [hold] * len(deps),
            out_specs=out_specs,
            scratch_shapes=scratch,
        ),
        out_shape=outs,
        compiler_params=params(),
        cost_estimate=cost(micros),
        name=name,
    )(sc, *args, *deps)


def shape(t, *dims):
    return jax.ShapeDtypeStruct(dims, t)


def kept(t, *dims):
    return pltpu.HBM(dims, t)


def far(*values):
    return tuple(pltpu.with_memory_space_constraint(v, pltpu.HBM) for v in values)


def whole(*dims):
    return pl.BlockSpec(dims, lambda i, s: (0,) * len(dims))


def attention_kernel(
    piece, sc_ref, x_ref, wq_ref, wk_ref, wv_ref, bq_ref, bv_ref, wo_ref, bo_ref, go_ref, so_ref,
    q_ref, k_ref, v_ref, ctxt_ref, lse_ref, xt_ref, xhat_ref, inv_ref, hid_ref, hidt_ref,
    acc, bias,
):
    step = pl.program_id(0)
    length = x_ref.shape[0]
    x = x_ref[...]
    q_ref[...] = (nn(x, wq_ref[...]) + bq_ref[...]).astype(bf16)
    k_ref[...] = nn(x, wk_ref[...]).astype(bf16)
    v_ref[...] = (nn(x, wv_ref[...]) + bv_ref[...]).astype(bf16)

    @pl.when(step == 0)
    def _():
        bias[...] = segment_bias(sc_ref, length, piece)
        acc[...] = x.astype(f32) + bo_ref[...]

    for h in range(GROUP):
        cols = slice(h * HEAD, (h + 1) * HEAD)
        raw = nt(k_ref[:, cols], q_ref[:, cols] * jnp.asarray(SCALE, bf16))
        scores = raw + bias[...]
        top = jnp.max(scores, 0, keepdims=True)
        e = jnp.exp(scores - top)
        total = jnp.sum(e, 0, keepdims=True)
        p = (e * (1.0 / total)).astype(bf16)
        ctxt_ref[cols, :] = tn(v_ref[:, cols], p).astype(bf16)
        lse_ref[0, h : h + 1, :] = top + jnp.log(total)
    acc[...] += tn(ctxt_ref[...], wo_ref[...])

    for j in range(x_ref.shape[1] // xt_ref.shape[0]):
        wide = xt_ref.shape[0]

        @pl.when(step == j)
        def _():
            xt_ref[...] = x_ref[:, j * wide : (j + 1) * wide].T

    @pl.when(step == pl.num_programs(0) - 1)
    def _():
        xhat, inv = stats(acc[...])
        xhat_ref[...] = xhat
        inv_ref[...] = inv
        hid = (xhat * go_ref[...] + so_ref[...]).astype(bf16)
        hid_ref[...] = hid
        hidt_ref[...] = hid.T


def attention_forward(sc, x, wq, wk, wv, bq, bv, wo, bo, go, so, piece):
    length, d = x.shape
    wide = GROUP * HEAD
    steps = d // wide
    cols = lambda r: pl.BlockSpec((r, wide), lambda i, s: (0, i))
    rows = lambda c: pl.BlockSpec((wide, c), lambda i, s: (i, 0))
    return call(
        functools.partial(attention_kernel, piece),
        sc,
        (x, *far(wq, wk, wv), bq, bv, *far(wo), bo, go, so),
        [
            whole(length, d), cols(d), cols(d), cols(d), cols(1), cols(1), rows(d),
            whole(1, d), whole(1, d), whole(1, d),
        ],
        [
            kept(bf16, length, d), kept(bf16, length, d), kept(bf16, length, d),
            kept(bf16, d, length), kept(f32, steps, SLOT, length), kept(bf16, d, length),
            kept(f32, length, d), kept(f32, length, 1), shape(bf16, length, d),
            kept(bf16, d, length),
        ],
        [
            cols(length), cols(length), cols(length), rows(length),
            pl.BlockSpec((1, SLOT, length), lambda i, s: (i, 0, 0)), rows(length),
            whole(length, d), whole(length, 1), whole(length, d), whole(d, length),
        ],
        (steps,),
        [pltpu.VMEM((length, d), f32), pltpu.VMEM((length, length), f32)],
        "attention_forward", 0,
    )


def feed_kernel(
    piece, sc_ref, hid_ref, wu_ref, bu_ref, wd_ref, bd_ref, gt_ref, st_ref,
    actt_ref, slope_ref, xhat_ref, inv_ref, mixed_ref, pool_ref,
    acc,
):
    step = pl.program_id(0)
    length = hid_ref.shape[0]

    @pl.when(step == 0)
    def _():
        acc[...] = hid_ref[...].astype(f32) + bd_ref[...]

    for c in range(0, wu_ref.shape[1], SUB):
        cols = slice(c, c + SUB)
        up = nn(hid_ref[...], wu_ref[:, cols]) + bu_ref[:, cols]
        e = jnp.exp(-0.5 * up * up)
        cum = 0.5 + 0.5 * lax.erf(up * (2.0 ** -0.5))
        slope_ref[0, :, cols] = (cum + up * (e * 0.3989422804014327)).astype(bf16)
        act = (up * cum).astype(bf16)
        actt_ref[cols, :] = act.T
        acc[...] += nn(act, wd_ref[cols, :])

    @pl.when(step == pl.num_programs(0) - 1)
    def _():
        xhat, inv = stats(acc[...])
        xhat_ref[...] = xhat
        inv_ref[...] = inv
        mixed = (xhat * gt_ref[...] + st_ref[...]).astype(bf16)
        mixed_ref[...] = mixed
        places = true_places(sc_ref[0], length, piece, 1)
        slot = lax.broadcasted_iota(jnp.int32, (SLOT, 1), 0)
        start = jnp.full((SLOT, 1), -1, jnp.int32)
        for j in range(PASS):
            start = jnp.where(slot == j, sc_ref[1 + j], start)
        pool_ref[...] = nn((places == start).astype(f32).astype(bf16), mixed)


def feed_forward(sc, hid, wu, bu, wd, bd, gt, st, piece, deps):
    length, d = hid.shape
    ff = wu.shape[1]
    steps = ff // d
    return call(
        functools.partial(feed_kernel, piece),
        sc,
        (hid, *far(wu), bu, *far(wd), bd, gt, st),
        [
            whole(length, d),
            pl.BlockSpec((d, d), lambda i, s: (0, i)),
            pl.BlockSpec((1, d), lambda i, s: (0, i)),
            pl.BlockSpec((d, d), lambda i, s: (i, 0)),
            whole(1, d), whole(1, d), whole(1, d),
        ],
        [
            kept(bf16, ff, length), kept(bf16, steps, length, d), kept(f32, length, d),
            kept(f32, length, 1), kept(bf16, length, d), shape(f32, SLOT, d),
        ],
        [
            pl.BlockSpec((d, length), lambda i, s: (i, 0)),
            pl.BlockSpec((1, length, d), lambda i, s: (i, 0, 0)),
            whole(length, d), whole(length, 1), whole(length, d), whole(SLOT, d),
        ],
        (steps,),
        [pltpu.VMEM((length, d), f32)],
        "feed_forward", 0, deps,
    )


def loss_kernel(
    piece, steps, devices, code_ref, sc_ref, q_ref, pool_ref, cot_ref, xhat_ref, inv_ref, gt_ref,
    loss_ref, gd_ref, gr_ref, sums_ref, gp,
):
    step = pl.program_id(0)
    d = pool_ref.shape[1]

    @pl.when(step == 0)
    def _():
        gp[...] = jnp.zeros_like(gp)
        sums_ref[...] = jnp.zeros_like(sums_ref)

    @pl.when(step < steps)
    def _():
        queries = q_ref[:, :d]
        logits = nt(queries, pool_ref[...])
        lanes = lax.broadcasted_iota(jnp.int32, (1, logits.shape[1]), 1)
        owner = q_ref[:, d : d + CH].astype(f32).astype(jnp.int32)
        inner = q_ref[:, d + CH :].astype(f32).astype(jnp.int32)
        pos = code_ref(owner, sc_ref[7], devices) * SLOT + inner
        first = (pos[:, 0:1] == lanes).astype(f32)
        times = first
        for c in range(1, CH):
            times += (pos[:, c : c + 1] == lanes).astype(f32)
        held = times > 0.0
        top = jnp.max(jnp.where(held, logits, -jnp.inf), -1, keepdims=True)
        e = jnp.where(held, times * jnp.exp(jnp.minimum(logits - top, 0.0)), 0.0)
        total = jnp.sum(e, -1, keepdims=True)
        positive = jnp.sum(first * logits, -1, keepdims=True)
        loss_ref[...] = top + jnp.log(total) - positive
        grad = e[:, :128] * (1.0 / total) - first[:, :128]
        high = grad.astype(bf16)
        lower = (grad - high.astype(f32)).astype(bf16)
        gp[...] += (tn(high, queries) + tn(lower, queries))[:SLOT]

    @pl.when(step >= steps)
    def _():
        block = (step - steps) ^ sc_ref[0]
        places = block * piece + lax.broadcasted_iota(jnp.int32, (piece, 1), 0)
        grad = cot_ref[...].astype(f32)
        for j in range(PASS):
            grad += jnp.where(places == sc_ref[1 + j], gp[j : j + 1, :], 0.0)
        xhat = xhat_ref[...]
        back = norm_back(grad, xhat, inv_ref[...], gt_ref[...])
        gr_ref[...] = back
        down = back.astype(bf16)
        gd_ref[...] = down
        sums_ref[0:1, :] += jnp.sum(down.astype(f32), 0, keepdims=True)
        sums_ref[1:2, :] += jnp.sum(grad * xhat, 0, keepdims=True)
        sums_ref[2:3, :] += jnp.sum(grad, 0, keepdims=True)


def cube_place(owner, own, devices):
    off = owner ^ own
    z = off >> 3
    return (off & 1) * 16 + (z ^ (z >> 1)) * 4 + ((off >> 1) & 3)


def turned_place(owner, own, devices):
    off = owner - own
    return jnp.where(off < 0, off + devices, off)


def retrieval(sc, code_all, pooled, cot, xhat, inv, gain, piece, places, devices, deps):
    count, width = code_all.shape
    length, d = cot.shape
    block = 256
    steps, pieces = count // block, length // piece
    first = lambda i: jnp.minimum(i, steps - 1)
    second = lambda i: jnp.maximum(i - steps, 0)
    part = lambda c: pl.BlockSpec((piece, c), lambda i, s: (second(i), 0))
    return call(
        functools.partial(loss_kernel, piece, steps, devices, places),
        sc,
        (*far(code_all), pooled, *far(cot, xhat, inv), gain),
        [
            pl.BlockSpec((block, width), lambda i, s: (first(i), 0)),
            whole(*pooled.shape), part(d), part(d), part(1), whole(1, d),
        ],
        [shape(f32, count, 1), shape(bf16, length, d), shape(f32, length, d), shape(f32, SLOT, d)],
        [
            pl.BlockSpec((block, 1), lambda i, s: (first(i), 0)), part(d), part(d), whole(SLOT, d),
        ],
        (steps + pieces,),
        [pltpu.VMEM((SLOT, d), f32)],
        "retrieval", 0, deps,
    )


def feed_back_kernel(
    sc_ref, gd_ref, gr_ref, wd_ref, wu_ref, slope_ref, xhat_ref, inv_ref, go_ref, wo_ref,
    gug_ref, bup_ref, gr1_ref, gctx_ref, sums_ref,
    acc,
):
    step = pl.program_id(0)
    last = pl.num_programs(0) - 1

    @pl.when(step == 0)
    def _():
        acc[...] = gr_ref[...]

    @pl.when(step < last)
    def _():
        gact = nt(gd_ref[...], wd_ref[...])
        gup = (gact * slope_ref[0].astype(f32)).astype(bf16)
        gug_ref[0] = gup
        bup_ref[0] = jnp.sum(gup.astype(f32), 0, keepdims=True)
        acc[...] += nt(gup, wu_ref[...])

    @pl.when(step == last)
    def _():
        grad = acc[...]
        xhat = xhat_ref[...]
        back = norm_back(grad, xhat, inv_ref[...], go_ref[...])
        gr1_ref[...] = back
        gab = back.astype(bf16)
        gug_ref[0] = gab
        gctx_ref[...] = nt(gab, wo_ref[...]).astype(bf16)
        sums_ref[0:1, :] = jnp.sum(gab.astype(f32), 0, keepdims=True)
        sums_ref[1:2, :] = jnp.sum(grad * xhat, 0, keepdims=True)
        sums_ref[2:3, :] = jnp.sum(grad, 0, keepdims=True)


def feed_back(sc, gd, gr, wd, wu, slope, xhat, inv, go, wo, deps):
    length, d = gd.shape
    steps = slope.shape[0]
    at = lambda i: jnp.minimum(i, steps - 1)
    return call(
        feed_back_kernel,
        sc,
        (gd, gr, *far(wd, wu, slope, xhat, inv), go, *far(wo)),
        [
            whole(length, d), whole(length, d),
            pl.BlockSpec((d, d), lambda i, s: (at(i), 0)),
            pl.BlockSpec((d, d), lambda i, s: (0, at(i))),
            pl.BlockSpec((1, length, d), lambda i, s: (at(i), 0, 0)),
            whole(length, d), whole(length, 1), whole(1, d), whole(d, d),
        ],
        [
            shape(bf16, steps + 1, length, d), shape(f32, steps, 1, d), shape(f32, length, d),
            shape(bf16, length, d), shape(f32, SLOT, d),
        ],
        [
            pl.BlockSpec((1, length, d), lambda i, s: (i, 0, 0)),
            pl.BlockSpec((1, 1, d), lambda i, s: (at(i), 0, 0)),
            whole(length, d), whole(length, d), whole(SLOT, d),
        ],
        (steps + 1,),
        [pltpu.VMEM((length, d), f32)],
        "feed_back", 0, deps,
    )


def attention_back_kernel(
    piece, sc_ref, q_ref, k_ref, v_ref, gctx_ref, lse_ref, wq_ref, wk_ref, wv_ref, gr_ref,
    gq_ref, gk_ref, gv_ref, gtok_ref, sums_ref,
    acc, bias, gkt, gvt,
):
    step = pl.program_id(0)
    length = q_ref.shape[0]

    @pl.when(step == 0)
    def _():
        bias[...] = segment_bias(sc_ref, length, piece)
        acc[...] = gr_ref[...]

    lse = lse_ref[0].T
    for h in range(GROUP):
        cols = slice(h * HEAD, (h + 1) * HEAD)
        q = q_ref[:, cols]
        k = k_ref[:, cols]
        gctx = gctx_ref[:, cols]
        scores = nt(q * jnp.asarray(SCALE, bf16), k) + bias[...]
        p = jnp.exp(scores - lse[:, h : h + 1])
        ga = nt(gctx, v_ref[:, cols])
        dots = jnp.sum(p * ga, -1, keepdims=True)
        g = (p * (ga - dots)).astype(bf16)
        gq_ref[:, cols] = (nn(g, k) * SCALE).astype(bf16)
        gkt[cols, :] = (tn(q, g) * SCALE).astype(bf16)
        gvt[cols, :] = tn(gctx, p.astype(bf16)).astype(bf16)
    gk_ref[...] = gkt[...].T
    gv_ref[...] = gvt[...].T
    gq, gk, gv = gq_ref[...], gk_ref[...], gv_ref[...]
    sums_ref[0:1, :] = jnp.sum(gq.astype(f32), 0, keepdims=True)
    sums_ref[1:2, :] = jnp.sum(gv.astype(f32), 0, keepdims=True)
    acc[...] += nt(gq, wq_ref[...]) + nt(gk, wk_ref[...]) + nt(gv, wv_ref[...])

    @pl.when(step == pl.num_programs(0) - 1)
    def _():
        gtok_ref[...] = acc[...].astype(bf16)


def attention_back(sc, q, k, v, gctx, lse, wq, wk, wv, gr, piece, deps):
    length, d = q.shape
    wide = GROUP * HEAD
    steps = d // wide
    cols = lambda r: pl.BlockSpec((r, wide), lambda i, s: (0, i))
    return call(
        functools.partial(attention_back_kernel, piece),
        sc,
        (*far(q, k, v), gctx, *far(lse, wq, wk, wv), gr),
        [
            cols(length), cols(length), cols(length), cols(length),
            pl.BlockSpec((1, SLOT, length), lambda i, s: (i, 0, 0)),
            cols(d), cols(d), cols(d), whole(length, d),
        ],
        [shape(bf16, length, d)] * 4 + [shape(f32, SLOT, d)],
        [cols(length), cols(length), cols(length), whole(length, d), cols(SLOT)],
        (steps,),
        [
            pltpu.VMEM((length, d), f32), pltpu.VMEM((length, length), f32),
            pltpu.VMEM((wide, length), bf16), pltpu.VMEM((wide, length), bf16),
        ],
        "attention_back", 0, deps,
    )


def weight_total(two, lo_refs, lp_ref, go_ref, gp_ref):
    lo = lo_refs[0][...].reshape(lo_refs[0].shape[-2:])
    if len(lo_refs) > 1:
        lo = jnp.where(pl.program_id(0) < two, lo, lo_refs[1][...].reshape(lo.shape))
    return nn(lo, go_ref[0]) + nn(lp_ref[0, 0], gp_ref[0])


def weight_send_kernel(lefts, two, sc_ref, *refs):
    lo_refs, (lp_ref, go_ref, gp_ref, out_ref) = refs[:lefts], refs[lefts:]
    out_ref[0] = weight_total(two, lo_refs, lp_ref, go_ref, gp_ref).astype(bf16)


def down_total(lo_ref, lp_ref, go_ref, gp_ref):
    return nn(lo_ref[0, 0], go_ref[...]) + nn(lp_ref[0], gp_ref[...])


def down_send_kernel(sc_ref, lo_ref, lp_ref, go_ref, gp_ref, out_ref):
    out_ref[0] = down_total(lo_ref, lp_ref, go_ref, gp_ref).astype(bf16)


def down_mid_kernel(sc_ref, lo_ref, lp_ref, go_ref, gp_ref, got_ref, near_ref, far_ref):
    total = down_total(lo_ref, lp_ref, go_ref, gp_ref) + got_ref[pl.program_id(0)].astype(f32)
    half = total.shape[0] // 2
    for z in range(2):
        part = total[z * half : (z + 1) * half].astype(bf16)

        @pl.when(sc_ref[3] == z)
        def _():
            near_ref[0] = part

        @pl.when(sc_ref[3] != z)
        def _():
            far_ref[0] = part


def down_stage(kernel, sc, operands, got, outs, out_specs, steps, x, h, name, deps, micros=0):
    lo, lp, go, gp = operands
    rows = lo.shape[2]
    return call(
        kernel, sc, far(lo, lp) + (go, gp) + got,
        [
            pl.BlockSpec((1, 1) + lo.shape[2:], lambda i, s: (2 * x(i, s) + s[1], h(s), 0, 0)),
            pl.BlockSpec((1, rows, lp.shape[2]), lambda i, s: (x(i, s), h(s), 0)),
            whole(*go.shape), whole(*gp.shape),
        ]
        + [whole(*g.shape) for g in got],
        outs, out_specs, (steps,), [], name, micros, deps,
    )


def deal(sc_ref, total, step, keep_ref, send_ref):
    rows = total.shape[0] // 4
    spot = pl.ds(step * rows if isinstance(step, int) else pl.multiple_of(step * rows, rows), rows)
    for h in range(2):
        for z in range(2):
            part = total[(2 * h + z) * rows : (2 * h + z + 1) * rows].astype(bf16)

            @pl.when(sc_ref[2] == h)
            def _():
                keep_ref[sc_ref[3] ^ z, spot, :] = part

            @pl.when(sc_ref[2] != h)
            def _():
                send_ref[sc_ref[3] ^ z, spot, :] = part


def weight_keep_kernel(lefts, two, sc_ref, *refs):
    lo_refs, (lp_ref, go_ref, gp_ref, recv_ref, keep_ref, send_ref) = refs[:lefts], refs[lefts:]
    total = weight_total(two, lo_refs, lp_ref, go_ref, gp_ref) + recv_ref[0].astype(f32)
    deal(sc_ref, total, pl.program_id(0), keep_ref, send_ref)


def pack_kernel(sc_ref, qkv_ref, one_ref, two_ref, bup_ref, own_ref, far_ref):
    rows = jnp.concatenate([qkv_ref[0:2], one_ref[0:3], two_ref[0:3]], 0)
    quarter = rows.shape[1] // 4
    own_ref[...] = jnp.zeros_like(own_ref)
    far_ref[...] = jnp.zeros_like(far_ref)
    for x in range(2):
        for c in range(2):
            q = 2 * x + c
            left = rows[:, q * quarter : (q + 1) * quarter]

            def put(ref):
                ref[x, 0:8, :quarter] = left
                for j in range(4):
                    ref[x, 8 + j : 9 + j, :quarter] = bup_ref[q, :, j * quarter : (j + 1) * quarter]

            @pl.when(sc_ref[1] == c)
            def _():
                put(own_ref)

            @pl.when(sc_ref[1] != c)
            def _():
                put(far_ref)


def pack(sc, qkv, one, two, bup):
    out = shape(f32, 2, EXTRA, 2 * SMALL)
    return call(
        pack_kernel, sc, (qkv, one, two, bup), [whole(*t.shape) for t in (qkv, one, two, bup)],
        [out, out], [whole(*out.shape)] * 2, (1,), [], "pack", 0,
    )


def qkv_totals(lo_ref, lp_ref, own, par):
    return [nn(lo_ref[0], o[...]) + nn(lp_ref[0, 0], p[...]) for o, p in zip(own, par)]


def qkv_send_kernel(sc_ref, lo_ref, lp_ref, own_ref, par_ref, *refs):
    out_ref = refs[6]
    rows = lo_ref.shape[1]
    for n, total in enumerate(qkv_totals(lo_ref, lp_ref, refs[:3], refs[3:6])):
        out_ref[n * rows : (n + 1) * rows, :] = total.astype(bf16)
    vec = own_ref[1 - sc_ref[0]] + par_ref[1 - sc_ref[0]]
    out_ref[3 * rows :, :] = jnp.zeros((EXTRA, out_ref.shape[1]), bf16)
    out_ref[3 * rows :, : vec.shape[1]] = vec.astype(bf16)


def qkv_keep_kernel(sc_ref, lo_ref, lp_ref, own_ref, par_ref, *refs):
    recv_ref, keep_ref, send_ref = refs[6:]
    rows = lo_ref.shape[1]
    for n, total in enumerate(qkv_totals(lo_ref, lp_ref, refs[:3], refs[3:6])):
        total += recv_ref[n * rows : (n + 1) * rows, :].astype(f32)
        deal(sc_ref, total, n, keep_ref, send_ref)
    base = keep_ref.shape[1] - EXTRA
    vec = own_ref[sc_ref[0]] + par_ref[sc_ref[0]]
    wide = vec.shape[1]
    vec += recv_ref[3 * rows :, :wide].astype(f32)
    blank = jnp.zeros((EXTRA, keep_ref.shape[2]), bf16)
    for ref in (keep_ref, send_ref):
        for z in range(2):
            ref[z, base:, :] = blank
            ref[z, base:, :wide] = vec.astype(bf16)


def qkv_specs(xt, halves, own, other):
    x = (lambda s: 1 - s[0]) if other else (lambda s: s[0])
    return [
        pl.BlockSpec((1,) + xt.shape[1:], lambda i, s: (2 * x(s) + s[1], 0, 0)),
        pl.BlockSpec((1, 1) + halves.shape[2:], lambda i, s: (x(s), 6, 0, 0)),
    ] + [whole(2, EXTRA, 2 * SMALL)] * 2 + [whole(*own.shape)] * 6


def qkv_send(sc, operands, deps):
    xt, halves, _, _, own = operands[:5]
    rows, wide = xt.shape[1], own.shape[1]
    out = shape(bf16, 3 * rows + EXTRA, wide)
    return call(
        qkv_send_kernel, sc, far(xt, halves) + operands[2:], qkv_specs(xt, halves, own, True), out, whole(*out.shape),
        (1,), [], "qkv_send", 0, deps,
    )


def qkv_keep(sc, operands, recv, deps):
    xt, halves, _, _, own = operands[:5]
    rows, wide = xt.shape[1], own.shape[1]
    out = shape(bf16, 2, 3 * rows // 4 + EXTRA, wide)
    return call(
        qkv_keep_kernel, sc, far(xt, halves) + operands[2:] + (recv,),
        qkv_specs(xt, halves, own, False) + [whole(*recv.shape)],
        [out, out], [whole(*out.shape)] * 2, (1,), [], "qkv_keep", 0, deps,
    )


def order_kernel(sc_ref, *refs):
    out_ref = refs[-1]
    for mask, piece in enumerate(refs[:-1]):
        out_ref[sc_ref[0] ^ mask] = piece[...]


def weight_specs(lefts, halves, grads, grads_p, other, steps, turn):
    x = (lambda s: 1 - s[0]) if other else (lambda s: s[0])
    specs = []
    for left in lefts:
        if left.ndim == 4:
            specs.append(
                pl.BlockSpec((1, 1) + left.shape[2:], lambda i, s: (2 * x(s) + s[1], i, 0, 0))
            )
        else:
            specs.append(pl.BlockSpec((1,) + left.shape[1:], lambda i, s: (2 * x(s) + s[1], 0, 0)))
    specs.append(pl.BlockSpec((1, 1) + halves.shape[2:], lambda i, s: (x(s), turn(i), 0, 0)))
    one = grads.shape[0] == 1
    block = pl.BlockSpec((1,) + grads.shape[1:], lambda i, s: (0 if one else i, 0, 0))
    return (*far(*lefts), *far(halves), grads, grads_p), specs + [block, block]


def weight_send(sc, operands, steps, two, turn, name, deps=(), micros=0):
    args, specs = weight_specs(*operands, True, steps, turn)
    rows, wide = operands[1].shape[2], operands[2].shape[2]
    return call(
        functools.partial(weight_send_kernel, len(operands[0]), two),
        sc, args, specs, shape(bf16, steps, rows, wide),
        pl.BlockSpec((1, rows, wide), lambda i, s: (i, 0, 0)), (steps,), [],
        name, micros, deps,
    )


def weight_keep(sc, operands, recv, steps, two, turn, name, deps=(), micros=0):
    args, specs = weight_specs(*operands, False, steps, turn)
    rows, wide = operands[1].shape[2], operands[2].shape[2]
    out = shape(bf16, 2, steps * rows // 4, wide)
    return call(
        functools.partial(weight_keep_kernel, len(operands[0]), two),
        sc, args + (recv,), specs + [pl.BlockSpec((1, rows, wide), lambda i, s: (i, 0, 0))],
        [out, out], [whole(*out.shape)] * 2, (steps,), [],
        name, micros, deps,
    )


def place_kernel(spots, extra, sc_ref, *refs):
    parts, out_refs = refs[:4], refs[4:]
    rows = (parts[0].shape[0] - extra) // len(spots)
    wide = parts[0].shape[1]
    for side, part in enumerate(parts):
        slot = 2 * (sc_ref[2] ^ (side // 2)) + (sc_ref[3] ^ (side % 2))
        for n, (out, down, left) in enumerate(spots):
            top = pl.multiple_of((4 * down + slot) * rows, rows)
            out_refs[out][pl.ds(top, rows), left * wide : (left + 1) * wide] = part[
                n * rows : (n + 1) * rows, :
            ].astype(f32)
    if extra:
        small = out_refs[-1]
        small[...] = parts[0][len(spots) * rows :, : small.shape[1]].astype(f32)


def place(sc, parts, spots, dims, extra, name, deps=()):
    return call(
        functools.partial(place_kernel, spots, extra),
        sc, parts, [whole(*parts[0].shape)] * 4,
        [shape(f32, *dim) for dim in dims], [whole(*dim) for dim in dims], (1,), [],
        name, 0, deps,
    )


def flip(value, axis, mask):
    count = lax.axis_size(axis)
    return lax.ppermute(value, axis, [(i, i ^ mask) for i in range(count)])


def flip_both(value, row_mask, seq_mask):
    rows, seq = lax.axis_size("rows"), lax.axis_size("seq")
    pairs = [
        (r * seq + s, (r ^ row_mask) * seq + (s ^ seq_mask)) for r in range(rows) for s in range(seq)
    ]
    return lax.ppermute(value, ("rows", "seq"), pairs)


def row_flips():
    count = lax.axis_size("rows")
    assert count >= 8 and count & (count - 1) == 0
    return [2, 6] + [1 << b for b in range(3, count.bit_length() - 1)]


def join_kernel(sc_ref, left_ref, right_ref, out_ref):
    out_ref[...] = add(left_ref[...], right_ref[...])


def join(sc, left, right, deps, name, micros=0):
    block = whole(*left.shape)
    return call(
        join_kernel, sc, (left, right), [block, block], shape(bf16, *left.shape), block, (1,), [],
        name, micros, deps,
    )


def join_two_kernel(slot, sc_ref, left_ref, right_ref, near_ref, far_ref):
    own = 0 if slot is None else sc_ref[slot]
    near_ref[...] = add(left_ref[own], right_ref[own])
    far_ref[...] = add(left_ref[1 - own], right_ref[1 - own])


def join_two(sc, left, right, deps, name, slot=None):
    block, half = whole(*left.shape), whole(*left.shape[1:])
    out = shape(bf16, *left.shape[1:])
    return call(
        functools.partial(join_two_kernel, slot), sc, (left, right), [block, block], [out, out],
        [half, half], (1,), [], name, 0, deps,
    )


def across(sc, value, masks, deps, name):
    first, *rest = masks
    value = join(sc, value, flip(value, "rows", first), deps, name)
    for mask in rest:
        value = add(value, flip(value, "rows", mask))
    return value


def gathered(value, near):
    return (value,) + tuple(flip(value, "rows", mask) for mask in (near, 1, near ^ 1))


def add(left, right):
    return (left.astype(f32) + right.astype(f32)).astype(bf16)


def spread(rows):
    own = lax.axis_index("seq")
    count = lax.axis_size("seq")
    assert rows.shape[0] == count
    pieces = [
        flip(lax.dynamic_index_in_dim(rows, own ^ mask, 0, keepdims=False), "seq", mask)
        if mask
        else lax.dynamic_index_in_dim(rows, own, 0, keepdims=False)
        for mask in range(count)
    ]
    return jnp.concatenate(pieces, 0)


def gather_back(sc, row, count, name, deps=()):
    row = row.reshape(count, -1, row.shape[-1])
    pieces = tuple(flip(row[mask], "seq", mask) if mask else row[0] for mask in range(count))
    return call(
        order_kernel, sc, pieces, [whole(*row.shape[1:])] * count, shape(row.dtype, *row.shape),
        whole(*row.shape), (1,), [], name, 0, deps,
    )


def per_device(
    tokens,
    w_query,
    b_query,
    w_key,
    w_value,
    b_value,
    w_out,
    b_out,
    gain_one,
    shift_one,
    w_up,
    b_up,
    w_down,
    b_down,
    gain_two,
    shift_two,
    passage_starts,
    queries,
    choices,
    cotangent,
):
    seq_count = lax.axis_size("seq")
    row_count = lax.axis_size("rows")
    own_s = lax.axis_index("seq")
    own_r = lax.axis_index("rows")
    row_block, piece, d = tokens.shape
    assert row_block == seq_count == 4
    ff = w_up.shape[1]
    quarter = d // 4
    core, xside = own_s % 2, own_s // 2
    own_lin = own_r * seq_count + own_s
    devices = row_count * seq_count
    masks = row_flips()
    wsc = jnp.stack([xside, core, own_r % 2, (own_r // 2 ^ own_r // 4) % 2]).astype(jnp.int32)
    starts = lax.dynamic_index_in_dim(passage_starts, own_s, 0, keepdims=False)
    sc = jnp.concatenate([own_s[None].astype(jnp.int32), starts, own_lin[None].astype(jnp.int32)])
    row = lambda v: v.reshape(1, -1)
    swap = lambda t: flip(t, "seq", 1)

    x = spread(tokens)

    code = jnp.concatenate(
        [queries, (choices // PASS).astype(bf16), (choices % PASS).astype(bf16)], axis=1
    )
    code_all = lax.all_gather(code, ("rows", "seq"), axis=0, tiled=True)

    cot = spread(cotangent)

    q, k, v, ctxt, lse, xt, xhat_one, inv_one, hid, hidt = attention_forward(
        sc, x, w_query, w_key, w_value, row(b_query), row(b_value), w_out, row(b_out),
        row(gain_one), row(shift_one), piece,
    )
    actt, slope, xhat_two, inv_two, mixed_row, pool = feed_forward(
        sc, hid, w_up, row(b_up), w_down, row(b_down), row(gain_two), row(shift_two), piece, (cot,)
    )

    pool = pool.astype(bf16)
    if row_count == 8:
        near = jnp.concatenate(
            [pool, flip(pool, "seq", 2), flip(pool, "rows", 1), flip_both(pool, 1, 2)], 0
        )
        mid = jnp.concatenate(
            [near, flip(near, "rows", 2), flip(near, "rows", 6), flip(near, "rows", 4)], 0
        )
        pooled = jnp.concatenate([mid, flip(mid, "seq", 1)], 0)
        places = cube_place
    else:
        pooled = lax.all_gather(pool, ("rows", "seq"), axis=0, tiled=True)
        pooled = jnp.roll(pooled, -own_lin * SLOT, 0)
        places = turned_place

    other_half = lambda t: lax.dynamic_index_in_dim(
        t.reshape(2, 2, -1, quarter, t.shape[-1]), 1 - core, 1, keepdims=False
    )
    halves = swap(
        jnp.concatenate([other_half(actt), other_half(hidt), other_half(ctxt), other_half(xt)], 1)
    )
    quarters = lambda t: t.reshape(4, -1, t.shape[-1])

    losses_all, gd, gr_two, sums_two = retrieval(
        sc, code_all, pooled, cot, xhat_two, inv_two, row(gain_two), piece, places, devices,
        (halves,),
    )
    query_losses = lax.dynamic_slice_in_dim(
        losses_all[:, 0], own_lin * queries.shape[0], queries.shape[0]
    )

    gd_p = swap(gd)
    gug, bup, gr_one, gctx, sums_one = feed_back(
        sc, gd, gr_two, w_down, w_up, slope, xhat_one, inv_one, row(gain_one), w_out, (gd_p,)
    )

    near, *rest = masks
    part = ff // 8
    down_ops = (actt.reshape(4, 2, part, -1), halves.reshape(2, -1, piece * seq_count), gd, gd_p)
    down_sent = down_stage(
        down_send_kernel, wsc, down_ops, (), shape(bf16, 2, part, d),
        pl.BlockSpec((1, part, d), lambda i, s: (i, 0, 0)), 2,
        lambda i, s: i, lambda s: 1 - s[2], "down_send", (gug,),
    )
    down_got = flip(down_sent, "rows", 1)

    up_ops = ((quarters(hidt), quarters(ctxt)), halves, gug, swap(gug))
    up_turn = lambda i: 4 + i // 4
    up_sent = weight_send(wsc, up_ops, 5, 4, up_turn, "up_send", (down_sent,))
    up_got = flip(up_sent, "seq", 2)

    gq, gk, gv, gtok, sums_qkv = attention_back(
        sc, q, k, v, gctx, lse, w_query, w_key, w_value, gr_one, piece, (up_sent,)
    )
    vec, vec_far = pack(wsc, sums_qkv, sums_one, sums_two, bup)
    qkv_ops = (
        quarters(xt), halves, vec, swap(vec_far), gq, gk, gv, swap(gq), swap(gk), swap(gv)
    )
    qkv_sent = qkv_send(wsc, qkv_ops, ())
    qkv_got = flip(qkv_sent, "seq", 2)
    pair = shape(bf16, 2, part // 2, d)
    each = pl.BlockSpec((1, part // 2, d), lambda i, s: (i, 0, 0))
    down_near, down_far = down_stage(
        down_mid_kernel, wsc, down_ops, (down_got,), [pair, pair], [each, each], 2,
        lambda i, s: i, lambda s: s[2], "down_mid", (qkv_sent,), 3,
    )
    up_parts = weight_keep(
        wsc, up_ops, up_got, 5, 4, up_turn, "up_keep", (vec, down_near), PIN
    )
    down_sum = join(wsc, down_near, flip(down_far, "rows", near), (up_parts[0],), "down_join_a", 3)
    for mask in rest[1:]:
        down_sum = add(down_sum, flip(down_sum, "rows", mask))
    qkv_parts = qkv_keep(wsc, qkv_ops, qkv_got, (down_sum,))
    up_near, up_far = join_two(
        wsc, up_parts[0], flip(up_parts[1], "rows", 1), (qkv_parts[0],), "up_join_y"
    )
    qkv_near, qkv_far = join_two(
        wsc, qkv_parts[0], flip(qkv_parts[1], "rows", 1), (up_near,), "qkv_join_y"
    )
    up_sum = join(wsc, up_near, flip(up_far, "rows", near), (qkv_near,), "up_join_a")
    down_own, down_other = join_two(
        wsc, down_sum, flip(down_sum, "rows", rest[0]), (up_sum,), "down_join_b", 0
    )
    qkv_sum = join(wsc, qkv_near, flip(qkv_far, "rows", near), (down_own,), "qkv_join_a")
    down_sum = join(wsc, down_own, flip(down_other, "seq", 2), (qkv_sum,), "down_join_x")
    down_all = gathered(down_sum, near)
    up_sum = across(wsc, up_sum, rest, (down_sum,), "up_join_b")
    up_all = gathered(up_sum, near)
    (grad_down,) = place(wsc, down_all, [(0, 0, 0)], [(4 * quarter, d)], 0, "down_place", (up_sum,))
    qkv_sum = across(wsc, qkv_sum, rest, (grad_down,), "qkv_join_b")
    qkv_all = gathered(qkv_sum, near)
    mixed = gather_back(sc, mixed_row, seq_count, "mixed_order", (down_sum,))
    grad_tokens = gather_back(sc, gtok, seq_count, "tokens_order", (qkv_sum,))
    grad_up, grad_o = place(
        wsc, up_all, [(0, 0, n) for n in range(4)] + [(1, 0, 0)],
        [(quarter, ff), (quarter, d)], 0, "up_place", (qkv_sum,),
    )
    grad_q, grad_k, grad_v, small = place(
        wsc, qkv_all, [(n, 0, 0) for n in range(3)], [(quarter, d)] * 3 + [(EXTRA, 2 * SMALL)],
        EXTRA, "qkv_place",
    )

    eight = small[:, :quarter]
    return (
        mixed,
        query_losses,
        grad_tokens,
        grad_q,
        eight[0],
        grad_k,
        grad_v,
        eight[1],
        grad_o,
        eight[2],
        eight[3],
        eight[4],
        grad_up,
        eight[8:12].reshape(-1),
        grad_down,
        eight[5],
        eight[6],
        eight[7],
    )


def solution(mesh):
    weights = (P(),) * 15
    placed = (
        (P("rows", "seq", None),)
        + weights
        + (
            P("rows", None),
            P(("rows", "seq"), None),
            P(("rows", "seq"), None),
            P("rows", "seq", None),
        )
    )
    return jax.shard_map(
        per_device,
        mesh=mesh,
        in_specs=placed,
        out_specs=(
            P("rows", "seq", None),
            P(("rows", "seq")),
            P("rows", "seq", None),
            P("seq", None),
            P("seq"),
            P("seq", None),
            P("seq", None),
            P("seq"),
            P("seq", None),
            P("seq"),
            P("seq"),
            P("seq"),
            P("seq", None),
            P("seq"),
            P("seq", None),
            P("seq"),
            P("seq"),
            P("seq"),
        ),
        check_vma=False,
    )
```

```python
import functools

import jax
import jax.numpy as jnp
from jax import lax
from jax.experimental import pallas as pl
from jax.experimental.pallas import tpu as pltpu
from jax.sharding import PartitionSpec as P

HEADS = 12
HEAD = 64
PASS = 6
CH = 32
SLOT = 8
GROUP = 4
SUB = 384
SCALE = HEAD ** (-0.5)

norm_eps = 1e-05
f32 = jnp.float32
bf16 = jnp.bfloat16
VMEM_BYTES = 28 * 1024 * 1024
PIN = 100
EXTRA = 16
SMALL = 128


def params():
    return pltpu.CompilerParams(vmem_limit_bytes=VMEM_BYTES)


def cost(micros):
    return pl.CostEstimate(flops=int(micros * 1.15e9), bytes_accessed=0, transcendentals=0)


def nt(a, b):
    return lax.dot_general(a, b, (((1,), (1,)), ((), ())), preferred_element_type=f32)


def tn(a, b):
    return lax.dot_general(a, b, (((0,), (0,)), ((), ())), preferred_element_type=f32)


def nn(a, b):
    return jnp.dot(a, b, preferred_element_type=f32)


def stats(values):
    center = values - jnp.mean(values, -1, keepdims=True)
    inv = lax.rsqrt(jnp.mean(center * center, -1, keepdims=True) + norm_eps)
    return center * inv, inv


def norm_back(grad, xhat, inv, gain):
    gx = grad * gain
    return inv * (
        gx - jnp.mean(gx, -1, keepdims=True) - xhat * jnp.mean(gx * xhat, -1, keepdims=True)
    )


def true_places(own_seq, count, piece, axis):
    shape = (count, 1) if axis == 0 else (1, count)
    local = lax.broadcasted_iota(jnp.int32, shape, axis)
    block = local // piece
    return (block ^ own_seq) * piece + (local - block * piece)


def segments(sc_ref, places):
    total = jnp.zeros(places.shape, jnp.int32)
    for j in range(PASS):
        total += (sc_ref[1 + j] <= places).astype(jnp.int32)
    return total


def segment_bias(sc_ref, length, piece):
    col = segments(sc_ref, true_places(sc_ref[0], length, piece, 0))
    row = segments(sc_ref, true_places(sc_ref[0], length, piece, 1))
    return jnp.where(col == row, 0.0, -1e30)


def call(kernel, sc, args, specs, outs, out_specs, grid, scratch, name, micros, deps=()):
    count = len(args)

    def body(sc_ref, *refs):
        kernel(sc_ref, *refs[:count], *refs[count + len(deps) :])

    hold = pl.BlockSpec(memory_space=pl.ANY)
    return pl.pallas_call(
        body,
        grid_spec=pltpu.PrefetchScalarGridSpec(
            num_scalar_prefetch=1,
            grid=grid,
            in_specs=list(specs) + [hold] * len(deps),
            out_specs=out_specs,
            scratch_shapes=scratch,
        ),
        out_shape=outs,
        compiler_params=params(),
        cost_estimate=cost(micros),
        name=name,
    )(sc, *args, *deps)


def shape(t, *dims):
    return jax.ShapeDtypeStruct(dims, t)


def kept(t, *dims):
    return pltpu.HBM(dims, t)


def far(*values):
    return tuple(pltpu.with_memory_space_constraint(v, pltpu.HBM) for v in values)


def whole(*dims):
    return pl.BlockSpec(dims, lambda i, s: (0,) * len(dims))


def attention_kernel(
    piece, sc_ref, x_ref, wq_ref, wk_ref, wv_ref, bq_ref, bv_ref, wo_ref, bo_ref, go_ref, so_ref,
    q_ref, k_ref, v_ref, ctxt_ref, lse_ref, xt_ref, xhat_ref, inv_ref, hid_ref, hidt_ref,
    acc, bias,
):
    step = pl.program_id(0)
    length = x_ref.shape[0]
    x = x_ref[...]
    q_ref[...] = (nn(x, wq_ref[...]) + bq_ref[...]).astype(bf16)
    k_ref[...] = nn(x, wk_ref[...]).astype(bf16)
    v_ref[...] = (nn(x, wv_ref[...]) + bv_ref[...]).astype(bf16)

    @pl.when(step == 0)
    def _():
        bias[...] = segment_bias(sc_ref, length, piece)
        acc[...] = x.astype(f32) + bo_ref[...]

    for h in range(GROUP):
        cols = slice(h * HEAD, (h + 1) * HEAD)
        raw = nt(k_ref[:, cols], q_ref[:, cols] * jnp.asarray(SCALE, bf16))
        scores = raw + bias[...]
        top = jnp.max(scores, 0, keepdims=True)
        e = jnp.exp(scores - top)
        total = jnp.sum(e, 0, keepdims=True)
        p = (e * (1.0 / total)).astype(bf16)
        ctxt_ref[cols, :] = tn(v_ref[:, cols], p).astype(bf16)
        lse_ref[0, h : h + 1, :] = top + jnp.log(total)
    acc[...] += tn(ctxt_ref[...], wo_ref[...])

    for j in range(x_ref.shape[1] // xt_ref.shape[0]):
        wide = xt_ref.shape[0]

        @pl.when(step == j)
        def _():
            xt_ref[...] = x_ref[:, j * wide : (j + 1) * wide].T

    @pl.when(step == pl.num_programs(0) - 1)
    def _():
        xhat, inv = stats(acc[...])
        xhat_ref[...] = xhat
        inv_ref[...] = inv
        hid = (xhat * go_ref[...] + so_ref[...]).astype(bf16)
        hid_ref[...] = hid
        hidt_ref[...] = hid.T


def attention_forward(sc, x, wq, wk, wv, bq, bv, wo, bo, go, so, piece):
    length, d = x.shape
    wide = GROUP * HEAD
    steps = d // wide
    cols = lambda r: pl.BlockSpec((r, wide), lambda i, s: (0, i))
    rows = lambda c: pl.BlockSpec((wide, c), lambda i, s: (i, 0))
    return call(
        functools.partial(attention_kernel, piece),
        sc,
        (x, *far(wq, wk, wv), bq, bv, *far(wo), bo, go, so),
        [
            whole(length, d), cols(d), cols(d), cols(d), cols(1), cols(1), rows(d),
            whole(1, d), whole(1, d), whole(1, d),
        ],
        [
            kept(bf16, length, d), kept(bf16, length, d), kept(bf16, length, d),
            kept(bf16, d, length), kept(f32, steps, SLOT, length), kept(bf16, d, length),
            kept(f32, length, d), kept(f32, length, 1), shape(bf16, length, d),
            kept(bf16, d, length),
        ],
        [
            cols(length), cols(length), cols(length), rows(length),
            pl.BlockSpec((1, SLOT, length), lambda i, s: (i, 0, 0)), rows(length),
            whole(length, d), whole(length, 1), whole(length, d), whole(d, length),
        ],
        (steps,),
        [pltpu.VMEM((length, d), f32), pltpu.VMEM((length, length), f32)],
        "attention_forward", 0,
    )


def feed_kernel(
    piece, sc_ref, hid_ref, wu_ref, bu_ref, wd_ref, bd_ref, gt_ref, st_ref,
    actt_ref, slope_ref, xhat_ref, inv_ref, mixed_ref, pool_ref,
    acc,
):
    step = pl.program_id(0)
    length = hid_ref.shape[0]

    @pl.when(step == 0)
    def _():
        acc[...] = hid_ref[...].astype(f32) + bd_ref[...]

    for c in range(0, wu_ref.shape[1], SUB):
        cols = slice(c, c + SUB)
        up = nn(hid_ref[...], wu_ref[:, cols]) + bu_ref[:, cols]
        e = jnp.exp(-0.5 * up * up)
        cum = 0.5 + 0.5 * lax.erf(up * (2.0 ** -0.5))
        slope_ref[0, :, cols] = (cum + up * (e * 0.3989422804014327)).astype(bf16)
        act = (up * cum).astype(bf16)
        actt_ref[cols, :] = act.T
        acc[...] += nn(act, wd_ref[cols, :])

    @pl.when(step == pl.num_programs(0) - 1)
    def _():
        xhat, inv = stats(acc[...])
        xhat_ref[...] = xhat
        inv_ref[...] = inv
        mixed = (xhat * gt_ref[...] + st_ref[...]).astype(bf16)
        mixed_ref[...] = mixed
        places = true_places(sc_ref[0], length, piece, 1)
        slot = lax.broadcasted_iota(jnp.int32, (SLOT, 1), 0)
        start = jnp.full((SLOT, 1), -1, jnp.int32)
        for j in range(PASS):
            start = jnp.where(slot == j, sc_ref[1 + j], start)
        pool_ref[...] = nn((places == start).astype(f32).astype(bf16), mixed)


def feed_forward(sc, hid, wu, bu, wd, bd, gt, st, piece, deps):
    length, d = hid.shape
    ff = wu.shape[1]
    steps = ff // d
    return call(
        functools.partial(feed_kernel, piece),
        sc,
        (hid, *far(wu), bu, *far(wd), bd, gt, st),
        [
            whole(length, d),
            pl.BlockSpec((d, d), lambda i, s: (0, i)),
            pl.BlockSpec((1, d), lambda i, s: (0, i)),
            pl.BlockSpec((d, d), lambda i, s: (i, 0)),
            whole(1, d), whole(1, d), whole(1, d),
        ],
        [
            kept(bf16, ff, length), kept(bf16, steps, length, d), kept(f32, length, d),
            kept(f32, length, 1), kept(bf16, length, d), shape(f32, SLOT, d),
        ],
        [
            pl.BlockSpec((d, length), lambda i, s: (i, 0)),
            pl.BlockSpec((1, length, d), lambda i, s: (i, 0, 0)),
            whole(length, d), whole(length, 1), whole(length, d), whole(SLOT, d),
        ],
        (steps,),
        [pltpu.VMEM((length, d), f32)],
        "feed_forward", 0, deps,
    )


def begin_kernel(sc_ref, tokens_ref, queries_ref, choices_ref, code_ref, *piece_refs):
    for mask, piece_ref in enumerate(piece_refs):
        piece_ref[...] = tokens_ref[sc_ref[0] ^ mask]
    d = queries_ref.shape[1]
    choices = choices_ref[...]
    owner = choices // PASS
    code_ref[:, :d] = queries_ref[...]
    code_ref[:, d : d + CH] = owner.astype(f32).astype(bf16)
    code_ref[:, d + CH :] = (choices - owner * PASS).astype(f32).astype(bf16)


def begin(sc, tokens, queries, choices):
    count, d = queries.shape
    outs = [shape(bf16, count, d + 2 * CH)] + [shape(bf16, *tokens.shape[1:])] * tokens.shape[0]
    code, *pieces = call(
        begin_kernel, sc, far(tokens, queries, choices), [whole(*tokens.shape), whole(count, d), whole(count, CH)],
        outs, [whole(*o.shape) for o in outs], (1,), [], "begin", 0,
    )
    return pieces, code


def pick_kernel(sc_ref, rows_ref, *piece_refs):
    for mask, piece_ref in enumerate(piece_refs):
        piece_ref[...] = rows_ref[sc_ref[0] ^ mask]


def pick(sc, rows, deps):
    outs = [shape(bf16, *rows.shape[1:])] * rows.shape[0]
    return call(
        pick_kernel, sc, far(rows), [whole(*rows.shape)], outs, [whole(*o.shape) for o in outs],
        (1,), [], "pick", 0, deps,
    )


def halves_kernel(sc_ref, act_ref, hid_ref, ctx_ref, x_ref, out_ref):
    rows = hid_ref.shape[1]
    for n in range(act_ref.shape[1] // rows):
        out_ref[0, n] = act_ref[0, n * rows : (n + 1) * rows, :]
    for n, ref in enumerate((hid_ref, ctx_ref, x_ref)):
        out_ref[0, act_ref.shape[1] // rows + n] = ref[0]


def core_halves(sc, act, rest, deps):
    block = lambda t: pl.BlockSpec((1,) + t.shape[1:], lambda i, s: (2 * i + 1 - s[1], 0, 0))
    rows, length = rest[0].shape[1:]
    blocks = act.shape[1] // rows + len(rest)
    return call(
        halves_kernel, sc, far(act, *rest), [block(t) for t in (act, *rest)],
        shape(bf16, 2, blocks, rows, length),
        pl.BlockSpec((1, blocks, rows, length), lambda i, s: (i, 0, 0, 0)), (2,), [],
        "core_halves", 0, deps,
    )


def loss_kernel(
    piece, steps, devices, code_ref, sc_ref, q_ref, pool_ref, cot_ref, xhat_ref, inv_ref, gt_ref,
    loss_ref, gd_ref, gr_ref, sums_ref, gp,
):
    step = pl.program_id(0)
    d = pool_ref.shape[1]

    @pl.when(step == 0)
    def _():
        gp[...] = jnp.zeros_like(gp)
        sums_ref[...] = jnp.zeros_like(sums_ref)

    @pl.when(step < steps)
    def _():
        queries = q_ref[:, :d]
        logits = nt(queries, pool_ref[...])
        lanes = lax.broadcasted_iota(jnp.int32, (1, logits.shape[1]), 1)
        owner = q_ref[:, d : d + CH].astype(f32).astype(jnp.int32)
        inner = q_ref[:, d + CH :].astype(f32).astype(jnp.int32)
        pos = code_ref(owner, sc_ref[7], devices) * SLOT + inner
        first = (pos[:, 0:1] == lanes).astype(f32)
        times = first
        for c in range(1, CH):
            times += (pos[:, c : c + 1] == lanes).astype(f32)
        held = times > 0.0
        top = jnp.max(jnp.where(held, logits, -jnp.inf), -1, keepdims=True)
        e = jnp.where(held, times * jnp.exp(jnp.minimum(logits - top, 0.0)), 0.0)
        total = jnp.sum(e, -1, keepdims=True)
        positive = jnp.sum(first * logits, -1, keepdims=True)
        loss_ref[...] = top + jnp.log(total) - positive
        grad = e[:, :128] * (1.0 / total) - first[:, :128]
        high = grad.astype(bf16)
        lower = (grad - high.astype(f32)).astype(bf16)
        gp[...] += (tn(high, queries) + tn(lower, queries))[:SLOT]

    @pl.when(step >= steps)
    def _():
        block = (step - steps) ^ sc_ref[0]
        places = block * piece + lax.broadcasted_iota(jnp.int32, (piece, 1), 0)
        grad = cot_ref[...].astype(f32)
        for j in range(PASS):
            grad += jnp.where(places == sc_ref[1 + j], gp[j : j + 1, :], 0.0)
        xhat = xhat_ref[...]
        back = norm_back(grad, xhat, inv_ref[...], gt_ref[...])
        gr_ref[...] = back
        down = back.astype(bf16)
        gd_ref[...] = down
        sums_ref[0:1, :] += jnp.sum(down.astype(f32), 0, keepdims=True)
        sums_ref[1:2, :] += jnp.sum(grad * xhat, 0, keepdims=True)
        sums_ref[2:3, :] += jnp.sum(grad, 0, keepdims=True)


def cube_place(owner, own, devices):
    off = owner ^ own
    z = off >> 3
    return (off & 1) * 16 + (z ^ (z >> 1)) * 4 + ((off >> 1) & 3)


def turned_place(owner, own, devices):
    off = owner - own
    return jnp.where(off < 0, off + devices, off)


def retrieval(sc, code_all, pooled, cot, xhat, inv, gain, piece, places, devices, deps):
    count, width = code_all.shape
    length, d = cot.shape
    block = 256
    steps, pieces = count // block, length // piece
    first = lambda i: jnp.minimum(i, steps - 1)
    second = lambda i: jnp.maximum(i - steps, 0)
    part = lambda c: pl.BlockSpec((piece, c), lambda i, s: (second(i), 0))
    return call(
        functools.partial(loss_kernel, piece, steps, devices, places),
        sc,
        (*far(code_all), pooled, *far(cot, xhat, inv), gain),
        [
            pl.BlockSpec((block, width), lambda i, s: (first(i), 0)),
            whole(*pooled.shape), part(d), part(d), part(1), whole(1, d),
        ],
        [shape(f32, count, 1), shape(bf16, length, d), shape(f32, length, d), shape(f32, SLOT, d)],
        [
            pl.BlockSpec((block, 1), lambda i, s: (first(i), 0)), part(d), part(d), whole(SLOT, d),
        ],
        (steps + pieces,),
        [pltpu.VMEM((SLOT, d), f32)],
        "retrieval", 0, deps,
    )


def feed_back_kernel(
    sc_ref, gd_ref, gr_ref, wd_ref, wu_ref, slope_ref, xhat_far, inv_ref, go_ref, wo_far,
    gug_ref, bup_ref, gr1_ref, gctx_ref, sums_ref,
    acc, xhat_ref, wo_ref, arrived,
):
    step = pl.program_id(0)
    last = pl.num_programs(0) - 1
    late = [
        pltpu.make_async_copy(xhat_far, xhat_ref, arrived.at[0]),
        pltpu.make_async_copy(wo_far, wo_ref, arrived.at[1]),
    ]

    @pl.when(step == 1)
    def _():
        for copy in late:
            copy.start()

    @pl.when(step == 0)
    def _():
        acc[...] = gr_ref[...]

    @pl.when(step < last)
    def _():
        gact = nt(gd_ref[...], wd_ref[...])
        gup = (gact * slope_ref[0].astype(f32)).astype(bf16)
        gug_ref[0] = gup
        bup_ref[0] = jnp.sum(gup.astype(f32), 0, keepdims=True)
        acc[...] += nt(gup, wu_ref[...])

    @pl.when(step == last)
    def _():
        for copy in late:
            copy.wait()
        grad = acc[...]
        xhat = xhat_ref[...]
        back = norm_back(grad, xhat, inv_ref[...], go_ref[...])
        gr1_ref[...] = back
        gab = back.astype(bf16)
        gug_ref[0] = gab
        gctx_ref[...] = nt(gab, wo_ref[...]).astype(bf16)
        sums_ref[0:1, :] = jnp.sum(gab.astype(f32), 0, keepdims=True)
        sums_ref[1:2, :] = jnp.sum(grad * xhat, 0, keepdims=True)
        sums_ref[2:3, :] = jnp.sum(grad, 0, keepdims=True)


def feed_back(sc, gd, gr, wd, wu, slope, xhat, inv, go, wo, deps):
    length, d = gd.shape
    steps = slope.shape[0]
    at = lambda i: jnp.minimum(i, steps - 1)
    return call(
        feed_back_kernel,
        sc,
        (gd, gr, *far(wd, wu, slope, xhat, inv), go, *far(wo)),
        [
            whole(length, d), whole(length, d),
            pl.BlockSpec((d, d), lambda i, s: (at(i), 0)),
            pl.BlockSpec((d, d), lambda i, s: (0, at(i))),
            pl.BlockSpec((1, length, d), lambda i, s: (at(i), 0, 0)),
            pl.BlockSpec(memory_space=pl.ANY), whole(length, 1), whole(1, d),
            pl.BlockSpec(memory_space=pl.ANY),
        ],
        [
            shape(bf16, steps + 1, length, d), shape(f32, steps, 1, d), shape(f32, length, d),
            shape(bf16, length, d), shape(f32, SLOT, d),
        ],
        [
            pl.BlockSpec((1, length, d), lambda i, s: (i, 0, 0)),
            pl.BlockSpec((1, 1, d), lambda i, s: (at(i), 0, 0)),
            whole(length, d), whole(length, d), whole(SLOT, d),
        ],
        (steps + 1,),
        [
            pltpu.VMEM((length, d), f32), pltpu.VMEM((length, d), f32), pltpu.VMEM((d, d), bf16),
            pltpu.SemaphoreType.DMA((2,)),
        ],
        "feed_back", 0, deps,
    )


def attention_back_kernel(
    piece, sc_ref, q_ref, k_ref, v_ref, gctx_ref, lse_ref, wq_ref, wk_ref, wv_ref, gr_ref,
    gq_ref, gk_ref, gv_ref, gtok_ref, sums_ref,
    acc, bias, gkt, gvt,
):
    step = pl.program_id(0)
    length = q_ref.shape[0]

    @pl.when(step == 0)
    def _():
        bias[...] = segment_bias(sc_ref, length, piece)
        acc[...] = gr_ref[...]

    lse = lse_ref[0].T
    for h in range(GROUP):
        cols = slice(h * HEAD, (h + 1) * HEAD)
        q = q_ref[:, cols]
        k = k_ref[:, cols]
        gctx = gctx_ref[:, cols]
        scores = nt(q * jnp.asarray(SCALE, bf16), k) + bias[...]
        p = jnp.exp(scores - lse[:, h : h + 1])
        ga = nt(gctx, v_ref[:, cols])
        dots = jnp.sum(p * ga, -1, keepdims=True)
        g = (p * (ga - dots)).astype(bf16)
        gq_ref[:, cols] = (nn(g, k) * SCALE).astype(bf16)
        gkt[cols, :] = (tn(q, g) * SCALE).astype(bf16)
        gvt[cols, :] = tn(gctx, p.astype(bf16)).astype(bf16)
    gk_ref[...] = gkt[...].T
    gv_ref[...] = gvt[...].T
    gq, gk, gv = gq_ref[...], gk_ref[...], gv_ref[...]
    sums_ref[0:1, :] = jnp.sum(gq.astype(f32), 0, keepdims=True)
    sums_ref[1:2, :] = jnp.sum(gv.astype(f32), 0, keepdims=True)
    acc[...] += nt(gq, wq_ref[...]) + nt(gk, wk_ref[...]) + nt(gv, wv_ref[...])

    @pl.when(step == pl.num_programs(0) - 1)
    def _():
        gtok_ref[...] = acc[...].astype(bf16)


def attention_back(sc, q, k, v, gctx, lse, wq, wk, wv, gr, piece, deps):
    length, d = q.shape
    wide = GROUP * HEAD
    steps = d // wide
    cols = lambda r: pl.BlockSpec((r, wide), lambda i, s: (0, i))
    return call(
        functools.partial(attention_back_kernel, piece),
        sc,
        (*far(q, k, v), gctx, *far(lse, wq, wk, wv), gr),
        [
            cols(length), cols(length), cols(length), cols(length),
            pl.BlockSpec((1, SLOT, length), lambda i, s: (i, 0, 0)),
            cols(d), cols(d), cols(d), whole(length, d),
        ],
        [shape(bf16, length, d)] * 4 + [shape(f32, SLOT, d)],
        [cols(length), cols(length), cols(length), whole(length, d), cols(SLOT)],
        (steps,),
        [
            pltpu.VMEM((length, d), f32), pltpu.VMEM((length, length), f32),
            pltpu.VMEM((wide, length), bf16), pltpu.VMEM((wide, length), bf16),
        ],
        "attention_back", 0, deps,
    )


def weight_total(two, lo_refs, lp_ref, go_ref, gp_ref):
    lo = lo_refs[0][...].reshape(lo_refs[0].shape[-2:])
    if len(lo_refs) > 1:
        lo = jnp.where(pl.program_id(0) < two, lo, lo_refs[1][...].reshape(lo.shape))
    return nn(lo, go_ref[0]) + nn(lp_ref[0, 0], gp_ref[0])


def weight_send_kernel(lefts, two, sc_ref, *refs):
    lo_refs, (lp_ref, go_ref, gp_ref, out_ref) = refs[:lefts], refs[lefts:]
    out_ref[0] = weight_total(two, lo_refs, lp_ref, go_ref, gp_ref).astype(bf16)


def down_total(lo_ref, lp_ref, go_ref, gp_ref):
    return nn(lo_ref[0, 0], go_ref[...]) + nn(lp_ref[0], gp_ref[...])


def down_send_kernel(sc_ref, lo_ref, lp_ref, go_ref, gp_ref, out_ref):
    out_ref[0] = down_total(lo_ref, lp_ref, go_ref, gp_ref).astype(bf16)


def down_mid_kernel(sc_ref, lo_ref, lp_ref, go_ref, gp_ref, got_ref, near_ref, far_ref):
    total = down_total(lo_ref, lp_ref, go_ref, gp_ref) + got_ref[pl.program_id(0)].astype(f32)
    half = total.shape[0] // 2
    for z in range(2):
        part = total[z * half : (z + 1) * half].astype(bf16)

        @pl.when(sc_ref[3] == z)
        def _():
            near_ref[0] = part

        @pl.when(sc_ref[3] != z)
        def _():
            far_ref[0] = part


def down_stage(kernel, sc, operands, got, outs, out_specs, steps, x, h, name, deps, micros=0):
    lo, lp, go, gp = operands
    rows = lo.shape[2]
    return call(
        kernel, sc, far(lo, lp) + (go, gp) + got,
        [
            pl.BlockSpec((1, 1) + lo.shape[2:], lambda i, s: (2 * x(i, s) + s[1], h(s), 0, 0)),
            pl.BlockSpec((1, rows, lp.shape[2]), lambda i, s: (x(i, s), h(s), 0)),
            whole(*go.shape), whole(*gp.shape),
        ]
        + [whole(*g.shape) for g in got],
        outs, out_specs, (steps,), [], name, micros, deps,
    )


def deal(sc_ref, total, step, keep_ref, send_ref):
    rows = total.shape[0] // 4
    spot = pl.ds(step * rows if isinstance(step, int) else pl.multiple_of(step * rows, rows), rows)
    for h in range(2):
        for z in range(2):
            part = total[(2 * h + z) * rows : (2 * h + z + 1) * rows].astype(bf16)

            @pl.when(sc_ref[2] == h)
            def _():
                keep_ref[sc_ref[3] ^ z, spot, :] = part

            @pl.when(sc_ref[2] != h)
            def _():
                send_ref[sc_ref[3] ^ z, spot, :] = part


def weight_keep_kernel(lefts, two, sc_ref, *refs):
    lo_refs, (lp_ref, go_ref, gp_ref, recv_ref, keep_ref, send_ref) = refs[:lefts], refs[lefts:]
    total = weight_total(two, lo_refs, lp_ref, go_ref, gp_ref) + recv_ref[0].astype(f32)
    deal(sc_ref, total, pl.program_id(0), keep_ref, send_ref)


def pack_kernel(sc_ref, qkv_ref, one_ref, two_ref, bup_ref, own_ref, far_ref):
    rows = jnp.concatenate([qkv_ref[0:2], one_ref[0:3], two_ref[0:3]], 0)
    quarter = rows.shape[1] // 4
    own_ref[...] = jnp.zeros_like(own_ref)
    far_ref[...] = jnp.zeros_like(far_ref)
    for x in range(2):
        for c in range(2):
            q = 2 * x + c
            left = rows[:, q * quarter : (q + 1) * quarter]

            def put(ref):
                ref[x, 0:8, :quarter] = left
                for j in range(4):
                    ref[x, 8 + j : 9 + j, :quarter] = bup_ref[q, :, j * quarter : (j + 1) * quarter]

            @pl.when(sc_ref[1] == c)
            def _():
                put(own_ref)

            @pl.when(sc_ref[1] != c)
            def _():
                put(far_ref)


def pack(sc, qkv, one, two, bup):
    out = shape(f32, 2, EXTRA, 2 * SMALL)
    return call(
        pack_kernel, sc, (qkv, one, two, bup), [whole(*t.shape) for t in (qkv, one, two, bup)],
        [out, out], [whole(*out.shape)] * 2, (1,), [], "pack", 0,
    )


def qkv_totals(lo_ref, lp_ref, own, par):
    return [nn(lo_ref[0], o[...]) + nn(lp_ref[0, 0], p[...]) for o, p in zip(own, par)]


def qkv_send_kernel(sc_ref, lo_ref, lp_ref, own_ref, par_ref, *refs):
    out_ref = refs[6]
    rows = lo_ref.shape[1]
    for n, total in enumerate(qkv_totals(lo_ref, lp_ref, refs[:3], refs[3:6])):
        out_ref[n * rows : (n + 1) * rows, :] = total.astype(bf16)
    vec = own_ref[1 - sc_ref[0]] + par_ref[1 - sc_ref[0]]
    out_ref[3 * rows :, :] = jnp.zeros((EXTRA, out_ref.shape[1]), bf16)
    out_ref[3 * rows :, : vec.shape[1]] = vec.astype(bf16)


def qkv_keep_kernel(sc_ref, lo_ref, lp_ref, own_ref, par_ref, *refs):
    recv_ref, keep_ref, send_ref = refs[6:]
    rows = lo_ref.shape[1]
    for n, total in enumerate(qkv_totals(lo_ref, lp_ref, refs[:3], refs[3:6])):
        total += recv_ref[n * rows : (n + 1) * rows, :].astype(f32)
        deal(sc_ref, total, n, keep_ref, send_ref)
    base = keep_ref.shape[1] - EXTRA
    vec = own_ref[sc_ref[0]] + par_ref[sc_ref[0]]
    wide = vec.shape[1]
    vec += recv_ref[3 * rows :, :wide].astype(f32)
    blank = jnp.zeros((EXTRA, keep_ref.shape[2]), bf16)
    for ref in (keep_ref, send_ref):
        for z in range(2):
            ref[z, base:, :] = blank
            ref[z, base:, :wide] = vec.astype(bf16)


def qkv_specs(xt, halves, own, other):
    x = (lambda s: 1 - s[0]) if other else (lambda s: s[0])
    return [
        pl.BlockSpec((1,) + xt.shape[1:], lambda i, s: (2 * x(s) + s[1], 0, 0)),
        pl.BlockSpec((1, 1) + halves.shape[2:], lambda i, s: (x(s), 6, 0, 0)),
    ] + [whole(2, EXTRA, 2 * SMALL)] * 2 + [whole(*own.shape)] * 6


def qkv_send(sc, operands, deps):
    xt, halves, _, _, own = operands[:5]
    rows, wide = xt.shape[1], own.shape[1]
    out = shape(bf16, 3 * rows + EXTRA, wide)
    return call(
        qkv_send_kernel, sc, far(xt, halves) + operands[2:], qkv_specs(xt, halves, own, True), out, whole(*out.shape),
        (1,), [], "qkv_send", 0, deps,
    )


def qkv_keep(sc, operands, recv, deps):
    xt, halves, _, _, own = operands[:5]
    rows, wide = xt.shape[1], own.shape[1]
    out = shape(bf16, 2, 3 * rows // 4 + EXTRA, wide)
    return call(
        qkv_keep_kernel, sc, far(xt, halves) + operands[2:] + (recv,),
        qkv_specs(xt, halves, own, False) + [whole(*recv.shape)],
        [out, out], [whole(*out.shape)] * 2, (1,), [], "qkv_keep", 0, deps,
    )


def order_kernel(sc_ref, *refs):
    out_ref = refs[-1]
    for mask, piece in enumerate(refs[:-1]):
        out_ref[sc_ref[0] ^ mask] = piece[...]


def weight_specs(lefts, halves, grads, grads_p, other, steps, turn):
    x = (lambda s: 1 - s[0]) if other else (lambda s: s[0])
    specs = []
    for left in lefts:
        if left.ndim == 4:
            specs.append(
                pl.BlockSpec((1, 1) + left.shape[2:], lambda i, s: (2 * x(s) + s[1], i, 0, 0))
            )
        else:
            specs.append(pl.BlockSpec((1,) + left.shape[1:], lambda i, s: (2 * x(s) + s[1], 0, 0)))
    specs.append(pl.BlockSpec((1, 1) + halves.shape[2:], lambda i, s: (x(s), turn(i), 0, 0)))
    one = grads.shape[0] == 1
    block = pl.BlockSpec((1,) + grads.shape[1:], lambda i, s: (0 if one else i, 0, 0))
    return (*far(*lefts), *far(halves), grads, grads_p), specs + [block, block]


def weight_send(sc, operands, steps, two, turn, name, deps=(), micros=0):
    args, specs = weight_specs(*operands, True, steps, turn)
    rows, wide = operands[1].shape[2], operands[2].shape[2]
    return call(
        functools.partial(weight_send_kernel, len(operands[0]), two),
        sc, args, specs, shape(bf16, steps, rows, wide),
        pl.BlockSpec((1, rows, wide), lambda i, s: (i, 0, 0)), (steps,), [],
        name, micros, deps,
    )


def weight_keep(sc, operands, recv, steps, two, turn, name, deps=(), micros=0):
    args, specs = weight_specs(*operands, False, steps, turn)
    rows, wide = operands[1].shape[2], operands[2].shape[2]
    out = shape(bf16, 2, steps * rows // 4, wide)
    return call(
        functools.partial(weight_keep_kernel, len(operands[0]), two),
        sc, args + (recv,), specs + [pl.BlockSpec((1, rows, wide), lambda i, s: (i, 0, 0))],
        [out, out], [whole(*out.shape)] * 2, (steps,), [],
        name, micros, deps,
    )


def place_kernel(spots, extra, sc_ref, *refs):
    parts, out_refs = refs[:4], refs[4:]
    rows = (parts[0].shape[0] - extra) // len(spots)
    wide = parts[0].shape[1]
    for side, part in enumerate(parts):
        slot = 2 * (sc_ref[2] ^ (side // 2)) + (sc_ref[3] ^ (side % 2))
        for n, (out, down, left) in enumerate(spots):
            top = pl.multiple_of((4 * down + slot) * rows, rows)
            out_refs[out][pl.ds(top, rows), left * wide : (left + 1) * wide] = part[
                n * rows : (n + 1) * rows, :
            ].astype(f32)


def place(sc, parts, spots, dims, extra, name, deps=()):
    return call(
        functools.partial(place_kernel, spots, extra),
        sc, parts, [whole(*parts[0].shape)] * 4,
        [shape(f32, *dim) for dim in dims], [whole(*dim) for dim in dims], (1,), [],
        name, 0, deps,
    )


def flip(value, axis, mask):
    count = lax.axis_size(axis)
    return lax.ppermute(value, axis, [(i, i ^ mask) for i in range(count)])


def flip_both(value, row_mask, seq_mask):
    rows, seq = lax.axis_size("rows"), lax.axis_size("seq")
    pairs = [
        (r * seq + s, (r ^ row_mask) * seq + (s ^ seq_mask)) for r in range(rows) for s in range(seq)
    ]
    return lax.ppermute(value, ("rows", "seq"), pairs)


def row_flips():
    count = lax.axis_size("rows")
    assert count >= 8 and count & (count - 1) == 0
    return [2, 6] + [1 << b for b in range(3, count.bit_length() - 1)]


def join_kernel(sc_ref, left_ref, right_ref, out_ref):
    out_ref[...] = add(left_ref[...], right_ref[...])


def join(sc, left, right, deps, name, micros=0):
    block = whole(*left.shape)
    return call(
        join_kernel, sc, (left, right), [block, block], shape(bf16, *left.shape), block, (1,), [],
        name, micros, deps,
    )


def join_two_kernel(slot, sc_ref, left_ref, right_ref, near_ref, far_ref):
    own = 0 if slot is None else sc_ref[slot]
    near_ref[...] = add(left_ref[own], right_ref[own])
    far_ref[...] = add(left_ref[1 - own], right_ref[1 - own])


def join_two(sc, left, right, deps, name, slot=None):
    block, half = whole(*left.shape), whole(*left.shape[1:])
    out = shape(bf16, *left.shape[1:])
    return call(
        functools.partial(join_two_kernel, slot), sc, (left, right), [block, block], [out, out],
        [half, half], (1,), [], name, 0, deps,
    )


def across(sc, value, masks, deps, name):
    first, *rest = masks
    value = join(sc, value, flip(value, "rows", first), deps, name)
    for mask in rest:
        value = add(value, flip(value, "rows", mask))
    return value


def gathered(value, near):
    return (value,) + tuple(flip(value, "rows", mask) for mask in (near, 1, near ^ 1))


def add(left, right):
    return (left.astype(f32) + right.astype(f32)).astype(bf16)


def moved(pieces):
    return [flip(piece, "seq", mask) if mask else piece for mask, piece in enumerate(pieces)]


def gather_back(sc, row, count, name, deps=()):
    row = row.reshape(count, -1, row.shape[-1])
    pieces = tuple(flip(row[mask], "seq", mask) if mask else row[0] for mask in range(count))
    return call(
        order_kernel, sc, pieces, [whole(*row.shape[1:])] * count, shape(row.dtype, *row.shape),
        whole(*row.shape), (1,), [], name, 0, deps,
    )


def per_device(
    tokens,
    w_query,
    b_query,
    w_key,
    w_value,
    b_value,
    w_out,
    b_out,
    gain_one,
    shift_one,
    w_up,
    b_up,
    w_down,
    b_down,
    gain_two,
    shift_two,
    passage_starts,
    queries,
    choices,
    cotangent,
):
    seq_count = lax.axis_size("seq")
    row_count = lax.axis_size("rows")
    own_s = lax.axis_index("seq")
    own_r = lax.axis_index("rows")
    row_block, piece, d = tokens.shape
    assert row_block == seq_count == 4
    ff = w_up.shape[1]
    quarter = d // 4
    core, xside = own_s % 2, own_s // 2
    own_lin = own_r * seq_count + own_s
    devices = row_count * seq_count
    masks = row_flips()
    wsc = jnp.stack([xside, core, own_r % 2, (own_r // 2 ^ own_r // 4) % 2]).astype(jnp.int32)
    starts = lax.dynamic_index_in_dim(passage_starts, own_s, 0, keepdims=False)
    sc = jnp.concatenate([own_s[None].astype(jnp.int32), starts, own_lin[None].astype(jnp.int32)])
    row = lambda v: v.reshape(1, -1)
    swap = lambda t: flip(t, "seq", 1)

    own = own_s[None].astype(jnp.int32)
    pieces, code = begin(own, tokens, queries, choices)
    pieces = moved(pieces)
    x = jnp.concatenate(pieces, 0)
    code_all = lax.all_gather(code, ("rows", "seq"), axis=0, tiled=True)

    cot = jnp.concatenate(moved(pick(own, cotangent, (pieces[1],))), 0)

    q, k, v, ctxt, lse, xt, xhat_one, inv_one, hid, hidt = attention_forward(
        sc, x, w_query, w_key, w_value, row(b_query), row(b_value), w_out, row(b_out),
        row(gain_one), row(shift_one), piece,
    )
    actt, slope, xhat_two, inv_two, mixed_row, pool = feed_forward(
        sc, hid, w_up, row(b_up), w_down, row(b_down), row(gain_two), row(shift_two), piece, (cot,)
    )

    pool = pool.astype(bf16)
    if row_count == 8:
        near = jnp.concatenate(
            [pool, flip(pool, "seq", 2), flip(pool, "rows", 1), flip_both(pool, 1, 2)], 0
        )
        mid = jnp.concatenate(
            [near, flip(near, "rows", 2), flip(near, "rows", 6), flip(near, "rows", 4)], 0
        )
        pooled = jnp.concatenate([mid, flip(mid, "seq", 1)], 0)
        places = cube_place
    else:
        near = pool
        pooled = lax.all_gather(pool, ("rows", "seq"), axis=0, tiled=True)
        pooled = jnp.roll(pooled, -own_lin * SLOT, 0)
        places = turned_place

    quarters = lambda t: t.reshape(4, -1, t.shape[-1])
    halves = swap(
        core_halves(wsc, quarters(actt), [quarters(t) for t in (hidt, ctxt, xt)], (near,))
    )

    losses_all, gd, gr_two, sums_two = retrieval(
        sc, code_all, pooled, cot, xhat_two, inv_two, row(gain_two), piece, places, devices,
        (halves,),
    )
    query_losses = lax.dynamic_slice_in_dim(
        losses_all[:, 0], own_lin * queries.shape[0], queries.shape[0]
    )

    gd_p = swap(gd)
    gug, bup, gr_one, gctx, sums_one = feed_back(
        sc, gd, gr_two, w_down, w_up, slope, xhat_one, inv_one, row(gain_one), w_out, (gd_p,)
    )

    near, *rest = masks
    part = ff // 8
    down_ops = (actt.reshape(4, 2, part, -1), halves.reshape(2, -1, piece * seq_count), gd, gd_p)
    down_sent = down_stage(
        down_send_kernel, wsc, down_ops, (), shape(bf16, 2, part, d),
        pl.BlockSpec((1, part, d), lambda i, s: (i, 0, 0)), 2,
        lambda i, s: i, lambda s: 1 - s[2], "down_send", (gug,),
    )
    down_got = flip(down_sent, "rows", 1)

    up_ops = ((quarters(hidt), quarters(ctxt)), halves, gug, swap(gug))
    up_turn = lambda i: 4 + i // 4
    up_sent = weight_send(wsc, up_ops, 5, 4, up_turn, "up_send", (down_sent,))
    up_got = flip(up_sent, "seq", 2)

    gq, gk, gv, gtok, sums_qkv = attention_back(
        sc, q, k, v, gctx, lse, w_query, w_key, w_value, gr_one, piece, (up_sent,)
    )
    vec, vec_far = pack(wsc, sums_qkv, sums_one, sums_two, bup)
    qkv_ops = (
        quarters(xt), halves, vec, swap(vec_far), gq, gk, gv, swap(gq), swap(gk), swap(gv)
    )
    qkv_sent = qkv_send(wsc, qkv_ops, ())
    qkv_got = flip(qkv_sent, "seq", 2)
    pair = shape(bf16, 2, part // 2, d)
    each = pl.BlockSpec((1, part // 2, d), lambda i, s: (i, 0, 0))
    down_near, down_far = down_stage(
        down_mid_kernel, wsc, down_ops, (down_got,), [pair, pair], [each, each], 2,
        lambda i, s: i, lambda s: s[2], "down_mid", (qkv_sent,), 3,
    )
    up_parts = weight_keep(
        wsc, up_ops, up_got, 5, 4, up_turn, "up_keep", (vec, down_near), PIN
    )
    down_sum = join(wsc, down_near, flip(down_far, "rows", near), (up_parts[0],), "down_join_a", 3)
    for mask in rest[1:]:
        down_sum = add(down_sum, flip(down_sum, "rows", mask))
    qkv_parts = qkv_keep(wsc, qkv_ops, qkv_got, (down_sum,))
    up_near, up_far = join_two(
        wsc, up_parts[0], flip(up_parts[1], "rows", 1), (qkv_parts[0],), "up_join_y"
    )
    qkv_near, qkv_far = join_two(
        wsc, qkv_parts[0], flip(qkv_parts[1], "rows", 1), (up_near,), "qkv_join_y"
    )
    up_sum = join(wsc, up_near, flip(up_far, "rows", near), (qkv_near,), "up_join_a")
    down_own, down_other = join_two(
        wsc, down_sum, flip(down_sum, "rows", rest[0]), (up_sum,), "down_join_b", 0
    )
    qkv_sum = join(wsc, qkv_near, flip(qkv_far, "rows", near), (down_own,), "qkv_join_a")
    down_sum = join(wsc, down_own, flip(down_other, "seq", 2), (qkv_sum,), "down_join_x")
    down_all = gathered(down_sum, near)
    up_sum = across(wsc, up_sum, rest, (down_sum,), "up_join_b")
    up_all = gathered(up_sum, near)
    (grad_down,) = place(wsc, down_all, [(0, 0, 0)], [(4 * quarter, d)], 0, "down_place", (up_sum,))
    qkv_sum = across(wsc, qkv_sum, rest, (grad_down,), "qkv_join_b")
    qkv_all = gathered(qkv_sum, near)
    mixed = gather_back(sc, mixed_row, seq_count, "mixed_order", (down_sum,))
    grad_tokens = gather_back(sc, gtok, seq_count, "tokens_order", (qkv_sum,))
    grad_up, grad_o = place(
        wsc, up_all, [(0, 0, n) for n in range(4)] + [(1, 0, 0)],
        [(quarter, ff), (quarter, d)], 0, "up_place", (qkv_sum,),
    )
    grad_q, grad_k, grad_v = place(
        wsc, qkv_all, [(n, 0, 0) for n in range(3)], [(quarter, d)] * 3, EXTRA, "qkv_place"
    )

    eight = qkv_sum[3 * quarter // 4 :, :quarter].astype(f32)
    return (
        mixed,
        query_losses,
        grad_tokens,
        grad_q,
        eight[0],
        grad_k,
        grad_v,
        eight[1],
        grad_o,
        eight[2],
        eight[3],
        eight[4],
        grad_up,
        eight[8:12].reshape(-1),
        grad_down,
        eight[5],
        eight[6],
        eight[7],
    )


def solution(mesh):
    weights = (P(),) * 15
    placed = (
        (P("rows", "seq", None),)
        + weights
        + (
            P("rows", None),
            P(("rows", "seq"), None),
            P(("rows", "seq"), None),
            P("rows", "seq", None),
        )
    )
    return jax.shard_map(
        per_device,
        mesh=mesh,
        in_specs=placed,
        out_specs=(
            P("rows", "seq", None),
            P(("rows", "seq")),
            P("rows", "seq", None),
            P("seq", None),
            P("seq"),
            P("seq", None),
            P("seq", None),
            P("seq"),
            P("seq", None),
            P("seq"),
            P("seq"),
            P("seq"),
            P("seq", None),
            P("seq"),
            P("seq", None),
            P("seq"),
            P("seq"),
            P("seq"),
        ),
        check_vma=False,
    )
```

```python
import functools

import jax
import jax.numpy as jnp
from jax import lax
from jax.experimental import pallas as pl
from jax.experimental.pallas import tpu as pltpu
from jax.sharding import PartitionSpec as P

HEADS = 12
HEAD = 64
PASS = 6
CH = 32
SLOT = 8
GROUP = 4
SUB = 768
SCALE = HEAD ** (-0.5)

norm_eps = 1e-05
f32 = jnp.float32
bf16 = jnp.bfloat16
VMEM_BYTES = 28 * 1024 * 1024
PIN = 100
EXTRA = 16
SMALL = 128


def params():
    return pltpu.CompilerParams(vmem_limit_bytes=VMEM_BYTES)


def cost(micros):
    return pl.CostEstimate(flops=int(micros * 1.15e9), bytes_accessed=0, transcendentals=0)


def nt(a, b):
    return lax.dot_general(a, b, (((1,), (1,)), ((), ())), preferred_element_type=f32)


def tn(a, b):
    return lax.dot_general(a, b, (((0,), (0,)), ((), ())), preferred_element_type=f32)


def nn(a, b):
    return jnp.dot(a, b, preferred_element_type=f32)


def stats(values):
    center = values - jnp.mean(values, -1, keepdims=True)
    inv = lax.rsqrt(jnp.mean(center * center, -1, keepdims=True) + norm_eps)
    return center * inv, inv


def norm_back(grad, xhat, inv, gain):
    gx = grad * gain
    return inv * (
        gx - jnp.mean(gx, -1, keepdims=True) - xhat * jnp.mean(gx * xhat, -1, keepdims=True)
    )


def true_places(own_seq, count, piece, axis):
    shape = (count, 1) if axis == 0 else (1, count)
    local = lax.broadcasted_iota(jnp.int32, shape, axis)
    block = local // piece
    return (block ^ own_seq) * piece + (local - block * piece)


def segments(sc_ref, places):
    total = jnp.zeros(places.shape, jnp.int32)
    for j in range(PASS):
        total += (sc_ref[1 + j] <= places).astype(jnp.int32)
    return total


def segment_bias(sc_ref, length, piece):
    col = segments(sc_ref, true_places(sc_ref[0], length, piece, 0))
    row = segments(sc_ref, true_places(sc_ref[0], length, piece, 1))
    return jnp.where(col == row, 0.0, -1e30)


def call(kernel, sc, args, specs, outs, out_specs, grid, scratch, name, micros, deps=()):
    count = len(args)

    def body(sc_ref, *refs):
        kernel(sc_ref, *refs[:count], *refs[count + len(deps) :])

    hold = pl.BlockSpec(memory_space=pl.ANY)
    return pl.pallas_call(
        body,
        grid_spec=pltpu.PrefetchScalarGridSpec(
            num_scalar_prefetch=1,
            grid=grid,
            in_specs=list(specs) + [hold] * len(deps),
            out_specs=out_specs,
            scratch_shapes=scratch,
        ),
        out_shape=outs,
        compiler_params=params(),
        cost_estimate=cost(micros),
        name=name,
    )(sc, *args, *deps)


def shape(t, *dims):
    return jax.ShapeDtypeStruct(dims, t)


def kept(t, *dims):
    return pltpu.HBM(dims, t)


def far(*values):
    return tuple(pltpu.with_memory_space_constraint(v, pltpu.HBM) for v in values)


def whole(*dims):
    return pl.BlockSpec(dims, lambda i, s: (0,) * len(dims))


def attention_kernel(
    piece, sc_ref, x_ref, wq_ref, wk_ref, wv_ref, bq_ref, bv_ref, wo_ref, bo_ref, go_ref, so_ref,
    q_ref, k_ref, v_ref, ctxt_ref, lse_ref, xt_ref, xhat_ref, inv_ref, hid_ref, hidt_ref,
    acc, bias,
):
    step = pl.program_id(0)
    length = x_ref.shape[0]
    x = x_ref[...]
    q_ref[...] = (nn(x, wq_ref[...]) + bq_ref[...]).astype(bf16)
    k_ref[...] = nn(x, wk_ref[...]).astype(bf16)
    v_ref[...] = (nn(x, wv_ref[...]) + bv_ref[...]).astype(bf16)

    @pl.when(step == 0)
    def _():
        bias[...] = segment_bias(sc_ref, length, piece)
        acc[...] = x.astype(f32) + bo_ref[...]

    for h in range(GROUP):
        cols = slice(h * HEAD, (h + 1) * HEAD)
        raw = nt(k_ref[:, cols], q_ref[:, cols] * jnp.asarray(SCALE, bf16))
        scores = raw + bias[...]
        top = jnp.max(scores, 0, keepdims=True)
        e = jnp.exp(scores - top)
        total = jnp.sum(e, 0, keepdims=True)
        p = (e * (1.0 / total)).astype(bf16)
        ctxt_ref[cols, :] = tn(v_ref[:, cols], p).astype(bf16)
        lse_ref[0, h : h + 1, :] = top + jnp.log(total)
    acc[...] += tn(ctxt_ref[...], wo_ref[...])

    for j in range(x_ref.shape[1] // xt_ref.shape[0]):
        wide = xt_ref.shape[0]

        @pl.when(step == j)
        def _():
            xt_ref[...] = x_ref[:, j * wide : (j + 1) * wide].T

    @pl.when(step == pl.num_programs(0) - 1)
    def _():
        xhat, inv = stats(acc[...])
        xhat_ref[...] = xhat
        inv_ref[...] = inv
        hid = (xhat * go_ref[...] + so_ref[...]).astype(bf16)
        hid_ref[...] = hid
        hidt_ref[...] = hid.T


def attention_forward(sc, x, wq, wk, wv, bq, bv, wo, bo, go, so, piece):
    length, d = x.shape
    wide = GROUP * HEAD
    steps = d // wide
    cols = lambda r: pl.BlockSpec((r, wide), lambda i, s: (0, i))
    rows = lambda c: pl.BlockSpec((wide, c), lambda i, s: (i, 0))
    return call(
        functools.partial(attention_kernel, piece),
        sc,
        (x, *far(wq, wk, wv), bq, bv, *far(wo), bo, go, so),
        [
            whole(length, d), cols(d), cols(d), cols(d), cols(1), cols(1), rows(d),
            whole(1, d), whole(1, d), whole(1, d),
        ],
        [
            kept(bf16, length, d), kept(bf16, length, d), kept(bf16, length, d),
            kept(bf16, d, length), kept(f32, steps, SLOT, length), kept(bf16, d, length),
            kept(f32, length, d), kept(f32, length, 1), shape(bf16, length, d),
            kept(bf16, d, length),
        ],
        [
            cols(length), cols(length), cols(length), rows(length),
            pl.BlockSpec((1, SLOT, length), lambda i, s: (i, 0, 0)), rows(length),
            whole(length, d), whole(length, 1), whole(length, d), whole(d, length),
        ],
        (steps,),
        [pltpu.VMEM((length, d), f32), pltpu.VMEM((length, length), f32)],
        "attention_forward", 0,
    )


def feed_kernel(
    piece, sc_ref, hid_ref, wu_ref, bu_ref, wd_ref, bd_ref, gt_ref, st_ref,
    actt_ref, slope_ref, xhat_ref, inv_ref, mixed_ref, pool_ref,
    acc,
):
    step = pl.program_id(0)
    length = hid_ref.shape[0]

    @pl.when(step == 0)
    def _():
        acc[...] = hid_ref[...].astype(f32) + bd_ref[...]

    for c in range(0, wu_ref.shape[1], SUB):
        cols = slice(c, c + SUB)
        up = nn(hid_ref[...], wu_ref[:, cols]) + bu_ref[:, cols]
        e = jnp.exp(-0.5 * up * up)
        cum = 0.5 + 0.5 * lax.erf(up * (2.0 ** -0.5))
        slope_ref[0, :, cols] = (cum + up * (e * 0.3989422804014327)).astype(bf16)
        act = (up * cum).astype(bf16)
        actt_ref[cols, :] = act.T
        acc[...] += nn(act, wd_ref[cols, :])

    @pl.when(step == pl.num_programs(0) - 1)
    def _():
        xhat, inv = stats(acc[...])
        xhat_ref[...] = xhat
        inv_ref[...] = inv
        mixed = (xhat * gt_ref[...] + st_ref[...]).astype(bf16)
        mixed_ref[...] = mixed
        places = true_places(sc_ref[0], length, piece, 1)
        slot = lax.broadcasted_iota(jnp.int32, (SLOT, 1), 0)
        start = jnp.full((SLOT, 1), -1, jnp.int32)
        for j in range(PASS):
            start = jnp.where(slot == j, sc_ref[1 + j], start)
        pool_ref[...] = nn((places == start).astype(f32).astype(bf16), mixed)


def feed_forward(sc, hid, wu, bu, wd, bd, gt, st, piece, deps):
    length, d = hid.shape
    ff = wu.shape[1]
    steps = ff // d
    return call(
        functools.partial(feed_kernel, piece),
        sc,
        (hid, *far(wu), bu, *far(wd), bd, gt, st),
        [
            whole(length, d),
            pl.BlockSpec((d, d), lambda i, s: (0, i)),
            pl.BlockSpec((1, d), lambda i, s: (0, i)),
            pl.BlockSpec((d, d), lambda i, s: (i, 0)),
            whole(1, d), whole(1, d), whole(1, d),
        ],
        [
            kept(bf16, ff, length), kept(bf16, steps, length, d), kept(f32, length, d),
            kept(f32, length, 1), kept(bf16, length, d), shape(f32, SLOT, d),
        ],
        [
            pl.BlockSpec((d, length), lambda i, s: (i, 0)),
            pl.BlockSpec((1, length, d), lambda i, s: (i, 0, 0)),
            whole(length, d), whole(length, 1), whole(length, d), whole(SLOT, d),
        ],
        (steps,),
        [pltpu.VMEM((length, d), f32)],
        "feed_forward", 0, deps,
    )


def begin_kernel(sc_ref, tokens_ref, queries_ref, choices_ref, code_ref, *piece_refs):
    for mask, piece_ref in enumerate(piece_refs):
        piece_ref[...] = tokens_ref[sc_ref[0] ^ mask]
    d = queries_ref.shape[1]
    choices = choices_ref[...]
    owner = choices // PASS
    code_ref[:, :d] = queries_ref[...]
    code_ref[:, d : d + CH] = owner.astype(f32).astype(bf16)
    code_ref[:, d + CH :] = (choices - owner * PASS).astype(f32).astype(bf16)


def begin(sc, tokens, queries, choices):
    count, d = queries.shape
    outs = [shape(bf16, count, d + 2 * CH)] + [shape(bf16, *tokens.shape[1:])] * tokens.shape[0]
    code, *pieces = call(
        begin_kernel, sc, far(tokens, queries, choices), [whole(*tokens.shape), whole(count, d), whole(count, CH)],
        outs, [whole(*o.shape) for o in outs], (1,), [], "begin", 0,
    )
    return pieces, code


def pick_kernel(sc_ref, rows_ref, *piece_refs):
    for mask, piece_ref in enumerate(piece_refs):
        piece_ref[...] = rows_ref[sc_ref[0] ^ mask]


def pick(sc, rows, deps):
    outs = [shape(bf16, *rows.shape[1:])] * rows.shape[0]
    return call(
        pick_kernel, sc, far(rows), [whole(*rows.shape)], outs, [whole(*o.shape) for o in outs],
        (1,), [], "pick", 0, deps,
    )


def halves_kernel(sc_ref, act_ref, hid_ref, ctx_ref, x_ref, out_ref):
    rows = hid_ref.shape[1]
    for n in range(act_ref.shape[1] // rows):
        out_ref[0, n] = act_ref[0, n * rows : (n + 1) * rows, :]
    for n, ref in enumerate((hid_ref, ctx_ref, x_ref)):
        out_ref[0, act_ref.shape[1] // rows + n] = ref[0]


def core_halves(sc, act, rest, deps):
    block = lambda t: pl.BlockSpec((1,) + t.shape[1:], lambda i, s: (2 * i + 1 - s[1], 0, 0))
    rows, length = rest[0].shape[1:]
    blocks = act.shape[1] // rows + len(rest)
    return call(
        halves_kernel, sc, far(act, *rest), [block(t) for t in (act, *rest)],
        shape(bf16, 2, blocks, rows, length),
        pl.BlockSpec((1, blocks, rows, length), lambda i, s: (i, 0, 0, 0)), (2,), [],
        "core_halves", 0, deps,
    )


def loss_kernel(
    piece, steps, devices, code_ref, sc_ref, q_ref, pool_ref, cot_ref, xhat_ref, inv_ref, gt_ref,
    loss_ref, gd_ref, gr_ref, sums_ref, gp,
):
    step = pl.program_id(0)
    d = pool_ref.shape[1]

    @pl.when(step == 0)
    def _():
        gp[...] = jnp.zeros_like(gp)
        sums_ref[...] = jnp.zeros_like(sums_ref)

    @pl.when(step < steps)
    def _():
        queries = q_ref[:, :d]
        logits = nt(queries, pool_ref[...])
        lanes = lax.broadcasted_iota(jnp.int32, (1, logits.shape[1]), 1)
        owner = q_ref[:, d : d + CH].astype(f32).astype(jnp.int32)
        inner = q_ref[:, d + CH :].astype(f32).astype(jnp.int32)
        pos = code_ref(owner, sc_ref[7], devices) * SLOT + inner
        first = (pos[:, 0:1] == lanes).astype(f32)
        times = first
        for c in range(1, CH):
            times += (pos[:, c : c + 1] == lanes).astype(f32)
        held = times > 0.0
        top = jnp.max(jnp.where(held, logits, -jnp.inf), -1, keepdims=True)
        e = jnp.where(held, times * jnp.exp(jnp.minimum(logits - top, 0.0)), 0.0)
        total = jnp.sum(e, -1, keepdims=True)
        positive = jnp.sum(first * logits, -1, keepdims=True)
        loss_ref[...] = top + jnp.log(total) - positive
        grad = e[:, :128] * (1.0 / total) - first[:, :128]
        high = grad.astype(bf16)
        lower = (grad - high.astype(f32)).astype(bf16)
        gp[...] += (tn(high, queries) + tn(lower, queries))[:SLOT]

    @pl.when(step >= steps)
    def _():
        block = (step - steps) ^ sc_ref[0]
        places = block * piece + lax.broadcasted_iota(jnp.int32, (piece, 1), 0)
        grad = cot_ref[...].astype(f32)
        for j in range(PASS):
            grad += jnp.where(places == sc_ref[1 + j], gp[j : j + 1, :], 0.0)
        xhat = xhat_ref[...]
        back = norm_back(grad, xhat, inv_ref[...], gt_ref[...])
        gr_ref[...] = back
        down = back.astype(bf16)
        gd_ref[...] = down
        sums_ref[0:1, :] += jnp.sum(down.astype(f32), 0, keepdims=True)
        sums_ref[1:2, :] += jnp.sum(grad * xhat, 0, keepdims=True)
        sums_ref[2:3, :] += jnp.sum(grad, 0, keepdims=True)


def cube_place(owner, own, devices):
    off = owner ^ own
    z = off >> 3
    return (off & 1) * 16 + (z ^ (z >> 1)) * 4 + ((off >> 1) & 3)


def turned_place(owner, own, devices):
    off = owner - own
    return jnp.where(off < 0, off + devices, off)


def retrieval(sc, code_all, pooled, cot, xhat, inv, gain, piece, places, devices, deps):
    count, width = code_all.shape
    length, d = cot.shape
    block = 512 if pooled.shape[0] <= 512 else 256
    steps, pieces = count // block, length // piece
    first = lambda i: jnp.minimum(i, steps - 1)
    second = lambda i: jnp.maximum(i - steps, 0)
    part = lambda c: pl.BlockSpec((piece, c), lambda i, s: (second(i), 0))
    return call(
        functools.partial(loss_kernel, piece, steps, devices, places),
        sc,
        (*far(code_all), pooled, *far(cot, xhat, inv), gain),
        [
            pl.BlockSpec((block, width), lambda i, s: (first(i), 0)),
            whole(*pooled.shape), part(d), part(d), part(1), whole(1, d),
        ],
        [shape(f32, count, 1), shape(bf16, length, d), shape(f32, length, d), shape(f32, SLOT, d)],
        [
            pl.BlockSpec((block, 1), lambda i, s: (first(i), 0)), part(d), part(d), whole(SLOT, d),
        ],
        (steps + pieces,),
        [pltpu.VMEM((SLOT, d), f32)],
        "retrieval", 0, deps,
    )


def feed_back_kernel(
    sc_ref, gd_ref, gr_ref, wd_ref, wu_ref, slope_ref, xhat_far, inv_ref, go_ref, wo_far,
    gug_ref, bup_ref, gr1_ref, gctx_ref, sums_ref,
    acc, xhat_ref, wo_ref, arrived,
):
    step = pl.program_id(0)
    last = pl.num_programs(0) - 1
    late = [
        pltpu.make_async_copy(xhat_far, xhat_ref, arrived.at[0]),
        pltpu.make_async_copy(wo_far, wo_ref, arrived.at[1]),
    ]

    @pl.when(step == 1)
    def _():
        for copy in late:
            copy.start()

    @pl.when(step == 0)
    def _():
        acc[...] = gr_ref[...]

    @pl.when(step < last)
    def _():
        gact = nt(gd_ref[...], wd_ref[...])
        gup = (gact * slope_ref[0].astype(f32)).astype(bf16)
        gug_ref[0] = gup
        bup_ref[0] = jnp.sum(gup.astype(f32), 0, keepdims=True)
        acc[...] += nt(gup, wu_ref[...])

    @pl.when(step == last)
    def _():
        for copy in late:
            copy.wait()
        grad = acc[...]
        xhat = xhat_ref[...]
        back = norm_back(grad, xhat, inv_ref[...], go_ref[...])
        gr1_ref[...] = back
        gab = back.astype(bf16)
        gug_ref[0] = gab
        gctx_ref[...] = nt(gab, wo_ref[...]).astype(bf16)
        sums_ref[0:1, :] = jnp.sum(gab.astype(f32), 0, keepdims=True)
        sums_ref[1:2, :] = jnp.sum(grad * xhat, 0, keepdims=True)
        sums_ref[2:3, :] = jnp.sum(grad, 0, keepdims=True)


def feed_back(sc, gd, gr, wd, wu, slope, xhat, inv, go, wo, deps):
    length, d = gd.shape
    steps = slope.shape[0]
    at = lambda i: jnp.minimum(i, steps - 1)
    return call(
        feed_back_kernel,
        sc,
        (gd, gr, *far(wd, wu, slope, xhat, inv), go, *far(wo)),
        [
            whole(length, d), whole(length, d),
            pl.BlockSpec((d, d), lambda i, s: (at(i), 0)),
            pl.BlockSpec((d, d), lambda i, s: (0, at(i))),
            pl.BlockSpec((1, length, d), lambda i, s: (at(i), 0, 0)),
            pl.BlockSpec(memory_space=pl.ANY), whole(length, 1), whole(1, d),
            pl.BlockSpec(memory_space=pl.ANY),
        ],
        [
            shape(bf16, steps + 1, length, d), shape(f32, steps, 1, d), shape(f32, length, d),
            shape(bf16, length, d), shape(f32, SLOT, d),
        ],
        [
            pl.BlockSpec((1, length, d), lambda i, s: (i, 0, 0)),
            pl.BlockSpec((1, 1, d), lambda i, s: (at(i), 0, 0)),
            whole(length, d), whole(length, d), whole(SLOT, d),
        ],
        (steps + 1,),
        [
            pltpu.VMEM((length, d), f32), pltpu.VMEM((length, d), f32), pltpu.VMEM((d, d), bf16),
            pltpu.SemaphoreType.DMA((2,)),
        ],
        "feed_back", 0, deps,
    )


def attention_back_kernel(
    piece, sc_ref, q_ref, k_ref, v_ref, gctx_ref, lse_ref, wq_ref, wk_ref, wv_ref, gr_ref,
    gq_ref, gk_ref, gv_ref, gtok_ref, sums_ref,
    acc, bias, gkt, gvt,
):
    step = pl.program_id(0)
    length = q_ref.shape[0]

    @pl.when(step == 0)
    def _():
        bias[...] = segment_bias(sc_ref, length, piece)
        acc[...] = gr_ref[...]

    lse = lse_ref[0].T
    for h in range(GROUP):
        cols = slice(h * HEAD, (h + 1) * HEAD)
        q = q_ref[:, cols]
        k = k_ref[:, cols]
        gctx = gctx_ref[:, cols]
        scores = nt(q * jnp.asarray(SCALE, bf16), k) + bias[...]
        p = jnp.exp(scores - lse[:, h : h + 1])
        ga = nt(gctx, v_ref[:, cols])
        dots = jnp.sum(p * ga, -1, keepdims=True)
        g = (p * (ga - dots)).astype(bf16)
        gq_ref[:, cols] = (nn(g, k) * SCALE).astype(bf16)
        gkt[cols, :] = (tn(q, g) * SCALE).astype(bf16)
        gvt[cols, :] = tn(gctx, p.astype(bf16)).astype(bf16)
    gk_ref[...] = gkt[...].T
    gv_ref[...] = gvt[...].T
    gq, gk, gv = gq_ref[...], gk_ref[...], gv_ref[...]
    sums_ref[0:1, :] = jnp.sum(gq.astype(f32), 0, keepdims=True)
    sums_ref[1:2, :] = jnp.sum(gv.astype(f32), 0, keepdims=True)
    acc[...] += nt(gq, wq_ref[...]) + nt(gk, wk_ref[...]) + nt(gv, wv_ref[...])

    @pl.when(step == pl.num_programs(0) - 1)
    def _():
        gtok_ref[...] = acc[...].astype(bf16)


def attention_back(sc, q, k, v, gctx, lse, wq, wk, wv, gr, piece, deps):
    length, d = q.shape
    wide = GROUP * HEAD
    steps = d // wide
    cols = lambda r: pl.BlockSpec((r, wide), lambda i, s: (0, i))
    return call(
        functools.partial(attention_back_kernel, piece),
        sc,
        (*far(q, k, v), gctx, *far(lse, wq, wk, wv), gr),
        [
            cols(length), cols(length), cols(length), cols(length),
            pl.BlockSpec((1, SLOT, length), lambda i, s: (i, 0, 0)),
            cols(d), cols(d), cols(d), whole(length, d),
        ],
        [shape(bf16, length, d)] * 4 + [shape(f32, SLOT, d)],
        [cols(length), cols(length), cols(length), whole(length, d), cols(SLOT)],
        (steps,),
        [
            pltpu.VMEM((length, d), f32), pltpu.VMEM((length, length), f32),
            pltpu.VMEM((wide, length), bf16), pltpu.VMEM((wide, length), bf16),
        ],
        "attention_back", 0, deps,
    )


def weight_total(two, lo_refs, lp_ref, go_ref, gp_ref):
    lo = lo_refs[0][...].reshape(lo_refs[0].shape[-2:])
    if len(lo_refs) > 1:
        lo = jnp.where(pl.program_id(0) < two, lo, lo_refs[1][...].reshape(lo.shape))
    return nn(lo, go_ref[0]) + nn(lp_ref[0, 0], gp_ref[0])


def weight_send_kernel(lefts, two, sc_ref, *refs):
    lo_refs, (lp_ref, go_ref, gp_ref, out_ref) = refs[:lefts], refs[lefts:]
    out_ref[0] = weight_total(two, lo_refs, lp_ref, go_ref, gp_ref).astype(bf16)


def down_total(lo_ref, lp_ref, go_ref, gp_ref):
    return nn(lo_ref[0, 0], go_ref[...]) + nn(lp_ref[0], gp_ref[...])


def down_send_kernel(sc_ref, lo_ref, lp_ref, go_ref, gp_ref, out_ref):
    out_ref[0] = down_total(lo_ref, lp_ref, go_ref, gp_ref).astype(bf16)


def down_mid_kernel(sc_ref, lo_ref, lp_ref, go_ref, gp_ref, got_ref, near_ref, far_ref):
    total = down_total(lo_ref, lp_ref, go_ref, gp_ref) + got_ref[pl.program_id(0)].astype(f32)
    half = total.shape[0] // 2
    for z in range(2):
        part = total[z * half : (z + 1) * half].astype(bf16)

        @pl.when(sc_ref[3] == z)
        def _():
            near_ref[0] = part

        @pl.when(sc_ref[3] != z)
        def _():
            far_ref[0] = part


def down_stage(kernel, sc, operands, got, outs, out_specs, steps, x, h, name, deps, micros=0):
    lo, lp, go, gp = operands
    rows = lo.shape[2]
    return call(
        kernel, sc, far(lo, lp) + (go, gp) + got,
        [
            pl.BlockSpec((1, 1) + lo.shape[2:], lambda i, s: (2 * x(i, s) + s[1], h(s), 0, 0)),
            pl.BlockSpec((1, rows, lp.shape[2]), lambda i, s: (x(i, s), h(s), 0)),
            whole(*go.shape), whole(*gp.shape),
        ]
        + [whole(*g.shape) for g in got],
        outs, out_specs, (steps,), [], name, micros, deps,
    )


def deal(sc_ref, total, step, keep_ref, send_ref):
    rows = total.shape[0] // 4
    spot = pl.ds(step * rows if isinstance(step, int) else pl.multiple_of(step * rows, rows), rows)
    for h in range(2):
        for z in range(2):
            part = total[(2 * h + z) * rows : (2 * h + z + 1) * rows].astype(bf16)

            @pl.when(sc_ref[2] == h)
            def _():
                keep_ref[sc_ref[3] ^ z, spot, :] = part

            @pl.when(sc_ref[2] != h)
            def _():
                send_ref[sc_ref[3] ^ z, spot, :] = part


def weight_keep_kernel(lefts, two, sc_ref, *refs):
    lo_refs, (lp_ref, go_ref, gp_ref, recv_ref, keep_ref, send_ref) = refs[:lefts], refs[lefts:]
    total = weight_total(two, lo_refs, lp_ref, go_ref, gp_ref) + recv_ref[0].astype(f32)
    deal(sc_ref, total, pl.program_id(0), keep_ref, send_ref)


def pack_kernel(sc_ref, qkv_ref, one_ref, two_ref, bup_ref, own_ref, far_ref):
    rows = jnp.concatenate([qkv_ref[0:2], one_ref[0:3], two_ref[0:3]], 0)
    quarter = rows.shape[1] // 4
    own_ref[...] = jnp.zeros_like(own_ref)
    far_ref[...] = jnp.zeros_like(far_ref)
    for x in range(2):
        for c in range(2):
            q = 2 * x + c
            left = rows[:, q * quarter : (q + 1) * quarter]

            def put(ref):
                ref[x, 0:8, :quarter] = left
                for j in range(4):
                    ref[x, 8 + j : 9 + j, :quarter] = bup_ref[q, :, j * quarter : (j + 1) * quarter]

            @pl.when(sc_ref[1] == c)
            def _():
                put(own_ref)

            @pl.when(sc_ref[1] != c)
            def _():
                put(far_ref)


def pack(sc, qkv, one, two, bup):
    out = shape(f32, 2, EXTRA, 2 * SMALL)
    return call(
        pack_kernel, sc, (qkv, one, two, bup), [whole(*t.shape) for t in (qkv, one, two, bup)],
        [out, out], [whole(*out.shape)] * 2, (1,), [], "pack", 0,
    )


def qkv_totals(lo_ref, lp_ref, own, par):
    return [nn(lo_ref[0], o[...]) + nn(lp_ref[0, 0], p[...]) for o, p in zip(own, par)]


def qkv_send_kernel(sc_ref, lo_ref, lp_ref, own_ref, par_ref, *refs):
    out_ref = refs[6]
    rows = lo_ref.shape[1]
    for n, total in enumerate(qkv_totals(lo_ref, lp_ref, refs[:3], refs[3:6])):
        out_ref[n * rows : (n + 1) * rows, :] = total.astype(bf16)
    vec = own_ref[1 - sc_ref[0]] + par_ref[1 - sc_ref[0]]
    out_ref[3 * rows :, :] = jnp.zeros((EXTRA, out_ref.shape[1]), bf16)
    out_ref[3 * rows :, : vec.shape[1]] = vec.astype(bf16)


def qkv_keep_kernel(sc_ref, lo_ref, lp_ref, own_ref, par_ref, *refs):
    recv_ref, keep_ref, send_ref = refs[6:]
    rows = lo_ref.shape[1]
    for n, total in enumerate(qkv_totals(lo_ref, lp_ref, refs[:3], refs[3:6])):
        total += recv_ref[n * rows : (n + 1) * rows, :].astype(f32)
        deal(sc_ref, total, n, keep_ref, send_ref)
    base = keep_ref.shape[1] - EXTRA
    vec = own_ref[sc_ref[0]] + par_ref[sc_ref[0]]
    wide = vec.shape[1]
    vec += recv_ref[3 * rows :, :wide].astype(f32)
    blank = jnp.zeros((EXTRA, keep_ref.shape[2]), bf16)
    for ref in (keep_ref, send_ref):
        for z in range(2):
            ref[z, base:, :] = blank
            ref[z, base:, :wide] = vec.astype(bf16)


def qkv_specs(xt, halves, own, other):
    x = (lambda s: 1 - s[0]) if other else (lambda s: s[0])
    return [
        pl.BlockSpec((1,) + xt.shape[1:], lambda i, s: (2 * x(s) + s[1], 0, 0)),
        pl.BlockSpec((1, 1) + halves.shape[2:], lambda i, s: (x(s), 6, 0, 0)),
    ] + [whole(2, EXTRA, 2 * SMALL)] * 2 + [whole(*own.shape)] * 6


def qkv_send(sc, operands, deps):
    xt, halves, _, _, own = operands[:5]
    rows, wide = xt.shape[1], own.shape[1]
    out = shape(bf16, 3 * rows + EXTRA, wide)
    return call(
        qkv_send_kernel, sc, far(xt, halves) + operands[2:], qkv_specs(xt, halves, own, True), out, whole(*out.shape),
        (1,), [], "qkv_send", 0, deps,
    )


def qkv_keep(sc, operands, recv, deps):
    xt, halves, _, _, own = operands[:5]
    rows, wide = xt.shape[1], own.shape[1]
    out = shape(bf16, 2, 3 * rows // 4 + EXTRA, wide)
    return call(
        qkv_keep_kernel, sc, far(xt, halves) + operands[2:] + (recv,),
        qkv_specs(xt, halves, own, False) + [whole(*recv.shape)],
        [out, out], [whole(*out.shape)] * 2, (1,), [], "qkv_keep", 0, deps,
    )


def order_kernel(sc_ref, *refs):
    out_ref = refs[-1]
    for mask, piece in enumerate(refs[:-1]):
        out_ref[sc_ref[0] ^ mask] = piece[...]


def weight_specs(lefts, halves, grads, grads_p, other, steps, turn):
    x = (lambda s: 1 - s[0]) if other else (lambda s: s[0])
    specs = []
    for left in lefts:
        if left.ndim == 4:
            specs.append(
                pl.BlockSpec((1, 1) + left.shape[2:], lambda i, s: (2 * x(s) + s[1], i, 0, 0))
            )
        else:
            specs.append(pl.BlockSpec((1,) + left.shape[1:], lambda i, s: (2 * x(s) + s[1], 0, 0)))
    specs.append(pl.BlockSpec((1, 1) + halves.shape[2:], lambda i, s: (x(s), turn(i), 0, 0)))
    one = grads.shape[0] == 1
    block = pl.BlockSpec((1,) + grads.shape[1:], lambda i, s: (0 if one else i, 0, 0))
    return (*far(*lefts), *far(halves), grads, grads_p), specs + [block, block]


def weight_send(sc, operands, steps, two, turn, name, deps=(), micros=0):
    args, specs = weight_specs(*operands, True, steps, turn)
    rows, wide = operands[1].shape[2], operands[2].shape[2]
    return call(
        functools.partial(weight_send_kernel, len(operands[0]), two),
        sc, args, specs, shape(bf16, steps, rows, wide),
        pl.BlockSpec((1, rows, wide), lambda i, s: (i, 0, 0)), (steps,), [],
        name, micros, deps,
    )


def weight_keep(sc, operands, recv, steps, two, turn, name, deps=(), micros=0):
    args, specs = weight_specs(*operands, False, steps, turn)
    rows, wide = operands[1].shape[2], operands[2].shape[2]
    out = shape(bf16, 2, steps * rows // 4, wide)
    return call(
        functools.partial(weight_keep_kernel, len(operands[0]), two),
        sc, args + (recv,), specs + [pl.BlockSpec((1, rows, wide), lambda i, s: (i, 0, 0))],
        [out, out], [whole(*out.shape)] * 2, (steps,), [],
        name, micros, deps,
    )


def place_kernel(spots, extra, sc_ref, *refs):
    parts, out_refs = refs[:4], refs[4:]
    rows = (parts[0].shape[0] - extra) // len(spots)
    wide = parts[0].shape[1]
    for side, part in enumerate(parts):
        slot = 2 * (sc_ref[2] ^ (side // 2)) + (sc_ref[3] ^ (side % 2))
        for n, (out, down, left) in enumerate(spots):
            top = pl.multiple_of((4 * down + slot) * rows, rows)
            out_refs[out][pl.ds(top, rows), left * wide : (left + 1) * wide] = part[
                n * rows : (n + 1) * rows, :
            ].astype(f32)


def place(sc, parts, spots, dims, extra, name, deps=()):
    return call(
        functools.partial(place_kernel, spots, extra),
        sc, parts, [whole(*parts[0].shape)] * 4,
        [shape(f32, *dim) for dim in dims], [whole(*dim) for dim in dims], (1,), [],
        name, 0, deps,
    )


def flip(value, axis, mask):
    count = lax.axis_size(axis)
    return lax.ppermute(value, axis, [(i, i ^ mask) for i in range(count)])


def flip_both(value, row_mask, seq_mask):
    rows, seq = lax.axis_size("rows"), lax.axis_size("seq")
    pairs = [
        (r * seq + s, (r ^ row_mask) * seq + (s ^ seq_mask)) for r in range(rows) for s in range(seq)
    ]
    return lax.ppermute(value, ("rows", "seq"), pairs)


def row_flips():
    count = lax.axis_size("rows")
    assert count >= 8 and count & (count - 1) == 0
    return [2, 6] + [1 << b for b in range(3, count.bit_length() - 1)]


def join_kernel(sc_ref, left_ref, right_ref, out_ref):
    out_ref[...] = add(left_ref[...], right_ref[...])


def join(sc, left, right, deps, name, micros=0):
    block = whole(*left.shape)
    return call(
        join_kernel, sc, (left, right), [block, block], shape(bf16, *left.shape), block, (1,), [],
        name, micros, deps,
    )


def join_two_kernel(slot, sc_ref, left_ref, right_ref, near_ref, far_ref):
    own = 0 if slot is None else sc_ref[slot]
    near_ref[...] = add(left_ref[own], right_ref[own])
    far_ref[...] = add(left_ref[1 - own], right_ref[1 - own])


def join_two(sc, left, right, deps, name, slot=None):
    block, half = whole(*left.shape), whole(*left.shape[1:])
    out = shape(bf16, *left.shape[1:])
    return call(
        functools.partial(join_two_kernel, slot), sc, (left, right), [block, block], [out, out],
        [half, half], (1,), [], name, 0, deps,
    )


def across(sc, value, masks, deps, name):
    first, *rest = masks
    value = join(sc, value, flip(value, "rows", first), deps, name)
    for mask in rest:
        value = add(value, flip(value, "rows", mask))
    return value


def gathered(value, near):
    return (value,) + tuple(flip(value, "rows", mask) for mask in (near, 1, near ^ 1))


def add(left, right):
    return (left.astype(f32) + right.astype(f32)).astype(bf16)


def moved(pieces):
    return [flip(piece, "seq", mask) if mask else piece for mask, piece in enumerate(pieces)]


def gather_back(sc, row, count, name, deps=()):
    row = row.reshape(count, -1, row.shape[-1])
    pieces = tuple(flip(row[mask], "seq", mask) if mask else row[0] for mask in range(count))
    return call(
        order_kernel, sc, pieces, [whole(*row.shape[1:])] * count, shape(row.dtype, *row.shape),
        whole(*row.shape), (1,), [], name, 0, deps,
    )


def per_device(
    tokens,
    w_query,
    b_query,
    w_key,
    w_value,
    b_value,
    w_out,
    b_out,
    gain_one,
    shift_one,
    w_up,
    b_up,
    w_down,
    b_down,
    gain_two,
    shift_two,
    passage_starts,
    queries,
    choices,
    cotangent,
):
    seq_count = lax.axis_size("seq")
    row_count = lax.axis_size("rows")
    own_s = lax.axis_index("seq")
    own_r = lax.axis_index("rows")
    row_block, piece, d = tokens.shape
    assert row_block == seq_count == 4
    ff = w_up.shape[1]
    quarter = d // 4
    core, xside = own_s % 2, own_s // 2
    own_lin = own_r * seq_count + own_s
    devices = row_count * seq_count
    masks = row_flips()
    wsc = jnp.stack([xside, core, own_r % 2, (own_r // 2 ^ own_r // 4) % 2]).astype(jnp.int32)
    starts = lax.dynamic_index_in_dim(passage_starts, own_s, 0, keepdims=False)
    sc = jnp.concatenate([own_s[None].astype(jnp.int32), starts, own_lin[None].astype(jnp.int32)])
    row = lambda v: v.reshape(1, -1)
    swap = lambda t: flip(t, "seq", 1)

    own = own_s[None].astype(jnp.int32)
    pieces, code = begin(own, tokens, queries, choices)
    pieces = moved(pieces)
    x = jnp.concatenate(pieces, 0)
    code_all = lax.all_gather(code, ("rows", "seq"), axis=0, tiled=True)

    cot = jnp.concatenate(moved(pick(own, cotangent, (pieces[1],))), 0)

    q, k, v, ctxt, lse, xt, xhat_one, inv_one, hid, hidt = attention_forward(
        sc, x, w_query, w_key, w_value, row(b_query), row(b_value), w_out, row(b_out),
        row(gain_one), row(shift_one), piece,
    )
    actt, slope, xhat_two, inv_two, mixed_row, pool = feed_forward(
        sc, hid, w_up, row(b_up), w_down, row(b_down), row(gain_two), row(shift_two), piece, (cot,)
    )

    pool = pool.astype(bf16)
    if row_count == 8:
        near = jnp.concatenate(
            [pool, flip(pool, "seq", 2), flip(pool, "rows", 1), flip_both(pool, 1, 2)], 0
        )
        mid = jnp.concatenate(
            [near, flip(near, "rows", 2), flip(near, "rows", 6), flip(near, "rows", 4)], 0
        )
        pooled = jnp.concatenate([mid, flip(mid, "seq", 1)], 0)
        places = cube_place
    else:
        near = pool
        pooled = lax.all_gather(pool, ("rows", "seq"), axis=0, tiled=True)
        pooled = jnp.roll(pooled, -own_lin * SLOT, 0)
        places = turned_place

    quarters = lambda t: t.reshape(4, -1, t.shape[-1])
    halves = swap(
        core_halves(wsc, quarters(actt), [quarters(t) for t in (hidt, ctxt, xt)], (near,))
    )

    losses_all, gd, gr_two, sums_two = retrieval(
        sc, code_all, pooled, cot, xhat_two, inv_two, row(gain_two), piece, places, devices,
        (halves,),
    )
    query_losses = lax.dynamic_slice_in_dim(
        losses_all[:, 0], own_lin * queries.shape[0], queries.shape[0]
    )

    gd_p = swap(gd)
    gug, bup, gr_one, gctx, sums_one = feed_back(
        sc, gd, gr_two, w_down, w_up, slope, xhat_one, inv_one, row(gain_one), w_out, (gd_p,)
    )

    near, *rest = masks
    part = ff // 8
    down_ops = (actt.reshape(4, 2, part, -1), halves.reshape(2, -1, piece * seq_count), gd, gd_p)
    down_sent = down_stage(
        down_send_kernel, wsc, down_ops, (), shape(bf16, 2, part, d),
        pl.BlockSpec((1, part, d), lambda i, s: (i, 0, 0)), 2,
        lambda i, s: i, lambda s: 1 - s[2], "down_send", (gug,),
    )
    down_got = flip(down_sent, "rows", 1)

    up_ops = ((quarters(hidt), quarters(ctxt)), halves, gug, swap(gug))
    up_turn = lambda i: 4 + i // 4
    up_sent = weight_send(wsc, up_ops, 5, 4, up_turn, "up_send", (down_sent,))
    up_got = flip(up_sent, "seq", 2)

    gq, gk, gv, gtok, sums_qkv = attention_back(
        sc, q, k, v, gctx, lse, w_query, w_key, w_value, gr_one, piece, (up_sent,)
    )
    vec, vec_far = pack(wsc, sums_qkv, sums_one, sums_two, bup)
    qkv_ops = (
        quarters(xt), halves, vec, swap(vec_far), gq, gk, gv, swap(gq), swap(gk), swap(gv)
    )
    qkv_sent = qkv_send(wsc, qkv_ops, ())
    qkv_got = flip(qkv_sent, "seq", 2)
    pair = shape(bf16, 2, part // 2, d)
    each = pl.BlockSpec((1, part // 2, d), lambda i, s: (i, 0, 0))
    down_near, down_far = down_stage(
        down_mid_kernel, wsc, down_ops, (down_got,), [pair, pair], [each, each], 2,
        lambda i, s: i, lambda s: s[2], "down_mid", (qkv_sent,), 3,
    )
    up_parts = weight_keep(
        wsc, up_ops, up_got, 5, 4, up_turn, "up_keep", (vec, down_near), PIN
    )
    down_sum = join(wsc, down_near, flip(down_far, "rows", near), (up_parts[0],), "down_join_a", 3)
    for mask in rest[1:]:
        down_sum = add(down_sum, flip(down_sum, "rows", mask))
    qkv_parts = qkv_keep(wsc, qkv_ops, qkv_got, (down_sum,))
    up_near, up_far = join_two(
        wsc, up_parts[0], flip(up_parts[1], "rows", 1), (qkv_parts[0],), "up_join_y"
    )
    qkv_near, qkv_far = join_two(
        wsc, qkv_parts[0], flip(qkv_parts[1], "rows", 1), (up_near,), "qkv_join_y"
    )
    up_sum = join(wsc, up_near, flip(up_far, "rows", near), (qkv_near,), "up_join_a")
    down_own, down_other = join_two(
        wsc, down_sum, flip(down_sum, "rows", rest[0]), (up_sum,), "down_join_b", 0
    )
    qkv_sum = join(wsc, qkv_near, flip(qkv_far, "rows", near), (down_own,), "qkv_join_a")
    down_sum = join(wsc, down_own, flip(down_other, "seq", 2), (qkv_sum,), "down_join_x")
    down_all = gathered(down_sum, near)
    up_sum = across(wsc, up_sum, rest, (down_sum,), "up_join_b")
    up_all = gathered(up_sum, near)
    (grad_down,) = place(wsc, down_all, [(0, 0, 0)], [(4 * quarter, d)], 0, "down_place", (up_sum,))
    qkv_sum = across(wsc, qkv_sum, rest, (grad_down,), "qkv_join_b")
    qkv_all = gathered(qkv_sum, near)
    mixed = gather_back(sc, mixed_row, seq_count, "mixed_order", (down_sum,))
    grad_tokens = gather_back(sc, gtok, seq_count, "tokens_order", (qkv_sum,))
    grad_up, grad_o = place(
        wsc, up_all, [(0, 0, n) for n in range(4)] + [(1, 0, 0)],
        [(quarter, ff), (quarter, d)], 0, "up_place", (qkv_sum,),
    )
    grad_q, grad_k, grad_v = place(
        wsc, qkv_all, [(n, 0, 0) for n in range(3)], [(quarter, d)] * 3, EXTRA, "qkv_place"
    )

    eight = qkv_sum[3 * quarter // 4 :, :quarter].astype(f32)
    return (
        mixed,
        query_losses,
        grad_tokens,
        grad_q,
        eight[0],
        grad_k,
        grad_v,
        eight[1],
        grad_o,
        eight[2],
        eight[3],
        eight[4],
        grad_up,
        eight[8:12].reshape(-1),
        grad_down,
        eight[5],
        eight[6],
        eight[7],
    )


def solution(mesh):
    weights = (P(),) * 15
    placed = (
        (P("rows", "seq", None),)
        + weights
        + (
            P("rows", None),
            P(("rows", "seq"), None),
            P(("rows", "seq"), None),
            P("rows", "seq", None),
        )
    )
    return jax.shard_map(
        per_device,
        mesh=mesh,
        in_specs=placed,
        out_specs=(
            P("rows", "seq", None),
            P(("rows", "seq")),
            P("rows", "seq", None),
            P("seq", None),
            P("seq"),
            P("seq", None),
            P("seq", None),
            P("seq"),
            P("seq", None),
            P("seq"),
            P("seq"),
            P("seq"),
            P("seq", None),
            P("seq"),
            P("seq", None),
            P("seq"),
            P("seq"),
            P("seq"),
        ),
        check_vma=False,
    )
```

```python
import functools

import jax
import jax.numpy as jnp
from jax import lax
from jax.experimental import pallas as pl
from jax.experimental.pallas import tpu as pltpu
from jax.sharding import PartitionSpec as P

HEADS = 12
HEAD = 64
PASS = 6
CH = 32
SLOT = 8
GROUP = 4
SUB = 768
SCALE = HEAD ** (-0.5)

norm_eps = 1e-05
f32 = jnp.float32
bf16 = jnp.bfloat16
VMEM_BYTES = 24 * 1024 * 1024
PIN = 100
EXTRA = 16
SMALL = 128


def params():
    return pltpu.CompilerParams(vmem_limit_bytes=VMEM_BYTES)


def cost(micros):
    return pl.CostEstimate(flops=int(micros * 1.15e9), bytes_accessed=0, transcendentals=0)


def nt(a, b):
    return lax.dot_general(a, b, (((1,), (1,)), ((), ())), preferred_element_type=f32)


def tn(a, b):
    return lax.dot_general(a, b, (((0,), (0,)), ((), ())), preferred_element_type=f32)


def nn(a, b):
    return jnp.dot(a, b, preferred_element_type=f32)


def stats(values):
    center = values - jnp.mean(values, -1, keepdims=True)
    inv = lax.rsqrt(jnp.mean(center * center, -1, keepdims=True) + norm_eps)
    return center * inv, inv


def norm_back(grad, xhat, inv, gain):
    gx = grad * gain
    return inv * (
        gx - jnp.mean(gx, -1, keepdims=True) - xhat * jnp.mean(gx * xhat, -1, keepdims=True)
    )


def true_places(own_seq, count, piece, axis):
    shape = (count, 1) if axis == 0 else (1, count)
    local = lax.broadcasted_iota(jnp.int32, shape, axis)
    block = local // piece
    return (block ^ own_seq) * piece + (local - block * piece)


def segments(sc_ref, places):
    total = jnp.zeros(places.shape, jnp.int32)
    for j in range(PASS):
        total += (sc_ref[1 + j] <= places).astype(jnp.int32)
    return total


def segment_bias(sc_ref, length, piece):
    col = segments(sc_ref, true_places(sc_ref[0], length, piece, 0))
    row = segments(sc_ref, true_places(sc_ref[0], length, piece, 1))
    return jnp.where(col == row, 0.0, -1e30)


def call(kernel, sc, args, specs, outs, out_specs, grid, scratch, name, micros, deps=()):
    count = len(args)

    def body(sc_ref, *refs):
        kernel(sc_ref, *refs[:count], *refs[count + len(deps) :])

    hold = pl.BlockSpec(memory_space=pl.ANY)
    return pl.pallas_call(
        body,
        grid_spec=pltpu.PrefetchScalarGridSpec(
            num_scalar_prefetch=1,
            grid=grid,
            in_specs=list(specs) + [hold] * len(deps),
            out_specs=out_specs,
            scratch_shapes=scratch,
        ),
        out_shape=outs,
        compiler_params=params(),
        cost_estimate=cost(micros),
        name=name,
    )(sc, *args, *deps)


def shape(t, *dims):
    return jax.ShapeDtypeStruct(dims, t)


def kept(t, *dims):
    return pltpu.HBM(dims, t)


def far(*values):
    return tuple(pltpu.with_memory_space_constraint(v, pltpu.HBM) for v in values)


def whole(*dims):
    return pl.BlockSpec(dims, lambda i, s: (0,) * len(dims))


def attention_kernel(
    piece, sc_ref, x_ref, wq_ref, wk_ref, wv_ref, bq_ref, bv_ref, wo_ref, bo_ref, go_ref, so_ref,
    q_ref, k_ref, v_ref, ctxt_ref, lse_ref, xt_ref, xhat_ref, inv_ref, hid_ref, hidt_ref,
    acc, bias,
):
    step = pl.program_id(0)
    length = x_ref.shape[0]
    x = x_ref[...]
    q_ref[...] = (nn(x, wq_ref[...]) + bq_ref[...]).astype(bf16)
    k_ref[...] = nn(x, wk_ref[...]).astype(bf16)
    v_ref[...] = (nn(x, wv_ref[...]) + bv_ref[...]).astype(bf16)

    @pl.when(step == 0)
    def _():
        bias[...] = segment_bias(sc_ref, length, piece)
        acc[...] = x.astype(f32) + bo_ref[...]

    for h in range(GROUP):
        cols = slice(h * HEAD, (h + 1) * HEAD)
        raw = nt(k_ref[:, cols], q_ref[:, cols] * jnp.asarray(SCALE, bf16))
        scores = raw + bias[...]
        top = jnp.max(scores, 0, keepdims=True)
        e = jnp.exp(scores - top)
        total = jnp.sum(e, 0, keepdims=True)
        p = (e * (1.0 / total)).astype(bf16)
        ctxt_ref[cols, :] = tn(v_ref[:, cols], p).astype(bf16)
        lse_ref[0, h : h + 1, :] = top + jnp.log(total)
    acc[...] += tn(ctxt_ref[...], wo_ref[...])

    for j in range(x_ref.shape[1] // xt_ref.shape[0]):
        wide = xt_ref.shape[0]

        @pl.when(step == j)
        def _():
            xt_ref[...] = x_ref[:, j * wide : (j + 1) * wide].T

    @pl.when(step == pl.num_programs(0) - 1)
    def _():
        xhat, inv = stats(acc[...])
        xhat_ref[...] = xhat
        inv_ref[...] = inv
        hid = (xhat * go_ref[...] + so_ref[...]).astype(bf16)
        hid_ref[...] = hid
        hidt_ref[...] = hid.T


def attention_forward(sc, x, wq, wk, wv, bq, bv, wo, bo, go, so, piece):
    length, d = x.shape
    wide = GROUP * HEAD
    steps = d // wide
    cols = lambda r: pl.BlockSpec((r, wide), lambda i, s: (0, i))
    rows = lambda c: pl.BlockSpec((wide, c), lambda i, s: (i, 0))
    return call(
        functools.partial(attention_kernel, piece),
        sc,
        (x, *far(wq, wk, wv), bq, bv, *far(wo), bo, go, so),
        [
            whole(length, d), cols(d), cols(d), cols(d), cols(1), cols(1), rows(d),
            whole(1, d), whole(1, d), whole(1, d),
        ],
        [
            kept(bf16, length, d), kept(bf16, length, d), kept(bf16, length, d),
            kept(bf16, d, length), kept(f32, steps, SLOT, length), kept(bf16, d, length),
            kept(f32, length, d), kept(f32, length, 1), shape(bf16, length, d),
            kept(bf16, d, length),
        ],
        [
            cols(length), cols(length), cols(length), rows(length),
            pl.BlockSpec((1, SLOT, length), lambda i, s: (i, 0, 0)), rows(length),
            whole(length, d), whole(length, 1), whole(length, d), whole(d, length),
        ],
        (steps,),
        [pltpu.VMEM((length, d), f32), pltpu.VMEM((length, length), f32)],
        "attention_forward", 0,
    )


def feed_kernel(
    piece, sc_ref, hid_ref, wu_ref, bu_ref, wd_ref, bd_ref, gt_ref, st_ref,
    actt_ref, slope_ref, xhat_ref, inv_ref, mixed_ref, pool_ref,
    acc,
):
    step = pl.program_id(0)
    length = hid_ref.shape[0]

    @pl.when(step == 0)
    def _():
        acc[...] = hid_ref[...].astype(f32) + bd_ref[...]

    for c in range(0, wu_ref.shape[1], SUB):
        cols = slice(c, c + SUB)
        up = nn(hid_ref[...], wu_ref[:, cols]) + bu_ref[:, cols]
        e = jnp.exp(-0.5 * up * up)
        cum = 0.5 + 0.5 * lax.erf(up * (2.0 ** -0.5))
        slope_ref[0, :, cols] = (cum + up * (e * 0.3989422804014327)).astype(bf16)
        act = (up * cum).astype(bf16)
        actt_ref[cols, :] = act.T
        acc[...] += nn(act, wd_ref[cols, :])

    @pl.when(step == pl.num_programs(0) - 1)
    def _():
        xhat, inv = stats(acc[...])
        xhat_ref[...] = xhat
        inv_ref[...] = inv
        mixed = (xhat * gt_ref[...] + st_ref[...]).astype(bf16)
        mixed_ref[...] = mixed
        places = true_places(sc_ref[0], length, piece, 1)
        slot = lax.broadcasted_iota(jnp.int32, (SLOT, 1), 0)
        start = jnp.full((SLOT, 1), -1, jnp.int32)
        for j in range(PASS):
            start = jnp.where(slot == j, sc_ref[1 + j], start)
        pool_ref[...] = nn((places == start).astype(f32).astype(bf16), mixed)


def feed_forward(sc, hid, wu, bu, wd, bd, gt, st, piece, deps):
    length, d = hid.shape
    ff = wu.shape[1]
    steps = ff // d
    return call(
        functools.partial(feed_kernel, piece),
        sc,
        (hid, *far(wu), bu, *far(wd), bd, gt, st),
        [
            whole(length, d),
            pl.BlockSpec((d, d), lambda i, s: (0, i)),
            pl.BlockSpec((1, d), lambda i, s: (0, i)),
            pl.BlockSpec((d, d), lambda i, s: (i, 0)),
            whole(1, d), whole(1, d), whole(1, d),
        ],
        [
            kept(bf16, ff, length), kept(bf16, steps, length, d), kept(f32, length, d),
            kept(f32, length, 1), kept(bf16, length, d), shape(f32, SLOT, d),
        ],
        [
            pl.BlockSpec((d, length), lambda i, s: (i, 0)),
            pl.BlockSpec((1, length, d), lambda i, s: (i, 0, 0)),
            whole(length, d), whole(length, 1), whole(length, d), whole(SLOT, d),
        ],
        (steps,),
        [pltpu.VMEM((length, d), f32)],
        "feed_forward", 0, deps,
    )


def begin_kernel(sc_ref, tokens_ref, queries_ref, choices_ref, code_ref, *piece_refs):
    for mask, piece_ref in enumerate(piece_refs):
        piece_ref[...] = tokens_ref[sc_ref[0] ^ mask]
    d = queries_ref.shape[1]
    choices = choices_ref[...]
    owner = choices // PASS
    code_ref[:, :d] = queries_ref[...]
    code_ref[:, d : d + CH] = owner.astype(f32).astype(bf16)
    code_ref[:, d + CH :] = (choices - owner * PASS).astype(f32).astype(bf16)


def begin(sc, tokens, queries, choices):
    count, d = queries.shape
    outs = [shape(bf16, count, d + 2 * CH)] + [shape(bf16, *tokens.shape[1:])] * tokens.shape[0]
    code, *pieces = call(
        begin_kernel, sc, far(tokens, queries, choices), [whole(*tokens.shape), whole(count, d), whole(count, CH)],
        outs, [whole(*o.shape) for o in outs], (1,), [], "begin", 0,
    )
    return pieces, code


def pick_kernel(sc_ref, rows_ref, *piece_refs):
    for mask, piece_ref in enumerate(piece_refs):
        piece_ref[...] = rows_ref[sc_ref[0] ^ mask]


def pick(sc, rows, deps):
    outs = [shape(bf16, *rows.shape[1:])] * rows.shape[0]
    return call(
        pick_kernel, sc, far(rows), [whole(*rows.shape)], outs, [whole(*o.shape) for o in outs],
        (1,), [], "pick", 0, deps,
    )


def halves_kernel(sc_ref, act_ref, hid_ref, ctx_ref, x_ref, out_ref):
    rows = hid_ref.shape[1]
    for n in range(act_ref.shape[1] // rows):
        out_ref[0, n] = act_ref[0, n * rows : (n + 1) * rows, :]
    for n, ref in enumerate((hid_ref, ctx_ref, x_ref)):
        out_ref[0, act_ref.shape[1] // rows + n] = ref[0]


def core_halves(sc, act, rest, deps):
    block = lambda t: pl.BlockSpec((1,) + t.shape[1:], lambda i, s: (2 * i + 1 - s[1], 0, 0))
    rows, length = rest[0].shape[1:]
    blocks = act.shape[1] // rows + len(rest)
    return call(
        halves_kernel, sc, far(act, *rest), [block(t) for t in (act, *rest)],
        shape(bf16, 2, blocks, rows, length),
        pl.BlockSpec((1, blocks, rows, length), lambda i, s: (i, 0, 0, 0)), (2,), [],
        "core_halves", 0, deps,
    )


def loss_kernel(
    piece, steps, devices, code_ref, sc_ref, q_ref, pool_ref, cot_ref, xhat_ref, inv_ref, gt_ref,
    loss_ref, gd_ref, gr_ref, sums_ref, gp,
):
    step = pl.program_id(0)
    d = pool_ref.shape[1]

    @pl.when(step == 0)
    def _():
        gp[...] = jnp.zeros_like(gp)
        sums_ref[...] = jnp.zeros_like(sums_ref)

    @pl.when(step < steps)
    def _():
        queries = q_ref[:, :d]
        logits = nt(queries, pool_ref[...])
        lanes = lax.broadcasted_iota(jnp.int32, (1, logits.shape[1]), 1)
        owner = q_ref[:, d : d + CH].astype(f32).astype(jnp.int32)
        inner = q_ref[:, d + CH :].astype(f32).astype(jnp.int32)
        pos = code_ref(owner, sc_ref[7], devices) * SLOT + inner
        first = (pos[:, 0:1] == lanes).astype(f32)
        times = first
        for c in range(1, CH):
            times += (pos[:, c : c + 1] == lanes).astype(f32)
        held = times > 0.0
        top = jnp.max(jnp.where(held, logits, -jnp.inf), -1, keepdims=True)
        e = jnp.where(held, times * jnp.exp(jnp.minimum(logits - top, 0.0)), 0.0)
        total = jnp.sum(e, -1, keepdims=True)
        positive = jnp.sum(first * logits, -1, keepdims=True)
        loss_ref[...] = top + jnp.log(total) - positive
        grad = e[:, :128] * (1.0 / total) - first[:, :128]
        high = grad.astype(bf16)
        lower = (grad - high.astype(f32)).astype(bf16)
        gp[...] += (tn(high, queries) + tn(lower, queries))[:SLOT]

    @pl.when(step >= steps)
    def _():
        block = (step - steps) ^ sc_ref[0]
        places = block * piece + lax.broadcasted_iota(jnp.int32, (piece, 1), 0)
        grad = cot_ref[...].astype(f32)
        for j in range(PASS):
            grad += jnp.where(places == sc_ref[1 + j], gp[j : j + 1, :], 0.0)
        xhat = xhat_ref[...]
        back = norm_back(grad, xhat, inv_ref[...], gt_ref[...])
        gr_ref[...] = back
        down = back.astype(bf16)
        gd_ref[...] = down
        sums_ref[0:1, :] += jnp.sum(down.astype(f32), 0, keepdims=True)
        sums_ref[1:2, :] += jnp.sum(grad * xhat, 0, keepdims=True)
        sums_ref[2:3, :] += jnp.sum(grad, 0, keepdims=True)


def cube_place(owner, own, devices):
    off = owner ^ own
    z = off >> 3
    return (off & 1) * 16 + (z ^ (z >> 1)) * 4 + ((off >> 1) & 3)


def turned_place(owner, own, devices):
    off = owner - own
    return jnp.where(off < 0, off + devices, off)


def retrieval(sc, code_all, pooled, cot, xhat, inv, gain, piece, places, devices, deps):
    count, width = code_all.shape
    length, d = cot.shape
    block = 512 if pooled.shape[0] <= 512 else 256
    steps, pieces = count // block, length // piece
    first = lambda i: jnp.minimum(i, steps - 1)
    second = lambda i: jnp.maximum(i - steps, 0)
    part = lambda c: pl.BlockSpec((piece, c), lambda i, s: (second(i), 0))
    return call(
        functools.partial(loss_kernel, piece, steps, devices, places),
        sc,
        (*far(code_all), pooled, *far(cot, xhat, inv), gain),
        [
            pl.BlockSpec((block, width), lambda i, s: (first(i), 0)),
            whole(*pooled.shape), part(d), part(d), part(1), whole(1, d),
        ],
        [shape(f32, count, 1), shape(bf16, length, d), shape(f32, length, d), shape(f32, SLOT, d)],
        [
            pl.BlockSpec((block, 1), lambda i, s: (first(i), 0)), part(d), part(d), whole(SLOT, d),
        ],
        (steps + pieces,),
        [pltpu.VMEM((SLOT, d), f32)],
        "retrieval", 0, deps,
    )


def feed_back_kernel(
    sc_ref, gd_ref, gr_ref, wd_ref, wu_ref, slope_ref, xhat_far, inv_ref, go_ref, wo_far,
    gug_ref, bup_ref, gr1_ref, gctx_ref, sums_ref,
    acc, xhat_ref, wo_ref, arrived,
):
    step = pl.program_id(0)
    last = pl.num_programs(0) - 1
    late = [
        pltpu.make_async_copy(xhat_far, xhat_ref, arrived.at[0]),
        pltpu.make_async_copy(wo_far, wo_ref, arrived.at[1]),
    ]

    @pl.when(step == 1)
    def _():
        for copy in late:
            copy.start()

    @pl.when(step == 0)
    def _():
        acc[...] = gr_ref[...]

    @pl.when(step < last)
    def _():
        gact = nt(gd_ref[...], wd_ref[...])
        gup = (gact * slope_ref[0].astype(f32)).astype(bf16)
        gug_ref[0] = gup
        bup_ref[0] = jnp.sum(gup.astype(f32), 0, keepdims=True)
        acc[...] += nt(gup, wu_ref[...])

    @pl.when(step == last)
    def _():
        for copy in late:
            copy.wait()
        grad = acc[...]
        xhat = xhat_ref[...]
        back = norm_back(grad, xhat, inv_ref[...], go_ref[...])
        gr1_ref[...] = back
        gab = back.astype(bf16)
        gug_ref[0] = gab
        gctx_ref[...] = nt(gab, wo_ref[...]).astype(bf16)
        sums_ref[0:1, :] = jnp.sum(gab.astype(f32), 0, keepdims=True)
        sums_ref[1:2, :] = jnp.sum(grad * xhat, 0, keepdims=True)
        sums_ref[2:3, :] = jnp.sum(grad, 0, keepdims=True)


def feed_back(sc, gd, gr, wd, wu, slope, xhat, inv, go, wo, deps):
    length, d = gd.shape
    steps = slope.shape[0]
    at = lambda i: jnp.minimum(i, steps - 1)
    return call(
        feed_back_kernel,
        sc,
        (gd, gr, *far(wd, wu, slope, xhat, inv), go, *far(wo)),
        [
            whole(length, d), whole(length, d),
            pl.BlockSpec((d, d), lambda i, s: (at(i), 0)),
            pl.BlockSpec((d, d), lambda i, s: (0, at(i))),
            pl.BlockSpec((1, length, d), lambda i, s: (at(i), 0, 0)),
            pl.BlockSpec(memory_space=pl.ANY), whole(length, 1), whole(1, d),
            pl.BlockSpec(memory_space=pl.ANY),
        ],
        [
            shape(bf16, steps + 1, length, d), shape(f32, steps, 1, d), shape(f32, length, d),
            shape(bf16, length, d), shape(f32, SLOT, d),
        ],
        [
            pl.BlockSpec((1, length, d), lambda i, s: (i, 0, 0)),
            pl.BlockSpec((1, 1, d), lambda i, s: (at(i), 0, 0)),
            whole(length, d), whole(length, d), whole(SLOT, d),
        ],
        (steps + 1,),
        [
            pltpu.VMEM((length, d), f32), pltpu.VMEM((length, d), f32), pltpu.VMEM((d, d), bf16),
            pltpu.SemaphoreType.DMA((2,)),
        ],
        "feed_back", 0, deps,
    )


def attention_back_kernel(
    piece, sc_ref, q_ref, k_ref, v_ref, gctx_ref, lse_ref, wq_ref, wk_ref, wv_ref, gr_ref,
    gq_ref, gk_ref, gv_ref, gtok_ref, sums_ref,
    acc, bias, gkt, gvt,
):
    step = pl.program_id(0)
    length = q_ref.shape[0]

    @pl.when(step == 0)
    def _():
        bias[...] = segment_bias(sc_ref, length, piece)
        acc[...] = gr_ref[...]

    lse = lse_ref[0].T
    for h in range(GROUP):
        cols = slice(h * HEAD, (h + 1) * HEAD)
        q = q_ref[:, cols]
        k = k_ref[:, cols]
        gctx = gctx_ref[:, cols]
        scores = nt(q * jnp.asarray(SCALE, bf16), k) + bias[...]
        p = jnp.exp(scores - lse[:, h : h + 1])
        ga = nt(gctx, v_ref[:, cols])
        dots = jnp.sum(p * ga, -1, keepdims=True)
        g = (p * (ga - dots)).astype(bf16)
        gq_ref[:, cols] = (nn(g, k) * SCALE).astype(bf16)
        gkt[cols, :] = (tn(q, g) * SCALE).astype(bf16)
        gvt[cols, :] = tn(gctx, p.astype(bf16)).astype(bf16)
    gk_ref[...] = gkt[...].T
    gv_ref[...] = gvt[...].T
    gq, gk, gv = gq_ref[...], gk_ref[...], gv_ref[...]
    sums_ref[0:1, :] = jnp.sum(gq.astype(f32), 0, keepdims=True)
    sums_ref[1:2, :] = jnp.sum(gv.astype(f32), 0, keepdims=True)
    acc[...] += nt(gq, wq_ref[...]) + nt(gk, wk_ref[...]) + nt(gv, wv_ref[...])

    @pl.when(step == pl.num_programs(0) - 1)
    def _():
        gtok_ref[...] = acc[...].astype(bf16)


def attention_back(sc, q, k, v, gctx, lse, wq, wk, wv, gr, piece, deps):
    length, d = q.shape
    wide = GROUP * HEAD
    steps = d // wide
    cols = lambda r: pl.BlockSpec((r, wide), lambda i, s: (0, i))
    return call(
        functools.partial(attention_back_kernel, piece),
        sc,
        (*far(q, k, v), gctx, *far(lse, wq, wk, wv), gr),
        [
            cols(length), cols(length), cols(length), cols(length),
            pl.BlockSpec((1, SLOT, length), lambda i, s: (i, 0, 0)),
            cols(d), cols(d), cols(d), whole(length, d),
        ],
        [shape(bf16, length, d)] * 4 + [shape(f32, SLOT, d)],
        [cols(length), cols(length), cols(length), whole(length, d), cols(SLOT)],
        (steps,),
        [
            pltpu.VMEM((length, d), f32), pltpu.VMEM((length, length), f32),
            pltpu.VMEM((wide, length), bf16), pltpu.VMEM((wide, length), bf16),
        ],
        "attention_back", 0, deps,
    )


def weight_total(two, lo_refs, lp_ref, go_ref, gp_ref):
    lo = lo_refs[0][...].reshape(lo_refs[0].shape[-2:])
    if len(lo_refs) > 1:
        lo = jnp.where(pl.program_id(0) < two, lo, lo_refs[1][...].reshape(lo.shape))
    return nn(lo, go_ref[0]) + nn(lp_ref[0, 0], gp_ref[0])


def weight_send_kernel(lefts, two, sc_ref, *refs):
    lo_refs, (lp_ref, go_ref, gp_ref, out_ref) = refs[:lefts], refs[lefts:]
    out_ref[0] = weight_total(two, lo_refs, lp_ref, go_ref, gp_ref).astype(bf16)


def down_total(lo_ref, lp_ref, go_ref, gp_ref):
    return nn(lo_ref[0, 0], go_ref[...]) + nn(lp_ref[0], gp_ref[...])


def down_send_kernel(sc_ref, lo_ref, lp_ref, go_ref, gp_ref, out_ref):
    out_ref[0] = down_total(lo_ref, lp_ref, go_ref, gp_ref).astype(bf16)


def down_mid_kernel(sc_ref, lo_ref, lp_ref, go_ref, gp_ref, got_ref, near_ref, far_ref):
    total = down_total(lo_ref, lp_ref, go_ref, gp_ref) + got_ref[pl.program_id(0)].astype(f32)
    half = total.shape[0] // 2
    for z in range(2):
        part = total[z * half : (z + 1) * half].astype(bf16)

        @pl.when(sc_ref[3] == z)
        def _():
            near_ref[0] = part

        @pl.when(sc_ref[3] != z)
        def _():
            far_ref[0] = part


def down_stage(kernel, sc, operands, got, outs, out_specs, steps, x, h, name, deps, micros=0):
    lo, lp, go, gp = operands
    rows = lo.shape[2]
    return call(
        kernel, sc, far(lo, lp) + (go, gp) + got,
        [
            pl.BlockSpec((1, 1) + lo.shape[2:], lambda i, s: (2 * x(i, s) + s[1], h(s), 0, 0)),
            pl.BlockSpec((1, rows, lp.shape[2]), lambda i, s: (x(i, s), h(s), 0)),
            whole(*go.shape), whole(*gp.shape),
        ]
        + [whole(*g.shape) for g in got],
        outs, out_specs, (steps,), [], name, micros, deps,
    )


def deal(sc_ref, total, step, keep_ref, send_ref):
    rows = total.shape[0] // 4
    spot = pl.ds(step * rows if isinstance(step, int) else pl.multiple_of(step * rows, rows), rows)
    for h in range(2):
        for z in range(2):
            part = total[(2 * h + z) * rows : (2 * h + z + 1) * rows].astype(bf16)

            @pl.when(sc_ref[2] == h)
            def _():
                keep_ref[sc_ref[3] ^ z, spot, :] = part

            @pl.when(sc_ref[2] != h)
            def _():
                send_ref[sc_ref[3] ^ z, spot, :] = part


def weight_keep_kernel(lefts, two, sc_ref, *refs):
    lo_refs, (lp_ref, go_ref, gp_ref, recv_ref, keep_ref, send_ref) = refs[:lefts], refs[lefts:]
    total = weight_total(two, lo_refs, lp_ref, go_ref, gp_ref) + recv_ref[0].astype(f32)
    deal(sc_ref, total, pl.program_id(0), keep_ref, send_ref)


def pack_kernel(sc_ref, qkv_ref, one_ref, two_ref, bup_ref, own_ref, far_ref):
    rows = jnp.concatenate([qkv_ref[0:2], one_ref[0:3], two_ref[0:3]], 0)
    quarter = rows.shape[1] // 4
    own_ref[...] = jnp.zeros_like(own_ref)
    far_ref[...] = jnp.zeros_like(far_ref)
    for x in range(2):
        for c in range(2):
            q = 2 * x + c
            left = rows[:, q * quarter : (q + 1) * quarter]

            def put(ref):
                ref[x, 0:8, :quarter] = left
                for j in range(4):
                    ref[x, 8 + j : 9 + j, :quarter] = bup_ref[q, :, j * quarter : (j + 1) * quarter]

            @pl.when(sc_ref[1] == c)
            def _():
                put(own_ref)

            @pl.when(sc_ref[1] != c)
            def _():
                put(far_ref)


def pack(sc, qkv, one, two, bup):
    out = shape(f32, 2, EXTRA, 2 * SMALL)
    return call(
        pack_kernel, sc, (qkv, one, two, bup), [whole(*t.shape) for t in (qkv, one, two, bup)],
        [out, out], [whole(*out.shape)] * 2, (1,), [], "pack", 0,
    )


def qkv_totals(lo_ref, lp_ref, own, par):
    return [nn(lo_ref[0], o[...]) + nn(lp_ref[0, 0], p[...]) for o, p in zip(own, par)]


def qkv_send_kernel(sc_ref, lo_ref, lp_ref, own_ref, par_ref, *refs):
    out_ref = refs[6]
    rows = lo_ref.shape[1]
    for n, total in enumerate(qkv_totals(lo_ref, lp_ref, refs[:3], refs[3:6])):
        out_ref[n * rows : (n + 1) * rows, :] = total.astype(bf16)
    vec = own_ref[1 - sc_ref[0]] + par_ref[1 - sc_ref[0]]
    out_ref[3 * rows :, :] = jnp.zeros((EXTRA, out_ref.shape[1]), bf16)
    out_ref[3 * rows :, : vec.shape[1]] = vec.astype(bf16)


def qkv_keep_kernel(sc_ref, lo_ref, lp_ref, own_ref, par_ref, *refs):
    recv_ref, keep_ref, send_ref = refs[6:]
    rows = lo_ref.shape[1]
    for n, total in enumerate(qkv_totals(lo_ref, lp_ref, refs[:3], refs[3:6])):
        total += recv_ref[n * rows : (n + 1) * rows, :].astype(f32)
        deal(sc_ref, total, n, keep_ref, send_ref)
    base = keep_ref.shape[1] - EXTRA
    vec = own_ref[sc_ref[0]] + par_ref[sc_ref[0]]
    wide = vec.shape[1]
    vec += recv_ref[3 * rows :, :wide].astype(f32)
    blank = jnp.zeros((EXTRA, keep_ref.shape[2]), bf16)
    for ref in (keep_ref, send_ref):
        for z in range(2):
            ref[z, base:, :] = blank
            ref[z, base:, :wide] = vec.astype(bf16)


def qkv_specs(xt, halves, own, other):
    x = (lambda s: 1 - s[0]) if other else (lambda s: s[0])
    return [
        pl.BlockSpec((1,) + xt.shape[1:], lambda i, s: (2 * x(s) + s[1], 0, 0)),
        pl.BlockSpec((1, 1) + halves.shape[2:], lambda i, s: (x(s), 6, 0, 0)),
    ] + [whole(2, EXTRA, 2 * SMALL)] * 2 + [whole(*own.shape)] * 6


def qkv_send(sc, operands, deps):
    xt, halves, _, _, own = operands[:5]
    rows, wide = xt.shape[1], own.shape[1]
    out = shape(bf16, 3 * rows + EXTRA, wide)
    return call(
        qkv_send_kernel, sc, far(xt, halves) + operands[2:], qkv_specs(xt, halves, own, True), out, whole(*out.shape),
        (1,), [], "qkv_send", 0, deps,
    )


def qkv_keep(sc, operands, recv, deps):
    xt, halves, _, _, own = operands[:5]
    rows, wide = xt.shape[1], own.shape[1]
    out = shape(bf16, 2, 3 * rows // 4 + EXTRA, wide)
    return call(
        qkv_keep_kernel, sc, far(xt, halves) + operands[2:] + (recv,),
        qkv_specs(xt, halves, own, False) + [whole(*recv.shape)],
        [out, out], [whole(*out.shape)] * 2, (1,), [], "qkv_keep", 0, deps,
    )


def order_kernel(sc_ref, *refs):
    out_ref = refs[-1]
    for mask, piece in enumerate(refs[:-1]):
        out_ref[sc_ref[0] ^ mask] = piece[...]


def weight_specs(lefts, halves, grads, grads_p, other, steps, turn):
    x = (lambda s: 1 - s[0]) if other else (lambda s: s[0])
    specs = []
    for left in lefts:
        if left.ndim == 4:
            specs.append(
                pl.BlockSpec((1, 1) + left.shape[2:], lambda i, s: (2 * x(s) + s[1], i, 0, 0))
            )
        else:
            specs.append(pl.BlockSpec((1,) + left.shape[1:], lambda i, s: (2 * x(s) + s[1], 0, 0)))
    specs.append(pl.BlockSpec((1, 1) + halves.shape[2:], lambda i, s: (x(s), turn(i), 0, 0)))
    one = grads.shape[0] == 1
    block = pl.BlockSpec((1,) + grads.shape[1:], lambda i, s: (0 if one else i, 0, 0))
    return (*far(*lefts), *far(halves), grads, grads_p), specs + [block, block]


def weight_send(sc, operands, steps, two, turn, name, deps=(), micros=0):
    args, specs = weight_specs(*operands, True, steps, turn)
    rows, wide = operands[1].shape[2], operands[2].shape[2]
    return call(
        functools.partial(weight_send_kernel, len(operands[0]), two),
        sc, args, specs, shape(bf16, steps, rows, wide),
        pl.BlockSpec((1, rows, wide), lambda i, s: (i, 0, 0)), (steps,), [],
        name, micros, deps,
    )


def weight_keep(sc, operands, recv, steps, two, turn, name, deps=(), micros=0):
    args, specs = weight_specs(*operands, False, steps, turn)
    rows, wide = operands[1].shape[2], operands[2].shape[2]
    out = shape(bf16, 2, steps * rows // 4, wide)
    return call(
        functools.partial(weight_keep_kernel, len(operands[0]), two),
        sc, args + (recv,), specs + [pl.BlockSpec((1, rows, wide), lambda i, s: (i, 0, 0))],
        [out, out], [whole(*out.shape)] * 2, (steps,), [],
        name, micros, deps,
    )


def place_kernel(spots, extra, sc_ref, *refs):
    parts, out_refs = refs[:4], refs[4:]
    rows = (parts[0].shape[0] - extra) // len(spots)
    wide = parts[0].shape[1]
    for side, part in enumerate(parts):
        slot = 2 * (sc_ref[2] ^ (side // 2)) + (sc_ref[3] ^ (side % 2))
        for n, (out, down, left) in enumerate(spots):
            top = pl.multiple_of((4 * down + slot) * rows, rows)
            out_refs[out][pl.ds(top, rows), left * wide : (left + 1) * wide] = part[
                n * rows : (n + 1) * rows, :
            ].astype(f32)


def place(sc, parts, spots, dims, extra, name, deps=()):
    return call(
        functools.partial(place_kernel, spots, extra),
        sc, parts, [whole(*parts[0].shape)] * 4,
        [shape(f32, *dim) for dim in dims], [whole(*dim) for dim in dims], (1,), [],
        name, 0, deps,
    )


def flip(value, axis, mask):
    count = lax.axis_size(axis)
    return lax.ppermute(value, axis, [(i, i ^ mask) for i in range(count)])


def flip_both(value, row_mask, seq_mask):
    rows, seq = lax.axis_size("rows"), lax.axis_size("seq")
    pairs = [
        (r * seq + s, (r ^ row_mask) * seq + (s ^ seq_mask)) for r in range(rows) for s in range(seq)
    ]
    return lax.ppermute(value, ("rows", "seq"), pairs)


def row_flips():
    count = lax.axis_size("rows")
    assert count >= 8 and count & (count - 1) == 0
    return [2, 6] + [1 << b for b in range(3, count.bit_length() - 1)]


def join_kernel(sc_ref, left_ref, right_ref, out_ref):
    out_ref[...] = add(left_ref[...], right_ref[...])


def join(sc, left, right, deps, name, micros=0):
    block = whole(*left.shape)
    return call(
        join_kernel, sc, (left, right), [block, block], shape(bf16, *left.shape), block, (1,), [],
        name, micros, deps,
    )


def join_two_kernel(slot, sc_ref, left_ref, right_ref, near_ref, far_ref):
    own = 0 if slot is None else sc_ref[slot]
    near_ref[...] = add(left_ref[own], right_ref[own])
    far_ref[...] = add(left_ref[1 - own], right_ref[1 - own])


def join_two(sc, left, right, deps, name, slot=None):
    block, half = whole(*left.shape), whole(*left.shape[1:])
    out = shape(bf16, *left.shape[1:])
    return call(
        functools.partial(join_two_kernel, slot), sc, (left, right), [block, block], [out, out],
        [half, half], (1,), [], name, 0, deps,
    )


def across(sc, value, masks, deps, name):
    first, *rest = masks
    value = join(sc, value, flip(value, "rows", first), deps, name)
    for mask in rest:
        value = add(value, flip(value, "rows", mask))
    return value


def gathered(value, near):
    return (value,) + tuple(flip(value, "rows", mask) for mask in (near, 1, near ^ 1))


def add(left, right):
    return (left.astype(f32) + right.astype(f32)).astype(bf16)


def moved(pieces):
    return [flip(piece, "seq", mask) if mask else piece for mask, piece in enumerate(pieces)]


def gather_back(sc, row, count, name, deps=()):
    row = row.reshape(count, -1, row.shape[-1])
    pieces = tuple(flip(row[mask], "seq", mask) if mask else row[0] for mask in range(count))
    return call(
        order_kernel, sc, pieces, [whole(*row.shape[1:])] * count, shape(row.dtype, *row.shape),
        whole(*row.shape), (1,), [], name, 0, deps,
    )


def per_device(
    tokens,
    w_query,
    b_query,
    w_key,
    w_value,
    b_value,
    w_out,
    b_out,
    gain_one,
    shift_one,
    w_up,
    b_up,
    w_down,
    b_down,
    gain_two,
    shift_two,
    passage_starts,
    queries,
    choices,
    cotangent,
):
    seq_count = lax.axis_size("seq")
    row_count = lax.axis_size("rows")
    own_s = lax.axis_index("seq")
    own_r = lax.axis_index("rows")
    row_block, piece, d = tokens.shape
    assert row_block == seq_count == 4
    ff = w_up.shape[1]
    quarter = d // 4
    core, xside = own_s % 2, own_s // 2
    own_lin = own_r * seq_count + own_s
    devices = row_count * seq_count
    masks = row_flips()
    wsc = jnp.stack([xside, core, own_r % 2, (own_r // 2 ^ own_r // 4) % 2]).astype(jnp.int32)
    starts = lax.dynamic_index_in_dim(passage_starts, own_s, 0, keepdims=False)
    sc = jnp.concatenate([own_s[None].astype(jnp.int32), starts, own_lin[None].astype(jnp.int32)])
    row = lambda v: v.reshape(1, -1)
    swap = lambda t: flip(t, "seq", 1)

    own = own_s[None].astype(jnp.int32)
    pieces, code = begin(own, tokens, queries, choices)
    pieces = moved(pieces)
    x = jnp.concatenate(pieces, 0)
    code_all = lax.all_gather(code, ("rows", "seq"), axis=0, tiled=True)

    cot = jnp.concatenate(moved(pick(own, cotangent, (pieces[1],))), 0)

    q, k, v, ctxt, lse, xt, xhat_one, inv_one, hid, hidt = attention_forward(
        sc, x, w_query, w_key, w_value, row(b_query), row(b_value), w_out, row(b_out),
        row(gain_one), row(shift_one), piece,
    )
    actt, slope, xhat_two, inv_two, mixed_row, pool = feed_forward(
        sc, hid, w_up, row(b_up), w_down, row(b_down), row(gain_two), row(shift_two), piece, (cot,)
    )

    pool = pool.astype(bf16)
    if row_count == 8:
        near = jnp.concatenate(
            [pool, flip(pool, "seq", 2), flip(pool, "rows", 1), flip_both(pool, 1, 2)], 0
        )
        mid = jnp.concatenate(
            [near, flip(near, "rows", 2), flip(near, "rows", 6), flip(near, "rows", 4)], 0
        )
        pooled = jnp.concatenate([mid, flip(mid, "seq", 1)], 0)
        places = cube_place
    else:
        near = pool
        pooled = lax.all_gather(pool, ("rows", "seq"), axis=0, tiled=True)
        pooled = jnp.roll(pooled, -own_lin * SLOT, 0)
        places = turned_place

    quarters = lambda t: t.reshape(4, -1, t.shape[-1])
    halves = swap(
        core_halves(wsc, quarters(actt), [quarters(t) for t in (hidt, ctxt, xt)], (near,))
    )

    losses_all, gd, gr_two, sums_two = retrieval(
        sc, code_all, pooled, cot, xhat_two, inv_two, row(gain_two), piece, places, devices,
        (halves,),
    )
    query_losses = lax.dynamic_slice_in_dim(
        losses_all[:, 0], own_lin * queries.shape[0], queries.shape[0]
    )

    gd_p = swap(gd)
    gug, bup, gr_one, gctx, sums_one = feed_back(
        sc, gd, gr_two, w_down, w_up, slope, xhat_one, inv_one, row(gain_one), w_out, (gd_p,)
    )

    near, *rest = masks
    part = ff // 8
    down_ops = (actt.reshape(4, 2, part, -1), halves.reshape(2, -1, piece * seq_count), gd, gd_p)
    down_sent = down_stage(
        down_send_kernel, wsc, down_ops, (), shape(bf16, 2, part, d),
        pl.BlockSpec((1, part, d), lambda i, s: (i, 0, 0)), 2,
        lambda i, s: i, lambda s: 1 - s[2], "down_send", (gug,),
    )
    down_got = flip(down_sent, "rows", 1)

    up_ops = ((quarters(hidt), quarters(ctxt)), halves, gug, swap(gug))
    up_turn = lambda i: 4 + i // 4
    up_sent = weight_send(wsc, up_ops, 5, 4, up_turn, "up_send", (down_sent,))
    up_got = flip(up_sent, "seq", 2)

    gq, gk, gv, gtok, sums_qkv = attention_back(
        sc, q, k, v, gctx, lse, w_query, w_key, w_value, gr_one, piece, (up_sent,)
    )
    vec, vec_far = pack(wsc, sums_qkv, sums_one, sums_two, bup)
    qkv_ops = (
        quarters(xt), halves, vec, swap(vec_far), gq, gk, gv, swap(gq), swap(gk), swap(gv)
    )
    qkv_sent = qkv_send(wsc, qkv_ops, ())
    qkv_got = flip(qkv_sent, "seq", 2)
    pair = shape(bf16, 2, part // 2, d)
    each = pl.BlockSpec((1, part // 2, d), lambda i, s: (i, 0, 0))
    down_near, down_far = down_stage(
        down_mid_kernel, wsc, down_ops, (down_got,), [pair, pair], [each, each], 2,
        lambda i, s: i, lambda s: s[2], "down_mid", (qkv_sent,), 3,
    )
    up_parts = weight_keep(
        wsc, up_ops, up_got, 5, 4, up_turn, "up_keep", (vec, down_near), PIN
    )
    down_sum = join(wsc, down_near, flip(down_far, "rows", near), (up_parts[0],), "down_join_a", 3)
    for mask in rest[1:]:
        down_sum = add(down_sum, flip(down_sum, "rows", mask))
    qkv_parts = qkv_keep(wsc, qkv_ops, qkv_got, (down_sum,))
    up_near, up_far = join_two(
        wsc, up_parts[0], flip(up_parts[1], "rows", 1), (qkv_parts[0],), "up_join_y"
    )
    qkv_near, qkv_far = join_two(
        wsc, qkv_parts[0], flip(qkv_parts[1], "rows", 1), (up_near,), "qkv_join_y"
    )
    up_sum = join(wsc, up_near, flip(up_far, "rows", near), (qkv_near,), "up_join_a")
    down_own, down_other = join_two(
        wsc, down_sum, flip(down_sum, "rows", rest[0]), (up_sum,), "down_join_b", 0
    )
    qkv_sum = join(wsc, qkv_near, flip(qkv_far, "rows", near), (down_own,), "qkv_join_a")
    down_sum = join(wsc, down_own, flip(down_other, "seq", 2), (qkv_sum,), "down_join_x")
    down_all = gathered(down_sum, near)
    up_sum = across(wsc, up_sum, rest, (down_sum,), "up_join_b")
    up_all = gathered(up_sum, near)
    (grad_down,) = place(wsc, down_all, [(0, 0, 0)], [(4 * quarter, d)], 0, "down_place", (up_sum,))
    qkv_sum = across(wsc, qkv_sum, rest, (grad_down,), "qkv_join_b")
    qkv_all = gathered(qkv_sum, near)
    mixed = gather_back(sc, mixed_row, seq_count, "mixed_order", (down_sum,))
    grad_tokens = gather_back(sc, gtok, seq_count, "tokens_order", (qkv_sum,))
    grad_up, grad_o = place(
        wsc, up_all, [(0, 0, n) for n in range(4)] + [(1, 0, 0)],
        [(quarter, ff), (quarter, d)], 0, "up_place", (qkv_sum,),
    )
    grad_q, grad_k, grad_v = place(
        wsc, qkv_all, [(n, 0, 0) for n in range(3)], [(quarter, d)] * 3, EXTRA, "qkv_place"
    )

    eight = qkv_sum[3 * quarter // 4 :, :quarter].astype(f32)
    return (
        mixed,
        query_losses,
        grad_tokens,
        grad_q,
        eight[0],
        grad_k,
        grad_v,
        eight[1],
        grad_o,
        eight[2],
        eight[3],
        eight[4],
        grad_up,
        eight[8:12].reshape(-1),
        grad_down,
        eight[5],
        eight[6],
        eight[7],
    )


def solution(mesh):
    weights = (P(),) * 15
    placed = (
        (P("rows", "seq", None),)
        + weights
        + (
            P("rows", None),
            P(("rows", "seq"), None),
            P(("rows", "seq"), None),
            P("rows", "seq", None),
        )
    )
    return jax.shard_map(
        per_device,
        mesh=mesh,
        in_specs=placed,
        out_specs=(
            P("rows", "seq", None),
            P(("rows", "seq")),
            P("rows", "seq", None),
            P("seq", None),
            P("seq"),
            P("seq", None),
            P("seq", None),
            P("seq"),
            P("seq", None),
            P("seq"),
            P("seq"),
            P("seq"),
            P("seq", None),
            P("seq"),
            P("seq", None),
            P("seq"),
            P("seq"),
            P("seq"),
        ),
        check_vma=False,
    )
```
